32 devices in a mesh: seq: 8 (over z, y), head: 4 (over x, core).
Axes of the slice: x: 2, y: 2, z: 4, core: 2. Of those that a mesh axis runs over, the one named last changes fastest.
Arguments:
- tokens: float32 [2, 4096, 2048], P(None, 'seq', 'head'), may hold values from -6 to 6
- norm_gain: bfloat16 [2048], P('seq'), may hold values from 0.5 to 1.5
- w_z: bfloat16 [2048, 4096], P('seq', 'head'), may hold values from -0.125 to 0.125
- w_x: bfloat16 [2048, 4096], P('seq', 'head'), may hold values from -0.125 to 0.125
- w_bc: bfloat16 [2048, 256], P('seq'), may hold values from -0.125 to 0.125
- w_dt: bfloat16 [2048, 64], P('seq', 'head'), may hold values from -0.125 to 0.125
- conv_x: bfloat16 [4, 4096], P(None, 'head'), may hold values from -3 to 3
- conv_bc: bfloat16 [4, 256], replicated, may hold values from -3 to 3
- dt_bias: float32 [64], P('head'), may hold values from -1 to 1
- decay_rate: float32 [64], P('head'), may hold values from 0.00024414062 to 0.05
- skip_gain: float32 [64], P('head'), may hold values from 0.5 to 1.5
- gate_gain: bfloat16 [4096], P('head'), may hold values from 0.5 to 1.5
- w_out: bfloat16 [4096, 2048], P('head', 'seq'), may hold values from -0.09375 to 0.09375
- grad_out: float32 [2, 4096, 2048], P(None, 'seq', 'head'), may hold values from -6 to 6
Outputs:
- mixed_out: float32 [2, 4096, 2048], P(None, 'seq', 'head')
- grad_tokens: float32 [2, 4096, 2048], P(None, 'seq', 'head')
- grad_norm_gain: float32 [2048], P('seq')
- grad_w_z: float32 [2048, 4096], P('seq', 'head')
- grad_w_x: float32 [2048, 4096], P('seq', 'head')
- grad_w_bc: float32 [2048, 256], P('seq')
- grad_w_dt: float32 [2048, 64], P('seq', 'head')
- grad_conv_x: float32 [4, 4096], P(None, 'head')
- grad_conv_bc: float32 [4, 256], replicated
- grad_dt_bias: float32 [64], P('head')
- grad_decay_rate: float32 [64], P('head')
- grad_skip_gain: float32 [64], P('head')
- grad_gate_gain: float32 [4096], P('head')
- grad_w_out: float32 [4096, 2048], P('head', 'seq')
The draws below stay inside these ranges and needn't reach their ends.
All inputs are finite; a program needn't handle non-finite values.
Results may differ from the reference program's by a relative error of at most 0.012.
The reference program's roundings to bfloat16 on the way count: a program that leaves them out, or rounds other values in their place, can miss the bound.
Values may be sent and summed in bfloat16 or wider, within the bound.
No kernel may reach another device: no remote copies, remote signals or barrier semaphores. Data moves between devices by JAX's collectives and lax.ppermute only.
A program may use at most 256 MiB of HBM per device.

```python
import math
import jax
import jax.numpy as jnp
from jax import lax

D = 2048
H = 64
P_SIZE = 64
N = 128
KERNEL = 4
SPAN = 256
LENGTH = 4096
DI = 4096
SEQS = 2


def shard_levels(rng, extent, cuts, least, top_value):
    gain, own = 1.0, jax.random.fold_in(rng, 6)
    for axis_at, blocks in cuts:
        heights = jnp.exp(jax.random.uniform(jax.random.fold_in(own, axis_at), (blocks,), jnp.float32, least / len(cuts), top_value / len(cuts)))
        gain = gain * jnp.repeat(heights, extent[axis_at] // blocks).reshape([-1 if axis == axis_at else 1 for axis in range(len(extent))])
    return gain


def bell_draw(own_key, dims, deviation, most, cuts=(), kind=jnp.bfloat16):
    entries = jax.random.normal(own_key, dims, jnp.float32) * deviation
    if len(cuts) > 0:
        entries = shard_levels(own_key, dims, cuts, -0.22, 0.18) * entries
    return jnp.clip(entries, min=-most, max=most).astype(kind)


def setup_inputs(seed: int = 0) -> dict:
    key_list = jax.random.split(jax.random.key(seed), 15)
    tokens = bell_draw(key_list[0], (SEQS, LENGTH, D), 1.0, 6.0, ((1, 8), (2, 4)), jnp.float32)
    norm_gain = jnp.clip(1.0 + 0.1 * jax.random.normal(key_list[1], (D,), jnp.float32), 0.5, 1.5).astype(jnp.bfloat16)
    w_z = bell_draw(key_list[2], (D, DI), D ** -0.5, 0.125, ((0, 8), (1, 4)))
    w_x = bell_draw(key_list[3], (D, DI), D ** -0.5, 0.125, ((0, 8), (1, 4)))
    w_bc = bell_draw(key_list[4], (D, 2 * N), D ** -0.5, 0.125, ((0, 8),))
    w_dt = bell_draw(key_list[5], (D, H), D ** -0.5, 0.125, ((0, 8), (1, 4)))
    conv_x = bell_draw(key_list[6], (KERNEL, DI), KERNEL ** -0.5, 3.0, ((1, 4),))
    conv_bc = bell_draw(key_list[7], (KERNEL, 2 * N), KERNEL ** -0.5, 3.0)
    dt_bias = jnp.clip(jax.random.uniform(key_list[8], (H,), jnp.float32, -1.0, 1.0) * shard_levels(key_list[8], (H,), ((0, 4),), -0.4, 0.0), -1.0, 1.0)
    decay_rate = jnp.clip(jnp.exp(math.log(0.05) - 5.322034 * jax.random.uniform(key_list[9], (H,), jnp.float32) ** shard_levels(key_list[9], (H,), ((0, 4),), -0.2, 0.2)), 0.00024414062, 0.05)
    skip_gain = jnp.clip(0.5 + 1.0 * jax.random.uniform(key_list[10], (H,), jnp.float32) ** shard_levels(key_list[10], (H,), ((0, 4),), -0.2, 0.2), 0.5, 1.5)
    gate_gain = jnp.clip(1.0 + 0.1 * jax.random.normal(key_list[11], (DI,), jnp.float32), 0.5, 1.5).astype(jnp.bfloat16)
    w_out = bell_draw(key_list[12], (DI, D), DI ** -0.5, 0.09375, ((0, 4), (1, 8)))
    grad_out = bell_draw(key_list[13], (SEQS, LENGTH, D), 1.0, 6.0, ((1, 8), (2, 4)), jnp.float32)
    return {"tokens": tokens, "norm_gain": norm_gain, "w_z": w_z, "w_x": w_x, "w_bc": w_bc, "w_dt": w_dt, "conv_x": conv_x, "conv_bc": conv_bc, "dt_bias": dt_bias, "decay_rate": decay_rate, "skip_gain": skip_gain, "gate_gain": gate_gain, "w_out": w_out, "grad_out": grad_out}


EPS = 1e-05
HIGHEST = lax.Precision.HIGHEST

@jax.custom_vjp
def low(v):
    return lax.optimization_barrier(v.astype(jnp.bfloat16)).astype(jnp.float32)

@jax.custom_vjp
def low_back(v):
    return v

def low_keep(v):
    return (low(v), None)

def low_pass(kept, grad):
    return (grad,)

def back_keep(v):
    return (v, None)

def back_low(kept, grad):
    return (low(grad),)
low.defvjp(low_keep, low_pass)
low_back.defvjp(back_keep, back_low)

def local_scan(inner, bmat, cmat, dt_raw, dt_bias, decay_rate, skip_gain):
    batch, length, heads, width = inner.shape
    block = min(SPAN, length)
    count = length // block
    steps = jax.nn.softplus(dt_raw + dt_bias)
    rates = steps * -decay_rate

    def split(array):
        return jnp.moveaxis(array.reshape((batch, count, block) + array.shape[2:]), 1, 0)

    def merge(array):
        return jnp.moveaxis(array, 0, 1).reshape((batch, length) + array.shape[3:])
    positions = lax.broadcasted_iota(jnp.int32, (block, block), 0)
    causal = positions >= lax.broadcasted_iota(jnp.int32, (block, block), 1)

    def one_block(carry, pieces):
        state, offset = carry
        part_inner, part_b, part_c, part_steps, part_rates = pieces
        within = jnp.cumsum(part_rates, axis=1)
        scores = jnp.einsum('btn,bsn->bts', part_c, part_b, precision=HIGHEST)
        gaps = within[:, :, None, :] - within[:, None, :, :]
        weights = jnp.exp(jnp.where(causal[None, :, :, None], gaps, -jnp.inf)) * scores[..., None]
        driven = part_inner * part_steps[..., None]
        inside = jnp.einsum('btsh,bshp->bthp', weights, driven, precision=HIGHEST)
        carried = jnp.exp(within)[..., None] * jnp.einsum('btn,bhpn->bthp', part_c, state, precision=HIGHEST)
        tail = jnp.exp(within[:, -1:, :] - within)
        new_state = jnp.exp(within[:, -1])[:, :, None, None] * state + jnp.einsum('bsh,bshp,bsn->bhpn', tail, driven, part_b, precision=HIGHEST)
        return ((new_state, offset + within[:, -1]), (inside + carried, offset[:, None, :] + within))
    start = (jnp.zeros((batch, heads, width, bmat.shape[-1]), jnp.float32), jnp.zeros((batch, heads), jnp.float32))
    final_pair, results = lax.scan(jax.checkpoint(one_block), start, (split(inner), split(bmat), split(cmat), split(steps), split(rates)))
    return (merge(results[0]) + skip_gain[:, None] * inner, final_pair[0], merge(results[1]))

def mixer_sequence(seq_tokens, norm_gain, w_z, w_x, w_bc, w_dt, conv_x, conv_bc, dt_bias, decay_rate, skip_gain, gate_gain, w_out):
    length = seq_tokens.shape[0]
    scale = lax.rsqrt(lax.optimization_barrier(jnp.mean(seq_tokens * seq_tokens, axis=-1, keepdims=True)) + EPS)
    normed = low(seq_tokens * scale * norm_gain)
    z_vals = low_back(jnp.dot(normed, w_z, precision=HIGHEST))
    dt_raw = low_back(jnp.dot(normed, w_dt, precision=HIGHEST))
    conv_in = low(low_back(jnp.dot(normed, jnp.concatenate([w_x, w_bc], axis=1), precision=HIGHEST)))
    conv_w = jnp.concatenate([conv_x, conv_bc], axis=1)
    padded = jnp.pad(conv_in, ((KERNEL - 1, 0), (0, 0)))
    conv_out = conv_w[0] * padded[0:length]
    for tap in range(1, KERNEL):
        conv_out = conv_out + conv_w[tap] * padded[tap:tap + length]
    conv_out = low_back(conv_out)
    act = jax.nn.silu(conv_out)
    inner = act[:, :DI].reshape(1, length, H, P_SIZE)
    bmat = act[None, :, DI:DI + N]
    cmat = act[None, :, DI + N:]
    ssd_out = local_scan(inner, bmat, cmat, dt_raw.reshape(1, length, H), dt_bias, decay_rate, skip_gain)[0]
    gated = ssd_out.reshape(length, DI) * jax.nn.silu(z_vals)
    gate_scale = lax.rsqrt(lax.optimization_barrier(jnp.mean(gated * gated, axis=-1, keepdims=True)) + EPS)
    mixed = low(gated * gate_scale * gate_gain)
    branch = low_back(jnp.dot(mixed, w_out, precision=HIGHEST))
    return seq_tokens + branch

def reference(tokens, norm_gain, w_z, w_x, w_bc, w_dt, conv_x, conv_bc, dt_bias, decay_rate, skip_gain, gate_gain, w_out, grad_out):
    params = tuple((array.astype(jnp.float32) for array in (norm_gain, w_z, w_x, w_bc, w_dt, conv_x, conv_bc, dt_bias, decay_rate, skip_gain, gate_gain, w_out)))

    def one_sequence(carry, pair):
        seq_tokens, seq_grad = pair
        outputs, backward = jax.vjp(mixer_sequence, seq_tokens, *params)
        grads = backward(seq_grad)
        return (tuple((total + grad for total, grad in zip(carry, grads[1:]))), (outputs, grads[0]))
    zeros = tuple((jnp.zeros_like(array) for array in params))
    sums, stacked = lax.scan(one_sequence, zeros, (tokens.astype(jnp.float32), grad_out.astype(jnp.float32)))
    return (stacked[0], stacked[1], sums[0], sums[1], sums[2], sums[3], sums[4], sums[5], sums[6], sums[7], sums[8], sums[9], sums[10], sums[11])
```

```python
import functools

import jax
import jax.numpy as jnp
from jax import lax
from jax.experimental import pallas as pl
from jax.experimental.pallas import tpu as pltpu
from jax.sharding import PartitionSpec as P

P_SIZE = 64
N = 128
KERNEL = 4
SPAN = 128
HALO = 8
LANES = 128
EPS = 1e-05
HIGHEST = lax.Precision.HIGHEST
F32 = jnp.float32
BF16 = jnp.bfloat16
NN = (((1,), (0,)), ((), ()))
NT = (((1,), (1,)), ((), ()))
TN = (((0,), (0,)), ((), ()))


def dot(left, right, dims=NN, precision=None):
    return lax.dot_general(left, right, dims, precision=precision, preferred_element_type=F32)


def silu_slope(value, logistic):
    return logistic * (1.0 + value * (1.0 - logistic))


class Ring:
    def __init__(self, size):
        self.size = size
        self.on = size == 8
        self.order = list(range(0, size, 2)) + list(range(size - 1, 0, -2))
        self.place = [self.order.index(i) for i in range(size)]

    def relative(self, block):
        if not self.on:
            return block
        place = jnp.asarray(self.place)
        return (place[block] - place[lax.axis_index("seq")]) % self.size

    def shift(self, array, by):
        order, size = self.order, self.size
        return lax.ppermute(array, "seq", [(order[i], order[(i + by) % size]) for i in range(size)])

    def gather(self, block, axis, after=None):
        if not self.on:
            return lax.all_gather(block, "seq", axis=axis, tiled=True), None
        if after is not None:
            block, _ = lax.optimization_barrier((block, after))
        half = self.size // 2
        items = [None] * self.size
        items[0] = block
        right = left = block
        for k in range(1, half):
            right, left = self.shift(right, 1), self.shift(left, -1)
            items[self.size - k], items[k] = right, left
        cut = block.shape[axis] // 2
        first = self.shift(lax.slice_in_dim(right, 0, cut, axis=axis), 1)
        second = self.shift(lax.slice_in_dim(left, cut, 2 * cut, axis=axis), -1)
        items[half] = jnp.concatenate([first, second], axis=axis)
        return jnp.concatenate(items, axis=axis), (right, left)

    def scatter(self, whole, axis, dtype=BF16, after=None):
        if not self.on:
            return lax.psum_scatter(
                whole.astype(dtype), "seq", scatter_dimension=axis, tiled=True
            ).astype(F32)
        size, half = self.size, self.size // 2
        width = whole.shape[axis] // size
        cut = width // 2

        def part(k, start=0, stop=width):
            k = k % size
            return lax.slice_in_dim(whole, k * width + start, k * width + stop, axis=axis)

        first = part(half, 0, cut).astype(dtype)
        second = part(half, cut, width).astype(dtype)
        if after is not None:
            first, second, _ = lax.optimization_barrier((first, second, after))
        first = self.shift(first, 1)
        second = self.shift(second, -1)
        right = jnp.concatenate(
            [part(half - 1, 0, cut) + first.astype(F32), part(half - 1, cut, width)], axis=axis
        ).astype(dtype)
        left = jnp.concatenate(
            [part(1 - half, 0, cut), part(1 - half, cut, width) + second.astype(F32)], axis=axis
        ).astype(dtype)
        for k in range(half - 2, -1, -1):
            right, left = self.shift(right, 1), self.shift(left, -1)
            if k:
                right = (part(k) + right.astype(F32)).astype(dtype)
                left = (part(-k) + left.astype(F32)).astype(dtype)
        return part(0) + right.astype(F32) + left.astype(F32)


def swap(array, axis, bit):
    size = lax.axis_size(axis)
    return lax.ppermute(array, axis, [(i, i ^ bit) for i in range(size)])


def head_sum(array):
    return lax.psum(array, "head")


def seq_sum(ring, array):
    if not ring.on:
        return lax.psum(array, "seq")
    bit = 1
    while bit < ring.size:
        array = array + swap(array, "seq", bit)
        bit *= 2
    return array


def seq_gather(ring, array):
    whole = jnp.zeros((ring.size,) + array.shape, array.dtype)
    whole = lax.dynamic_update_slice(
        whole, array[None], (lax.axis_index("seq"),) + (0,) * array.ndim
    )
    return seq_sum(ring, whole)


def head_gather(ring, own, after=None):
    heads = lax.axis_size("head")
    if not (ring.on and heads == 4):
        return lax.all_gather(own, "head", axis=1, tiled=True)
    here = lax.axis_index("head")
    if after is not None:
        own, _ = lax.optimization_barrier((own, after))
    far = swap(own, "head", 2)
    near = swap(own, "head", 1)
    both = swap(far, "head", 1)
    per = ring.size // heads
    width = own.shape[1] // per
    whole = jnp.zeros((own.shape[0], own.shape[1] * heads), own.dtype)
    for block, bit in ((own, 0), (near, 1), (far, 2), (both, 3)):
        for part in range(per):
            spot = ring.relative((here ^ bit) * per + part)
            whole = lax.dynamic_update_slice(
                whole, block[:, part * width : (part + 1) * width], (0, spot * width)
            )
    return whole


def head_scatter(ring, whole):
    heads = lax.axis_size("head")
    if not (ring.on and heads == 4):
        return lax.psum_scatter(
            whole.astype(BF16), "head", scatter_dimension=1, tiled=True
        ).astype(F32)
    here = lax.axis_index("head")
    per = ring.size // heads
    width = whole.shape[1] // ring.size

    def columns(bit):
        return [
            lax.dynamic_slice_in_dim(
                whole, ring.relative((here ^ bit) * per + part) * width, width, 1
            )
            for part in range(per)
        ]

    far = jnp.concatenate(columns(3), axis=1).astype(BF16)
    near = jnp.concatenate(columns(1), axis=1).astype(BF16)
    far = swap(far, "head", 1)
    near = swap(near, "head", 1)
    far = (jnp.concatenate(columns(2), axis=1) + far.astype(F32)).astype(BF16)
    far = swap(far, "head", 2)
    return jnp.concatenate(columns(0), axis=1) + near.astype(F32) + far.astype(F32)


def expand_scale(log_decay):
    return jnp.exp(log_decay)


def states_before(ring, state, log_decay, direction):
    size = ring.size
    incl_s, incl_w = state, log_decay
    excl_s, excl_w = jnp.zeros_like(state), jnp.zeros_like(log_decay)
    by = 1
    while by < size:
        if direction > 0:
            route = [(i, i + by) for i in range(size - by)]
        else:
            route = [(i + by, i) for i in range(size - by)]
        got_s = lax.ppermute(incl_s.astype(BF16), "seq", route).astype(F32)
        got_w = lax.ppermute(incl_w, "seq", route)
        excl_s = jnp.exp(excl_w) * got_s + excl_s
        excl_w = excl_w + got_w
        if 2 * by < size:
            incl_s = jnp.exp(incl_w) * got_s + incl_s
            incl_w = incl_w + got_w
        by *= 2
    return excl_s


def lane_is_low(rows):
    return lax.broadcasted_iota(jnp.int32, (rows, LANES), 1) < P_SIZE


def spread(columns, j, rows):
    low = jnp.broadcast_to(columns[:, 2 * j : 2 * j + 1], (rows, LANES))
    high = jnp.broadcast_to(columns[:, 2 * j + 1 : 2 * j + 2], (rows, LANES))
    return jnp.where(lane_is_low(rows), low, high), low, high


def triangle(rows, keep):
    first = lax.broadcasted_iota(jnp.int32, (rows, rows), 0)
    second = lax.broadcasted_iota(jnp.int32, (rows, rows), 1)
    return keep(first, second)


def decays(rates, rows):
    lower = triangle(rows, lambda t, s: t >= s)
    within = dot(lower.astype(F32), rates, NN, HIGHEST)
    upper = triangle(rows, lambda s, t: s <= t).astype(F32)
    within_t = dot(rates, upper, TN, HIGHEST)
    return within, within_t, lower


def window(column, row, keep):
    rows = row.shape[1]
    return jnp.exp(jnp.where(keep, column[:, :rows] - row, -1e30))


def scan_kernel(
    pairs, x_ref, bc_ref, halo_ref, dt_ref, cw_ref, bias_ref, rate_ref, skip_ref,
    v_ref, y_ref, st_ref, wc_ref, sb_ref, wo_ref, sl_ref, we_ref,
    hal, state, off, off_l,
):
    rows = x_ref.shape[0]
    inner = pairs * LANES

    @pl.when(pl.program_id(1) == 0)
    def _():
        hal[...] = halo_ref[0]
        state[...] = jnp.zeros_like(state)
        off[...] = jnp.zeros_like(off)
        off_l[...] = jnp.zeros_like(off_l)

    def convolve(ref, at, start):
        now = ref[:, start : start + LANES].astype(F32)
        chunk = jnp.concatenate([hal[:, at : at + LANES], now], axis=0)
        hal[:, at : at + LANES] = now[rows - HALO :]
        shift = HALO - KERNEL + 1
        out = cw_ref[0:1, at : at + LANES] * chunk[shift : shift + rows]
        for k in range(1, KERNEL):
            out = out + cw_ref[k : k + 1, at : at + LANES] * chunk[shift + k : shift + k + rows]
        v_ref[:, at : at + LANES] = out
        return out * jax.nn.sigmoid(out)

    bmat = convolve(bc_ref, inner, 0)
    cmat = convolve(bc_ref, inner + LANES, LANES)
    b_half, c_half = bmat.astype(BF16), cmat.astype(BF16)
    scores = dot(cmat, bmat, NT, HIGHEST)
    steps = jax.nn.softplus(dt_ref[...] + bias_ref[...])
    rates = steps * -rate_ref[...]
    within, within_t, lower = decays(rates, rows)
    low_lanes = lane_is_low(rows)
    st_ref[...] = steps
    wc_ref[...] = off[0:1] + within
    off[0:1] = off[0:1] + within[rows - 1 : rows]
    wo_ref[0] = off_l[0:1]
    for j in range(pairs):
        at = slice(j * LANES, (j + 1) * LANES)
        x = convolve(x_ref, j * LANES, j * LANES)
        u = x * spread(steps, j, rows)[0]
        u_half = u.astype(BF16)
        grow, low, high = spread(within, j, rows)
        end = grow[rows - 1 : rows]
        a_low = (window(low, within_t[2 * j : 2 * j + 1], lower) * scores).astype(BF16)
        a_high = (window(high, within_t[2 * j + 1 : 2 * j + 2], lower) * scores).astype(BF16)
        inside = jnp.where(low_lanes, dot(a_low, u_half), dot(a_high, u_half))
        before = state[:, at]
        carried = jnp.exp(grow) * dot(c_half, before.astype(BF16))
        y_ref[:, at] = inside + carried + skip_ref[0:1, at] * x
        tail = (u * jnp.exp(end - grow)).astype(BF16)
        sb_ref[0, :, at] = before
        after = jnp.exp(end) * before + dot(b_half, tail, TN)
        state[:, at] = after
        sl_ref[0, :, at] = after
        ends = off_l[0:1, at] + end
        off_l[0:1, at] = ends
        we_ref[0, :, at] = ends


def gate_kernel(pairs, y_ref, vc_ref, s_ref, wc_ref, z_ref, ssd_ref, sq_ref):
    rows = y_ref.shape[0]
    vc = vc_ref[...]
    c_half = (vc * jax.nn.sigmoid(vc)).astype(BF16)
    cumulative = wc_ref[...]
    total = jnp.zeros((rows, LANES), F32)
    for j in range(pairs):
        at = slice(j * LANES, (j + 1) * LANES)
        grow = jnp.exp(spread(cumulative, j, rows)[0])
        ssd = y_ref[:, at] + grow * dot(c_half, s_ref[0, :, at].astype(BF16))
        ssd_ref[:, at] = ssd
        z = z_ref[:, at]
        gated = ssd * (z * jax.nn.sigmoid(z))
        total = total + gated * gated
    sq_ref[0] = jnp.sum(total.T, axis=0, keepdims=True)


def as_column(row):
    return jnp.broadcast_to(row, (LANES, row.shape[1])).T


def inner_kernel(pairs, dm_ref, ssd_ref, z_ref, gs_ref, gg_ref, ip_ref, gate_ref):
    rows = dm_ref.shape[0]
    scale = as_column(gs_ref[0])

    @pl.when(pl.program_id(0) == 0)
    def _():
        gate_ref[...] = jnp.zeros_like(gate_ref)

    total = jnp.zeros((rows, LANES), F32)
    for j in range(pairs):
        at = slice(j * LANES, (j + 1) * LANES)
        z = z_ref[:, at]
        gated = ssd_ref[:, at] * (z * jax.nn.sigmoid(z))
        prod = dm_ref[:, at] * gated
        total = total + prod * gg_ref[0:1, at]
        gate_ref[0:1, at] += jnp.sum(prod * scale, axis=0, keepdims=True)
    ip_ref[0] = jnp.sum(total.T, axis=0, keepdims=True)


def gate_back_kernel(
    pairs, width, dm_ref, ssd_ref, z_ref, gs_ref, ip_ref, gg_ref, wc_ref, vc_ref,
    dz_ref, dy_ref, ds_ref,
):
    rows = dm_ref.shape[0]

    @pl.when(pl.program_id(1) == 0)
    def _():
        ds_ref[...] = jnp.zeros_like(ds_ref)

    scale = as_column(gs_ref[0])
    pull = as_column(gs_ref[0] * gs_ref[0] * gs_ref[0] * ip_ref[0] * (1.0 / width))
    vc = vc_ref[...]
    c_half = (vc * jax.nn.sigmoid(vc)).astype(BF16)
    cumulative = wc_ref[...]
    for j in range(pairs):
        at = slice(j * LANES, (j + 1) * LANES)
        z = z_ref[:, at]
        ssd = ssd_ref[:, at]
        logistic = jax.nn.sigmoid(z)
        opened = z * logistic
        d_gated = scale * (dm_ref[:, at] * gg_ref[0:1, at]) - ssd * opened * pull
        dz_ref[:, at] = (d_gated * ssd * silu_slope(z, logistic)).astype(BF16)
        dy = d_gated * opened
        dy_ref[:, at] = dy
        grown = (jnp.exp(spread(cumulative, j, rows)[0]) * dy).astype(BF16)
        ds_ref[0, :, at] += dot(c_half, grown, TN)


def scan_back_kernel(
    pairs, v_ref, dy_ref, st_ref, rate_ref, sb_ref, wo_ref, s_ref,
    du_ref, dbc_ref, grad,
):
    rows = v_ref.shape[0]
    inner = pairs * LANES

    @pl.when(pl.program_id(1) == 0)
    def _():
        grad[...] = jnp.zeros_like(grad)

    def act(at):
        value = v_ref[:, at : at + LANES]
        return value * jax.nn.sigmoid(value)

    bmat, cmat = act(inner), act(inner + LANES)
    b_half, c_half = bmat.astype(BF16), cmat.astype(BF16)
    scores = dot(cmat, bmat, NT, HIGHEST)
    steps = st_ref[...]
    rates = steps * -rate_ref[...]
    within, within_t, lower = decays(rates, rows)
    low_lanes = lane_is_low(rows)
    d_c = jnp.zeros((rows, LANES), F32)
    d_b = jnp.zeros((rows, LANES), F32)
    d_scores = jnp.zeros((rows, rows), F32)
    none = jnp.zeros((rows, LANES), BF16)
    for j in range(pairs):
        at = slice(j * LANES, (j + 1) * LANES)
        x = act(j * LANES)
        u = x * spread(steps, j, rows)[0]
        u_half = u.astype(BF16)
        dy = dy_ref[:, at]
        dy_half = dy.astype(BF16)
        grow, low, high = spread(within, j, rows)
        end = grow[rows - 1 : rows]
        back = jnp.exp(end - grow)
        grown = (jnp.exp(grow) * dy).astype(BF16)
        begun = sb_ref[0, :, at] + jnp.exp(wo_ref[0, :, at]) * s_ref[0, :, at]
        d_c = d_c + dot(grown, begun.astype(BF16), NT)
        later = grad[:, at]
        later_half = later.astype(BF16)
        d_b = d_b + dot((u * back).astype(BF16), later_half, NT)
        w_low = window(low, within_t[2 * j : 2 * j + 1], lower)
        w_high = window(high, within_t[2 * j + 1 : 2 * j + 2], lower)
        d_scores = d_scores + w_low * dot(jnp.where(low_lanes, dy_half, none), u_half, NT)
        d_scores = d_scores + w_high * dot(jnp.where(low_lanes, none, dy_half), u_half, NT)
        a_low = (w_low * scores).astype(BF16)
        a_high = (w_high * scores).astype(BF16)
        inside = jnp.where(low_lanes, dot(a_low, dy_half, TN), dot(a_high, dy_half, TN))
        du_ref[:, at] = inside + back * dot(b_half, later_half)
        grad[:, at] = jnp.exp(end) * later + dot(c_half, grown, TN)
    d_half = d_scores.astype(BF16)
    dbc_ref[:, :LANES] = d_b + dot(d_half, c_half, TN)
    dbc_ref[:, LANES:] = d_c + dot(d_half, b_half)


def head_picker(j, heads):
    lane = lax.broadcasted_iota(jnp.int32, (LANES, heads), 0) // P_SIZE
    head = lax.broadcasted_iota(jnp.int32, (LANES, heads), 1)
    return (lane + 2 * j == head).astype(F32)


def finish_kernel(
    pairs, v_ref, dy_ref, du_ref, ssd_ref, st_ref, wc_ref, we_ref, la_ref, se_ref, dbc_ref,
    dt_ref, bias_ref, rate_ref, skip_ref,
    dcx_ref, dbo_ref, ddt_ref, dskip_ref, dhead_ref, run,
):
    rows = v_ref.shape[0]
    heads = 2 * pairs
    inner = pairs * LANES

    @pl.when((pl.program_id(0) == 0) & (pl.program_id(1) == 0))
    def _():
        dskip_ref[...] = jnp.zeros_like(dskip_ref)
        dhead_ref[...] = jnp.zeros_like(dhead_ref)

    @pl.when(pl.program_id(1) == 0)
    def _():
        total = jnp.zeros((1, heads), F32)
        for j in range(pairs):
            at = slice(j * LANES, (j + 1) * LANES)
            both = jnp.sum(la_ref[0, :, at] * se_ref[0, :, at], axis=0, keepdims=True)
            total = total + dot(both, head_picker(j, heads), NN, HIGHEST)
        run[0:1] = total

    value_b = v_ref[:, inner : inner + LANES]
    b_half = (value_b * jax.nn.sigmoid(value_b)).astype(BF16)
    steps = st_ref[...]
    cumulative = wc_ref[...]
    moved = jnp.zeros((rows, heads), F32)
    driven = jnp.zeros((rows, heads), F32)
    d_b = dbc_ref[:, :LANES]
    for j in range(pairs):
        at = slice(j * LANES, (j + 1) * LANES)
        value = v_ref[:, at]
        logistic = jax.nn.sigmoid(value)
        x = value * logistic
        wide = spread(steps, j, rows)[0]
        u = x * wide
        dy = dy_ref[:, at]
        skip = skip_ref[0:1, at]
        tail = jnp.exp(we_ref[0, :, at] - spread(cumulative, j, rows)[0])
        later = la_ref[0, :, at].astype(BF16)
        du = du_ref[:, at] + tail * dot(b_half, later)
        d_b = d_b + dot((u * tail).astype(BF16), later, NT)
        picker = head_picker(j, heads)
        moved = moved + dot(dy * (ssd_ref[:, at] - skip * x) - u * du, picker, NN, HIGHEST)
        driven = driven + dot(x * du, picker, NN, HIGHEST)
        dskip_ref[0:1, at] += jnp.sum(dy * x, axis=0, keepdims=True)
        d_inner = wide * du + skip * dy
        dcx_ref[:, at] = (d_inner * silu_slope(value, logistic)).astype(BF16)
    dbo_ref[:, :LANES] = d_b
    dbo_ref[:, LANES:] = dbc_ref[:, LANES:]
    upper = triangle(rows, lambda t, s: s >= t).astype(F32)
    d_rates = dot(upper, moved, NN, HIGHEST) + run[0:1]
    run[0:1] = d_rates[0:1]
    d_steps = driven - rate_ref[...] * d_rates
    d_raw = d_steps * jax.nn.sigmoid(dt_ref[...] + bias_ref[...])
    ddt_ref[...] = d_raw.astype(BF16)
    dhead_ref[0:1] += jnp.sum(d_raw, axis=0, keepdims=True)
    dhead_ref[1:2] -= jnp.sum(steps * d_rates, axis=0, keepdims=True)


def conv_back_kernel(d_ref, in_ref, halo_ref, cw_ref, dx_ref, gw_ref, hal):
    rows, width = d_ref.shape

    @pl.when((pl.program_id(0) == 0) & (pl.program_id(1) == 0))
    def _():
        gw_ref[...] = jnp.zeros_like(gw_ref)

    @pl.when(pl.program_id(1) == 0)
    def _():
        hal[...] = halo_ref[0]

    for c in range(width // LANES):
        at = slice(c * LANES, (c + 1) * LANES)
        now = d_ref[:, at].astype(F32)
        chunk = jnp.concatenate([now, hal[:, at]], axis=0)
        hal[:, at] = now[:HALO]
        given = in_ref[:, at].astype(F32)
        total = jnp.zeros((rows, LANES), F32)
        for k in range(KERNEL):
            moved = chunk[KERNEL - 1 - k : KERNEL - 1 - k + rows]
            total = total + cw_ref[k : k + 1, at] * moved
            gw_ref[k : k + 1, at] += jnp.sum(given * moved, axis=0, keepdims=True)
        dx_ref[:, at] = total.astype(BF16)


def shaped(*shape, dtype=F32):
    return jax.ShapeDtypeStruct(shape, dtype)


def call(kernel, grid, ins, outs, shapes, scratch=(), flops=0, moved=0):
    return pl.pallas_call(
        kernel,
        grid=grid,
        in_specs=ins,
        out_specs=outs,
        out_shape=shapes,
        scratch_shapes=list(scratch),
        compiler_params=pltpu.CompilerParams(vmem_limit_bytes=40 * 1024 * 1024),
        cost_estimate=pl.CostEstimate(flops=flops, bytes_accessed=moved, transcendentals=0),
    )


def conv_back(d_conv, given, after, taps, batch, length, rows):
    width = d_conv.shape[1]
    count = length // rows
    turn = lambda b, i: (b * count + count - 1 - i, 0)
    block = pl.BlockSpec((rows, width), turn)
    total = batch * length
    return call(
        conv_back_kernel,
        (batch, count),
        [
            block,
            block,
            pl.BlockSpec((1, HALO, width), lambda b, i: (b, 0, 0)),
            pl.BlockSpec((KERNEL, width), lambda b, i: (0, 0)),
        ],
        [block, pl.BlockSpec((KERNEL, width), lambda b, i: (0, 0))],
        [shaped(total, width, dtype=BF16), shaped(KERNEL, width)],
        [pltpu.VMEM((HALO, width), F32)],
        flops=16 * total * width,
        moved=6 * total * width,
    )(d_conv, given, after, taps)


def body(
    tokens, norm_gain, w_z, w_x, w_bc, w_dt, conv_x, conv_bc, dt_bias, decay_rate,
    skip_gain, gate_gain, w_out, grad_out,
):
    ring = Ring(lax.axis_size("seq"))
    batch, length, own_width = tokens.shape
    model = norm_gain.shape[0] * ring.size
    total = batch * length
    inner = w_z.shape[1]
    heads = dt_bias.shape[0]
    inner_all = inner * lax.axis_size("head")
    pairs = heads // 2
    rows = min(SPAN, length)
    count = length // rows
    blocks = batch * count
    margin = KERNEL - 1
    here = lax.axis_index("head")

    slab = tokens.reshape(total, own_width)
    cot_rows = grad_out.reshape(total, own_width)
    bias_row = dt_bias.reshape(1, heads)
    rate_row = decay_rate.reshape(1, heads)
    skip_lanes = jnp.repeat(skip_gain, P_SIZE).reshape(1, inner)
    gate_f = gate_gain.astype(F32).reshape(1, inner)
    conv_xf = conv_x.astype(F32)
    conv_bcf = conv_bc.astype(F32)
    conv_w = jnp.concatenate([conv_xf, conv_bcf], axis=1)

    dt_w, _ = ring.gather(w_dt.T, 1)
    xbc_w, mark = ring.gather(jnp.concatenate([w_x, w_bc], axis=1), 0)
    z_w, mark = ring.gather(w_z, 0, mark)
    out_w, mark = ring.gather(w_out, 1, mark)

    gain = seq_gather(ring, norm_gain.astype(F32)).reshape(model)
    own_gain = lax.dynamic_slice_in_dim(gain, here * own_width, own_width)
    square = head_sum(jnp.sum(slab * slab, axis=1))
    scale = lax.rsqrt(square / model + EPS)
    own_normed = (slab * scale[:, None] * own_gain).astype(BF16)
    normed = head_gather(ring, own_normed)
    cot = head_gather(ring, cot_rows.astype(BF16), normed)

    xbc = dot(normed, xbc_w).astype(BF16)
    dt_raw = dot(normed, dt_w, NT)
    x_in, bc_in = xbc[:, :inner], xbc[:, inner:]

    def edge(array, last):
        cut = array.reshape(batch, length, -1)
        cut = cut[:, length - margin :] if last else cut[:, :margin]
        moves = [(i, i + 1) for i in range(ring.size - 1)]
        if not last:
            moves = [(b, a) for a, b in moves]
        got = lax.ppermute(cut, "seq", moves).astype(F32)
        pad = ((0, 0), (HALO - margin, 0), (0, 0)) if last else ((0, 0), (0, HALO - margin), (0, 0))
        return jnp.pad(got, pad)

    halo = edge(xbc, True)

    at = lambda b, i: (b * count + i, 0)
    back = lambda b, i: (b * count + count - 1 - i, 0)
    at3 = lambda b, i: (b * count + i, 0, 0)
    back3 = lambda b, i: (b * count + count - 1 - i, 0, 0)
    seq3 = lambda b, i: (b, 0, 0)
    fixed = lambda b, i: (0, 0)
    row_heads = pl.BlockSpec((1, heads), fixed)
    row_inner = pl.BlockSpec((1, inner), fixed)
    state_spec = pl.BlockSpec((1, N, inner), seq3)
    pair_flops = total * rows * inner

    conv_out, y_local, steps, cumulative, begun, offsets, left, left_w = call(
        functools.partial(scan_kernel, pairs),
        (batch, count),
        [
            pl.BlockSpec((rows, inner), at),
            pl.BlockSpec((rows, 2 * N), at),
            pl.BlockSpec((1, HALO, inner + 2 * N), seq3),
            pl.BlockSpec((rows, heads), at),
            pl.BlockSpec((KERNEL, inner + 2 * N), fixed),
            row_heads,
            row_heads,
            row_inner,
        ],
        [
            pl.BlockSpec((rows, inner + 2 * N), at),
            pl.BlockSpec((rows, inner), at),
            pl.BlockSpec((rows, heads), at),
            pl.BlockSpec((rows, heads), at),
            pl.BlockSpec((1, N, inner), at3),
            pl.BlockSpec((1, 1, inner), at3),
            state_spec,
            pl.BlockSpec((1, 1, inner), seq3),
        ],
        [
            shaped(total, inner + 2 * N),
            shaped(total, inner),
            shaped(total, heads),
            shaped(total, heads),
            shaped(blocks, N, inner),
            shaped(blocks, 1, inner),
            shaped(batch, N, inner),
            shaped(batch, 1, inner),
        ],
        [
            pltpu.VMEM((HALO, inner + 2 * N), F32),
            pltpu.VMEM((N, inner), F32),
            pltpu.VMEM((8, heads), F32),
            pltpu.VMEM((8, inner), F32),
        ],
        flops=20 * pair_flops,
        moved=total * inner * 20,
    )(x_in, bc_in, halo, dt_raw, conv_w, bias_row, rate_row, skip_lanes)

    came = states_before(ring, left, left_w, 1)
    z_vals = dot(normed, z_w)

    block_spec = pl.BlockSpec((rows, inner), at)
    row_out = pl.BlockSpec((1, 1, rows), at3)
    c_spec = pl.BlockSpec((rows, LANES), lambda b, i: (b * count + i, inner // LANES + 1))
    head_cols = pl.BlockSpec((rows, heads), at)
    ssd, square_g = call(
        functools.partial(gate_kernel, pairs),
        (batch, count),
        [block_spec, c_spec, state_spec, head_cols, block_spec],
        [block_spec, row_out],
        [shaped(total, inner), shaped(blocks, 1, rows)],
        flops=2 * total * inner * N,
        moved=total * inner * 12,
    )(y_local, conv_out, came, cumulative, z_vals)

    gate_scale = lax.rsqrt(head_sum(square_g) / inner_all + EPS)
    scale_col = gate_scale.reshape(total, 1)
    mixed = (ssd * (z_vals * jax.nn.sigmoid(z_vals)) * scale_col * gate_f).astype(BF16)

    g_out = ring.scatter(dot(mixed, cot, TN), 1)
    d_mixed = dot(cot, out_w, NT)
    flat_block = pl.BlockSpec((rows, inner), lambda i: (i, 0))
    flat_row = pl.BlockSpec((1, 1, rows), lambda i: (i, 0, 0))
    flat_inner = pl.BlockSpec((1, inner), lambda i: (0, 0))
    product, g_gate = call(
        functools.partial(inner_kernel, pairs),
        (blocks,),
        [flat_block, flat_block, flat_block, flat_row, flat_inner],
        [flat_row, flat_inner],
        [shaped(blocks, 1, rows), shaped(1, inner)],
        flops=10 * total * inner,
        moved=total * inner * 12,
    )(d_mixed, ssd, z_vals, gate_scale, gate_f)
    product = head_sum(product)

    d_z, d_ssd, d_left = call(
        functools.partial(gate_back_kernel, pairs, inner_all),
        (batch, count),
        [
            block_spec, block_spec, block_spec, row_out, row_out, row_inner, head_cols, c_spec,
        ],
        [block_spec, block_spec, state_spec],
        [shaped(total, inner, dtype=BF16), shaped(total, inner), shaped(batch, N, inner)],
        flops=2 * total * inner * N,
        moved=total * inner * 18,
    )(d_mixed, ssd, z_vals, gate_scale, product, gate_f, cumulative, conv_out)

    later = states_before(ring, d_left, left_w, -1)
    g_z = ring.scatter(dot(normed, d_z, TN), 0)

    v_back = pl.BlockSpec((rows, inner + 2 * N), back)
    block_back = pl.BlockSpec((rows, inner), back)
    heads_back = pl.BlockSpec((rows, heads), back)
    bc_back = pl.BlockSpec((rows, 2 * N), back)
    du_local, dbc_local = call(
        functools.partial(scan_back_kernel, pairs),
        (batch, count),
        [
            v_back, block_back, heads_back, row_heads,
            pl.BlockSpec((1, N, inner), back3),
            pl.BlockSpec((1, 1, inner), back3),
            state_spec,
        ],
        [block_back, bc_back],
        [shaped(total, inner), shaped(total, 2 * N)],
        [pltpu.VMEM((N, inner), F32)],
        flops=40 * pair_flops,
        moved=total * inner * 20,
    )(conv_out, d_ssd, steps, rate_row, begun, offsets, came)

    at_end = jnp.exp(left_w) * came + left
    d_conv_x, d_bc_part, d_dt, g_skip, g_heads = call(
        functools.partial(finish_kernel, pairs),
        (batch, count),
        [
            v_back, block_back, block_back, block_back, heads_back, heads_back,
            pl.BlockSpec((1, 1, inner), seq3), state_spec, state_spec, bc_back, heads_back,
            row_heads, row_heads, row_inner,
        ],
        [
            block_back, bc_back, heads_back, row_inner,
            pl.BlockSpec((2, heads), fixed),
        ],
        [
            shaped(total, inner, dtype=BF16),
            shaped(total, 2 * N),
            shaped(total, heads, dtype=BF16),
            shaped(1, inner),
            shaped(2, heads),
        ],
        [pltpu.VMEM((8, heads), F32)],
        flops=4 * total * inner * N,
        moved=total * inner * 22,
    )(
        conv_out, d_ssd, du_local, ssd, steps, cumulative, left_w, later, at_end, dbc_local,
        dt_raw, bias_row, rate_row, skip_lanes,
    )

    if lax.axis_size("head") == 4:
        d_bc_sum = d_bc_part + swap(d_bc_part, "head", 1)
        d_bc_sum = d_bc_sum.astype(BF16)
        d_bc_sum = d_bc_sum.astype(F32) + swap(d_bc_sum, "head", 2).astype(F32)
    else:
        d_bc_sum = head_sum(d_bc_part)
    v_bc = conv_out[:, inner:]
    d_conv_bc = (d_bc_sum * silu_slope(v_bc, jax.nn.sigmoid(v_bc))).astype(BF16)

    d_x, g_conv_x = conv_back(
        d_conv_x, x_in, edge(d_conv_x, False), conv_xf, batch, length, rows
    )
    d_bc, g_conv_bc = conv_back(
        d_conv_bc, bc_in, edge(d_conv_bc, False), conv_bcf, batch, length, rows
    )

    d_xbc = jnp.concatenate([d_x, d_bc], axis=1)
    x_w, bc_w = xbc_w[:, :inner], xbc_w[:, inner:]
    own_terms = dot(d_z, z_w, NT) + dot(d_x, x_w, NT) + dot(d_dt, dt_w)
    own_terms = own_terms + jnp.where(here == 0, 1.0, 0.0) * dot(d_bc, bc_w, NT)
    d_normed = head_scatter(ring, own_terms)
    g_xbc = ring.scatter(dot(normed, d_xbc, TN), 0)
    g_dt = ring.scatter(dot(d_dt, normed, TN), 1, F32).T

    out_own = head_scatter(ring, dot(mixed, out_w))
    mixed_out = slab + out_own

    g_gain_own = jnp.sum(d_normed * slab * scale[:, None], axis=0)
    gain_grad = d_normed * own_gain
    dots = head_sum(jnp.sum(gain_grad * slab, axis=1))
    grad_tokens = (
        cot_rows
        + scale[:, None] * gain_grad
        - slab * (scale * scale * scale * dots / model)[:, None]
    )
    g_gain = jnp.zeros((model,), F32)
    g_gain = lax.dynamic_update_slice_in_dim(g_gain, g_gain_own, here * own_width, 0)
    if lax.axis_size("head") == 4:
        g_gain = g_gain + swap(g_gain, "head", 1)
        g_gain = g_gain + swap(g_gain, "head", 2)
    else:
        g_gain = head_sum(g_gain)
    g_gain = seq_sum(ring, g_gain)
    slice_width = norm_gain.shape[0]
    g_gain = lax.dynamic_slice_in_dim(g_gain, lax.axis_index("seq") * slice_width, slice_width)

    small = jnp.concatenate(
        [
            g_conv_x.reshape(-1), g_conv_bc.reshape(-1), g_gate.reshape(-1),
            g_skip.reshape(-1), g_heads.reshape(-1),
        ]
    )
    small = seq_sum(ring, small)
    cuts = [KERNEL * inner, KERNEL * 2 * N, inner, inner, heads, heads]
    parts, start = [], 0
    for width in cuts:
        parts.append(small[start : start + width])
        start += width
    sum_x, sum_bc, sum_gate, sum_skip, sum_bias, sum_rate = parts

    return (
        mixed_out.reshape(batch, length, own_width),
        grad_tokens.reshape(batch, length, own_width),
        g_gain,
        g_z,
        g_xbc[:, :inner],
        g_xbc[:, inner:],
        g_dt,
        sum_x.reshape(KERNEL, inner),
        sum_bc.reshape(KERNEL, 2 * N),
        sum_bias,
        sum_rate,
        jnp.sum(sum_skip.reshape(heads, P_SIZE), axis=1),
        sum_gate,
        g_out,
    )


def solution(mesh):
    in_specs = (
        P(None, "seq", "head"),
        P("seq"),
        P("seq", "head"),
        P("seq", "head"),
        P("seq", None),
        P("seq", "head"),
        P(None, "head"),
        P(),
        P("head"),
        P("head"),
        P("head"),
        P("head"),
        P("head", "seq"),
        P(None, "seq", "head"),
    )
    out_specs = (
        P(None, "seq", "head"),
        P(None, "seq", "head"),
        P("seq"),
        P("seq", "head"),
        P("seq", "head"),
        P("seq", None),
        P("seq", "head"),
        P(None, "head"),
        P(),
        P("head"),
        P("head"),
        P("head"),
        P("head"),
        P("head", "seq"),
    )
    return jax.shard_map(body, mesh=mesh, in_specs=in_specs, out_specs=out_specs, check_vma=False)
```

```python
import functools

import jax
import jax.numpy as jnp
from jax import lax
from jax.experimental import pallas as pl
from jax.experimental.pallas import tpu as pltpu
from jax.sharding import PartitionSpec as P

P_SIZE = 64
N = 128
KERNEL = 4
SPAN = 128
HALO = 8
LANES = 128
EPS = 1e-05
HIGHEST = lax.Precision.HIGHEST
F32 = jnp.float32
BF16 = jnp.bfloat16
VMEM_LIMIT = 50 * 1024 * 1024
NN = (((1,), (0,)), ((), ()))
NT = (((1,), (1,)), ((), ()))
TN = (((0,), (0,)), ((), ()))


def dot(left, right, dims=NN, precision=None):
    return lax.dot_general(left, right, dims, precision=precision, preferred_element_type=F32)


def silu_slope(value, logistic):
    return logistic * (1.0 + value * (1.0 - logistic))


class Ring:
    def __init__(self, size):
        self.size = size
        self.on = size == 8 and lax.axis_size("head") == 4
        self.order = list(range(0, size, 2)) + list(range(size - 1, 0, -2))
        here = lax.axis_index("seq")
        self.line, self.side = here >> 1, here & 1
        self.place = jnp.where(self.side == 0, self.line, size - 1 - self.line)

    def spots(self):
        place = (self.place + jnp.arange(self.size, dtype=jnp.int32)) & (self.size - 1)
        side = place >> 2
        line = jnp.where(side == 1, self.size - 1 - place, place)
        bit = lax.axis_index("head") ^ line
        return 2 * jnp.where(bit == 3, 0, jnp.where(bit == 0, 3, bit)) + side

    def blocks(self):
        spot = jnp.arange(self.size, dtype=jnp.int32)
        side, bit = spot & 1, spot >> 1
        bit = jnp.where(bit == 0, 3, jnp.where(bit == 3, 0, bit))
        line = lax.axis_index("head") ^ bit
        place = jnp.where(side == 1, self.size - 1 - line, line)
        return (place - self.place) & (self.size - 1)

    def shift(self, array, by):
        order, size = self.order, self.size
        return lax.ppermute(array, "seq", [(order[i], order[(i + by) % size]) for i in range(size)])

    def hop(self, moving):
        if not self.on:
            return moving
        return self.shift(moving[0], 1), self.shift(moving[1], -1)

    def last_hop(self, moving):
        if not self.on:
            return moving
        cut = moving[0].shape[0] // 2
        return self.shift(moving[0][:cut], 1), self.shift(moving[1][cut:], -1)

    def part(self, whole, k):
        n = whole.shape[0] // self.size
        k = k % self.size
        return whole[k * n : (k + 1) * n]

    def send(self, whole):
        if not self.on:
            return None
        far = self.part(whole, self.size // 2)
        cut = far.shape[0] // 2
        return self.shift(far[:cut], 1), self.shift(far[cut:], -1)

    def add(self, whole, came, k):
        if not self.on:
            return None
        right, left = self.part(whole, k).astype(F32), self.part(whole, -k).astype(F32)
        first, second = came[0].astype(F32), came[1].astype(F32)
        if k == self.size // 2 - 1:
            cut = first.shape[0]
            right = jnp.concatenate([right[:cut] + first, right[cut:]], axis=0)
            left = jnp.concatenate([left[:cut], left[cut:] + second], axis=0)
        else:
            right, left = right + first, left + second
        return right.astype(BF16), left.astype(BF16)

    def total(self, whole, came):
        if not self.on:
            return lax.psum_scatter(whole, "seq", scatter_dimension=0, tiled=True).astype(F32)
        return self.part(whole, 0).astype(F32) + came[0].astype(F32) + came[1].astype(F32)

    def phase(self, work, *args):
        if not self.on:
            return work(*args)
        shapes = jax.eval_shape(work, *args)

        def idle(*args):
            return jax.tree.map(lambda x: jnp.zeros(x.shape, x.dtype), shapes)

        return lax.cond(lax.axis_index("seq") < self.size, work, idle, *args)


def swap(array, axis, bit):
    size = lax.axis_size(axis)
    return lax.ppermute(array, axis, [(i, i ^ bit) for i in range(size)])


def head_sum(array):
    return lax.psum(array, "head")


def seq_sum(ring, array):
    if not ring.on:
        return lax.psum(array, "seq")
    bit = 1
    while bit < ring.size:
        array = array + swap(array, "seq", bit)
        bit *= 2
    return array


def own_features(ring, block, own_width):
    if not ring.on:
        whole = lax.all_gather(block, "seq", axis=0, tiled=True)
        return lax.dynamic_slice_in_dim(whole, lax.axis_index("head") * own_width, own_width)

    def fetch(flip):
        index = lambda line, side, head: (2 * line + side) * 4 + head
        return lax.ppermute(
            block,
            ("seq", "head"),
            [
                (index(head, side ^ flip, line), index(line, side, head))
                for line in range(4)
                for side in range(2)
                for head in range(4)
            ],
        )

    same, other = fetch(0), fetch(1)
    even = ring.side == 0
    return jnp.concatenate([jnp.where(even, same, other), jnp.where(even, other, same)])


def corner(ring, own, far):
    if not ring.on:
        return lax.all_gather(own, "head", axis=1, tiled=True)
    return swap(far, "head", 1)


def beside(ring, array):
    return swap(array, "head", 1) if ring.on else array


def across(ring, array):
    return swap(array, "head", 2) if ring.on else array


def scatter_near(ring, whole):
    if not ring.on:
        return whole, None
    width = whole.shape[1] // 4
    part = lambda k: whole[:, k * width : (k + 1) * width]
    far = swap(part(0), "head", 1)
    near = swap(part(1), "head", 1)
    far = (part(2).astype(F32) + far.astype(F32)).astype(BF16)
    return far, part(3).astype(F32) + near.astype(F32)


def scatter_sum(ring, far, mine):
    if not ring.on:
        return lax.psum_scatter(far, "head", scatter_dimension=1, tiled=True).astype(F32)
    return mine + far.astype(F32)


def shift_flat(array, by):
    size = lax.axis_size("seq")
    return lax.ppermute(array, "seq", [(i, i + by) for i in range(size) if 0 <= i + by < size])


def states_scan(state, log_decay, direction):
    incl_s, incl_w = state, log_decay
    excl_s, excl_w = jnp.zeros_like(state), jnp.zeros_like(log_decay)
    by = 1
    while by < lax.axis_size("seq"):
        got_s = shift_flat(incl_s.astype(BF16), by * direction).astype(F32)
        got_w = shift_flat(incl_w, by * direction)
        excl_s = jnp.exp(excl_w) * got_s + excl_s
        excl_w = excl_w + got_w
        incl_s = jnp.exp(incl_w) * got_s + incl_s
        incl_w = incl_w + got_w
        by *= 2
    return excl_s


def log_rows(log_decay):
    high = log_decay.astype(BF16).astype(F32)
    middle = (log_decay - high).astype(BF16).astype(F32)
    low = log_decay - high - middle
    row = lax.broadcasted_iota(jnp.int32, (16, log_decay.shape[1]), 0)
    parts = jnp.where(row == 0, high, jnp.where(row == 1, middle, low))
    return jnp.where(row < 3, parts, 0.0).astype(BF16)


def log_sum(rows):
    rows = rows.astype(F32)
    return rows[0:1] + rows[1:2] + rows[2:3]


def pass_begin_kernel(even_ref, lead_ref, state_ref, log_ref, keep_ref, kept_ref, send_ref):
    even = even_ref[0] == 1
    keep_ref[...] = jnp.where(even, state_ref[0], state_ref[1])
    kept_ref[...] = jnp.where(even, log_ref[0], log_ref[1])
    send_ref[:N] = jnp.where(even, state_ref[1], state_ref[0]).astype(BF16)
    send_ref[N:] = log_rows(jnp.where(even, log_ref[1], log_ref[0]))


def pass_pair_kernel(
    even_ref, lead_ref, keep_ref, kept_ref, got_ref, first_ref, d_first_ref, both_ref, pair_ref, send_ref
):
    leads = lead_ref[0] == 1
    keep, kept = keep_ref[...], kept_ref[...]
    got, gotten = got_ref[:N].astype(F32), log_sum(got_ref[N:])
    first = jnp.where(leads, keep, got)
    both = jnp.exp(jnp.where(leads, gotten, kept)) * first + jnp.where(leads, got, keep)
    first_ref[...] = first
    d_first_ref[...] = jnp.exp(jnp.where(leads, kept, gotten))
    both_ref[...] = both
    pair_ref[...] = jnp.exp(kept + gotten)
    send_ref[:N] = both.astype(BF16)
    send_ref[N:] = log_rows(kept + gotten)


def pass_line_kernel(even_ref, lead_ref, both_ref, pair_ref, got_ref, carry_ref, before_ref, send_ref):
    carry = got_ref[:N].astype(F32)
    carry_ref[...] = carry
    before_ref[...] = jnp.exp(log_sum(got_ref[N:]))
    send_ref[...] = (pair_ref[...] * carry + both_ref[...]).astype(BF16)


def pass_far_kernel(
    even_ref, lead_ref, first_ref, d_first_ref, carry_ref, before_ref, got_ref, mine_ref, send_ref
):
    leads = lead_ref[0] == 1
    carry = before_ref[...] * got_ref[...].astype(F32) + carry_ref[...]
    further = d_first_ref[...] * carry + first_ref[...]
    mine_ref[...] = jnp.where(leads, carry, further)
    send_ref[...] = jnp.where(leads, further, carry).astype(BF16)


def pass_end_kernel(even_ref, lead_ref, mine_ref, got_ref, out_ref):
    even = even_ref[0] == 1
    mine, got = mine_ref[...], got_ref[...].astype(F32)
    out_ref[0] = jnp.where(even, mine, got)
    out_ref[1] = jnp.where(even, got, mine)


class Passing:
    def __init__(self, ring, direction, inner):
        self.direction = direction
        leads = ring.side == 0 if direction > 0 else ring.side == 1
        self.flags = [jnp.where(f, 1, 0).astype(jnp.int32).reshape(1) for f in (ring.side == 0, leads)]
        row = shaped(1, inner)
        self.state, self.row = shaped(N, inner), row
        self.sent, self.sent_log = shaped(N, inner, dtype=BF16), shaped(N + 16, inner, dtype=BF16)

    def step(self, kernel, outs, *args):
        return pl.pallas_call(
            kernel,
            in_specs=[pl.BlockSpec(memory_space=pltpu.SMEM)] * 2
            + [pl.BlockSpec(memory_space=pltpu.VMEM)] * len(args),
            out_specs=jax.tree.map(lambda _: pl.BlockSpec(memory_space=pltpu.VMEM), outs),
            out_shape=outs,
            compiler_params=pltpu.CompilerParams(vmem_limit_bytes=VMEM_LIMIT),
        )(*self.flags, *args)

    def begin(self, state, log_decay):
        return self.step(pass_begin_kernel, [self.state, self.row, self.sent_log], state, log_decay)

    def pair(self, held):
        keep, kept, send = held
        got = swap(send, "seq", 1)
        outs = [self.state, self.row, self.state, self.row, self.sent_log]
        return self.step(pass_pair_kernel, outs, keep, kept, got)

    def next_line(self, held):
        first, d_first, both, pair, send = held
        got = shift_flat(send, 2 * self.direction)
        outs = [self.state, self.row, self.sent]
        return (first, d_first, *self.step(pass_line_kernel, outs, both, pair, got))

    def further_lines(self, held):
        first, d_first, carry, before, send = held
        got = shift_flat(send, 4 * self.direction)
        outs = [self.state, self.sent]
        return self.step(pass_far_kernel, outs, first, d_first, carry, before, got)

    def end(self, held):
        mine, send = held
        out = shaped(2, *self.state.shape)
        return self.step(pass_end_kernel, out, mine, swap(send, "seq", 1))


def lane_is_low(rows):
    return lax.broadcasted_iota(jnp.int32, (rows, LANES), 1) < P_SIZE


def spread(columns, j, rows):
    low = jnp.broadcast_to(columns[:, 2 * j : 2 * j + 1], (rows, LANES))
    high = jnp.broadcast_to(columns[:, 2 * j + 1 : 2 * j + 2], (rows, LANES))
    return jnp.where(lane_is_low(rows), low, high), low, high


def triangle(rows, keep):
    first = lax.broadcasted_iota(jnp.int32, (rows, rows), 0)
    second = lax.broadcasted_iota(jnp.int32, (rows, rows), 1)
    return keep(first, second)


def decays(rates, rows):
    lower = triangle(rows, lambda t, s: t >= s)
    within = dot(lower.astype(F32), rates, NN, HIGHEST)
    upper = triangle(rows, lambda s, t: s <= t).astype(F32)
    within_t = dot(rates, upper, TN, HIGHEST)
    return within, within_t, lower


def window(column, row, keep):
    rows = row.shape[1]
    return jnp.exp(jnp.where(keep, column[:, :rows] - row, -1e30))


def scan_kernel(
    pairs, x_ref, bc_ref, halo_ref, dt_ref, cw_ref, bias_ref, rate_ref, skip_ref,
    v_ref, y_ref, st_ref, wc_ref, sb_ref, wo_ref, sl_ref, we_ref,
    hal, state, off, off_l,
):
    rows = x_ref.shape[0]
    inner = pairs * LANES

    @pl.when(pl.program_id(1) == 0)
    def _():
        hal[...] = halo_ref[0]
        state[...] = jnp.zeros_like(state)
        off[...] = jnp.zeros_like(off)
        off_l[...] = jnp.zeros_like(off_l)

    def convolve(ref, at, start):
        now = ref[:, start : start + LANES].astype(F32)
        chunk = jnp.concatenate([hal[:, at : at + LANES], now], axis=0)
        hal[:, at : at + LANES] = now[rows - HALO :]
        shift = HALO - KERNEL + 1
        out = cw_ref[0:1, at : at + LANES] * chunk[shift : shift + rows]
        for k in range(1, KERNEL):
            out = out + cw_ref[k : k + 1, at : at + LANES] * chunk[shift + k : shift + k + rows]
        v_ref[:, at : at + LANES] = out
        return out * jax.nn.sigmoid(out)

    bmat = convolve(bc_ref, inner, 0)
    cmat = convolve(bc_ref, inner + LANES, LANES)
    b_half, c_half = bmat.astype(BF16), cmat.astype(BF16)
    scores = dot(cmat, bmat, NT, HIGHEST)
    steps = jax.nn.softplus(dt_ref[...] + bias_ref[...])
    rates = steps * -rate_ref[...]
    within, within_t, lower = decays(rates, rows)
    low_lanes = lane_is_low(rows)
    st_ref[...] = steps
    wc_ref[...] = off[0:1] + within
    off[0:1] = off[0:1] + within[rows - 1 : rows]
    wo_ref[0] = off_l[0:1]
    for j in range(pairs):
        at = slice(j * LANES, (j + 1) * LANES)
        x = convolve(x_ref, j * LANES, j * LANES)
        u = x * spread(steps, j, rows)[0]
        u_half = u.astype(BF16)
        grow, low, high = spread(within, j, rows)
        end = grow[rows - 1 : rows]
        a_low = (window(low, within_t[2 * j : 2 * j + 1], lower) * scores).astype(BF16)
        a_high = (window(high, within_t[2 * j + 1 : 2 * j + 2], lower) * scores).astype(BF16)
        inside = jnp.where(low_lanes, dot(a_low, u_half), dot(a_high, u_half))
        before = state[:, at]
        carried = jnp.exp(grow) * dot(c_half, before.astype(BF16))
        y_ref[:, at] = inside + carried + skip_ref[0:1, at] * x
        tail = (u * jnp.exp(end - grow)).astype(BF16)
        sb_ref[0, :, at] = before
        after = jnp.exp(end) * before + dot(b_half, tail, TN)
        state[:, at] = after
        sl_ref[0, :, at] = after
        ends = off_l[0:1, at] + end
        off_l[0:1, at] = ends
        we_ref[0, :, at] = ends


def gate_kernel(
    pairs, y_ref, vc_ref, s_ref, wc_ref, zp_ref, dmp_ref, gg_ref, na_ref, ca_ref, wz_ref, wo_ref,
    ssd_ref, sq_ref, z_ref, dm_ref
):
    rows = y_ref.shape[0]
    z_ref[...] = zp_ref[...] + dot(na_ref[...], wz_ref[...])
    dm_ref[...] = dmp_ref[...] + dot(ca_ref[...], wo_ref[...])
    vc = vc_ref[...]
    c_half = (vc * jax.nn.sigmoid(vc)).astype(BF16)
    cumulative = wc_ref[...]
    total = jnp.zeros((rows, LANES), F32)
    meet = jnp.zeros((rows, LANES), F32)
    for j in range(pairs):
        at = slice(j * LANES, (j + 1) * LANES)
        grow = jnp.exp(spread(cumulative, j, rows)[0])
        ssd = y_ref[:, at] + grow * dot(c_half, s_ref[0, :, at].astype(BF16))
        ssd_ref[:, at] = ssd
        z = z_ref[:, at]
        gated = ssd * (z * jax.nn.sigmoid(z))
        total = total + gated * gated
        meet = meet + dm_ref[:, at] * gg_ref[0:1, at] * gated
    sq_ref[0, 0:1] = jnp.sum(total.T, axis=0, keepdims=True)
    sq_ref[0, 1:2] = jnp.sum(meet.T, axis=0, keepdims=True)


def as_column(row):
    return jnp.broadcast_to(row, (LANES, row.shape[1])).T


def gate_back_kernel(
    pairs, width, dmp_ref, ssd_ref, zp_ref, gs_ref, ip_ref, gg_ref, wc_ref, vc_ref,
    na_ref, ca_ref, wz_ref, wo_ref,
    dz_ref, dy_ref, ds_ref, zz_ref, gate_ref, mixed_ref, z_ref, dm_ref,
):
    rows = dmp_ref.shape[0]
    z_ref[...] = zp_ref[...] + dot(na_ref[...], wz_ref[...])
    dm_ref[...] = dmp_ref[...] + dot(ca_ref[...], wo_ref[...])

    @pl.when(pl.program_id(1) == 0)
    def _():
        ds_ref[...] = jnp.zeros_like(ds_ref)

    @pl.when((pl.program_id(0) == 0) & (pl.program_id(1) == 0))
    def _():
        gate_ref[...] = jnp.zeros_like(gate_ref)

    scale = as_column(gs_ref[0])
    pull = as_column(gs_ref[0] * gs_ref[0] * gs_ref[0] * ip_ref[0] * (1.0 / width))
    vc = vc_ref[...]
    c_half = (vc * jax.nn.sigmoid(vc)).astype(BF16)
    cumulative = wc_ref[...]
    total = jnp.zeros((rows, LANES), F32)
    for j in range(pairs):
        at = slice(j * LANES, (j + 1) * LANES)
        z = z_ref[:, at]
        ssd = ssd_ref[:, at]
        logistic = jax.nn.sigmoid(z)
        opened = z * logistic
        gated = ssd * opened
        mixed_ref[:, at] = (gated * scale * gg_ref[0:1, at]).astype(BF16)
        scaled = scale * dm_ref[:, at]
        gate_ref[0:1, at] += jnp.sum(scaled * gated, axis=0, keepdims=True)
        d_gated = scaled * gg_ref[0:1, at] - gated * pull
        d_z = (d_gated * ssd * silu_slope(z, logistic)).astype(BF16)
        dz_ref[:, at] = d_z
        total = total + d_z.astype(F32) * z
        dy = d_gated * opened
        dy_ref[:, at] = dy
        grown = (jnp.exp(spread(cumulative, j, rows)[0]) * dy).astype(BF16)
        ds_ref[0, :, at] += dot(c_half, grown, TN)
    zz_ref[0] = jnp.sum(total.T, axis=0, keepdims=True)


def scan_back_kernel(
    pairs, v_ref, dy_ref, st_ref, rate_ref, sb_ref, wo_ref, s_ref,
    du_ref, dbc_ref, grad,
):
    rows = v_ref.shape[0]
    inner = pairs * LANES

    @pl.when(pl.program_id(1) == 0)
    def _():
        grad[...] = jnp.zeros_like(grad)

    def act(at):
        value = v_ref[:, at : at + LANES]
        return value * jax.nn.sigmoid(value)

    bmat, cmat = act(inner), act(inner + LANES)
    b_half, c_half = bmat.astype(BF16), cmat.astype(BF16)
    scores = dot(cmat, bmat, NT, HIGHEST)
    steps = st_ref[...]
    rates = steps * -rate_ref[...]
    within, within_t, lower = decays(rates, rows)
    low_lanes = lane_is_low(rows)
    d_c = jnp.zeros((rows, LANES), F32)
    d_b = jnp.zeros((rows, LANES), F32)
    d_scores = jnp.zeros((rows, rows), F32)
    none = jnp.zeros((rows, LANES), BF16)
    for j in range(pairs):
        at = slice(j * LANES, (j + 1) * LANES)
        x = act(j * LANES)
        u = x * spread(steps, j, rows)[0]
        u_half = u.astype(BF16)
        dy = dy_ref[:, at]
        dy_half = dy.astype(BF16)
        grow, low, high = spread(within, j, rows)
        end = grow[rows - 1 : rows]
        back = jnp.exp(end - grow)
        grown = (jnp.exp(grow) * dy).astype(BF16)
        begun = sb_ref[0, :, at] + jnp.exp(wo_ref[0, :, at]) * s_ref[0, :, at]
        d_c = d_c + dot(grown, begun.astype(BF16), NT)
        later = grad[:, at]
        later_half = later.astype(BF16)
        d_b = d_b + dot((u * back).astype(BF16), later_half, NT)
        w_low = window(low, within_t[2 * j : 2 * j + 1], lower)
        w_high = window(high, within_t[2 * j + 1 : 2 * j + 2], lower)
        d_scores = d_scores + w_low * dot(jnp.where(low_lanes, dy_half, none), u_half, NT)
        d_scores = d_scores + w_high * dot(jnp.where(low_lanes, none, dy_half), u_half, NT)
        a_low = (w_low * scores).astype(BF16)
        a_high = (w_high * scores).astype(BF16)
        inside = jnp.where(low_lanes, dot(a_low, dy_half, TN), dot(a_high, dy_half, TN))
        du_ref[:, at] = inside + back * dot(b_half, later_half)
        grad[:, at] = jnp.exp(end) * later + dot(c_half, grown, TN)
    d_half = d_scores.astype(BF16)
    dbc_ref[:, :LANES] = d_b + dot(d_half, c_half, TN)
    dbc_ref[:, LANES:] = d_c + dot(d_half, b_half)


def put_split(ref, at, value):
    rows = value.shape[0]
    high = value.astype(BF16)
    ref[:rows, at] = high
    ref[rows : 2 * rows, at] = (value - high.astype(F32)).astype(BF16)


def per_head(ref, picker, rows):
    both = dot(ref[: 2 * rows], picker)
    return both[:rows] + both[rows:]


def finish_kernel(
    pairs, v_ref, dy_ref, du_ref, ssd_ref, st_ref, wc_ref, we_ref, la_ref, se_ref, dbc_ref,
    dt_ref, bias_ref, rate_ref, skip_ref, pick_ref,
    dcx_ref, dbo_ref, ddt_ref, dskip_ref, dhead_ref, run, moves, drives,
):
    rows = v_ref.shape[0]
    inner = pairs * LANES
    picker = pick_ref[...]

    @pl.when((pl.program_id(0) == 0) & (pl.program_id(1) == 0))
    def _():
        dskip_ref[...] = jnp.zeros_like(dskip_ref)
        dhead_ref[...] = jnp.zeros_like(dhead_ref)

    @pl.when(pl.program_id(1) == 0)
    def _():
        for j in range(pairs):
            at = slice(j * LANES, (j + 1) * LANES)
            both = jnp.sum(la_ref[0, :, at] * se_ref[0, :, at], axis=0, keepdims=True)
            put_split(moves, at, jnp.broadcast_to(both, (rows, LANES)))
        run[...] = per_head(moves, picker, rows)[0:8]

    value_b = v_ref[:, inner : inner + LANES]
    b_half = (value_b * jax.nn.sigmoid(value_b)).astype(BF16)
    steps = st_ref[...]
    cumulative = wc_ref[...]
    d_b = dbc_ref[:, :LANES]
    for j in range(pairs):
        at = slice(j * LANES, (j + 1) * LANES)
        value = v_ref[:, at]
        logistic = jax.nn.sigmoid(value)
        x = value * logistic
        wide = spread(steps, j, rows)[0]
        u = x * wide
        dy = dy_ref[:, at]
        skip = skip_ref[0:1, at]
        tail = jnp.exp(we_ref[0, :, at] - spread(cumulative, j, rows)[0])
        later = la_ref[0, :, at].astype(BF16)
        du = du_ref[:, at] + tail * dot(b_half, later)
        d_b = d_b + dot((u * tail).astype(BF16), later, NT)
        put_split(moves, at, dy * (ssd_ref[:, at] - skip * x) - u * du)
        put_split(drives, at, x * du)
        dskip_ref[0:1, at] += jnp.sum(dy * x, axis=0, keepdims=True)
        d_inner = wide * du + skip * dy
        dcx_ref[:, at] = (d_inner * silu_slope(value, logistic)).astype(BF16)
    dbo_ref[:, :LANES] = d_b
    dbo_ref[:, LANES:] = dbc_ref[:, LANES:]
    moved = per_head(moves, picker, rows)
    driven = per_head(drives, picker, rows)
    upper = triangle(rows, lambda t, s: s >= t).astype(F32)
    d_rates = dot(upper, moved, NN, HIGHEST) + run[0:1]
    run[0:1] = d_rates[0:1]
    d_steps = driven - rate_ref[...] * d_rates
    d_raw = d_steps * jax.nn.sigmoid(dt_ref[...] + bias_ref[...])
    ddt_ref[...] = d_raw.astype(BF16)
    dhead_ref[0:1] += jnp.sum(d_raw, axis=0, keepdims=True)
    dhead_ref[1:2] -= jnp.sum(steps * d_rates, axis=0, keepdims=True)


def conv_back_kernel(d_ref, in_ref, halo_ref, cw_ref, dx_ref, gw_ref, xx_ref, hal):
    rows, width = d_ref.shape

    @pl.when((pl.program_id(0) == 0) & (pl.program_id(1) == 0))
    def _():
        gw_ref[...] = jnp.zeros_like(gw_ref)

    @pl.when(pl.program_id(1) == 0)
    def _():
        hal[...] = halo_ref[0]

    meet = jnp.zeros((rows, LANES), F32)
    for c in range(width // LANES):
        at = slice(c * LANES, (c + 1) * LANES)
        now = d_ref[:, at].astype(F32)
        chunk = jnp.concatenate([now, hal[:, at]], axis=0)
        hal[:, at] = now[:HALO]
        given = in_ref[:, at].astype(F32)
        total = jnp.zeros((rows, LANES), F32)
        for k in range(KERNEL):
            moved = chunk[KERNEL - 1 - k : KERNEL - 1 - k + rows]
            total = total + cw_ref[k : k + 1, at] * moved
            gw_ref[k : k + 1, at] += jnp.sum(given * moved, axis=0, keepdims=True)
        d_x = total.astype(BF16)
        dx_ref[:, at] = d_x
        meet = meet + d_x.astype(F32) * given
    xx_ref[0] = jnp.sum(meet.T, axis=0, keepdims=True)


def place_blocks(spot_ref, target, items, down, along=slice(None)):
    order = [0]
    for k in range(1, 4):
        order += [8 - k, k]

    rows = down.stop - down.start

    def put(k, shift, block):
        at = pl.multiple_of(spot_ref[k] * rows + shift, LANES)
        target[pl.ds(at, block.shape[0]), :] = block

    for k, item in zip(order, items):
        put(k, 0, item[down, along])
    return put


def in_project_kernel(spot_ref, *refs):
    acts, items, halves = refs[:4], refs[4:11], refs[11:13]
    x_ref, bc_ref, dt_ref, w_ref, r_ref = refs[13:]
    rows = items[0].shape[0]
    inner = x_ref.shape[1]

    @pl.when(pl.program_id(0) == 0)
    def _():
        for target, cut in ((w_ref, slice(0, inner)), (r_ref, slice(inner, None))):
            put = place_blocks(spot_ref, target, items, slice(0, rows), cut)
            put(4, 0, halves[0][:, cut])
            put(4, rows // 2, halves[1][:, cut])

    act = jnp.concatenate([a[...] for a in acts], axis=1)
    x_ref[...] = dot(act, w_ref[...]).astype(BF16)
    rest = dot(act, r_ref[...])
    bc_ref[...] = rest[:, : 2 * N].astype(BF16)
    dt_ref[...] = rest[:, 2 * N :]


def gate_project_kernel(spot_ref, *refs):
    acts, cots, items = refs[:4], refs[4:8], refs[8:15]
    z_ref, dm_ref, wz_ref, wo_ref, na_ref, ca_ref = refs[15:]
    rows = items[0].shape[0] // 2
    last = spot_ref[4]

    @pl.when(pl.program_id(0) == 0)
    def _():
        for target, down in ((wz_ref, slice(0, rows)), (wo_ref, slice(rows, 2 * rows))):
            put = place_blocks(spot_ref, target, items, down)
            put(4, 0, jnp.zeros((rows, target.shape[1]), BF16))

    for i in range(8):

        @pl.when(last == i)
        def _():
            cut = slice((i % 2) * rows, (i % 2 + 1) * rows)
            na_ref[...] = acts[i // 2][:, cut]
            ca_ref[...] = cots[i // 2][:, cut]

    z_ref[...] = dot(jnp.concatenate([a[...] for a in acts], axis=1), wz_ref[...])
    dm_ref[...] = dot(jnp.concatenate([a[...] for a in cots], axis=1), wo_ref[...])


def with_spots(kernel, spots, acts, items, outs, shapes):
    total, width = acts[0].shape
    rows = min(256, total)
    fixed = lambda i, spot: (0, 0)
    return pl.pallas_call(
        kernel,
        grid_spec=pltpu.PrefetchScalarGridSpec(
            num_scalar_prefetch=1,
            grid=(total // rows,),
            in_specs=[pl.BlockSpec((rows, width), lambda i, spot: (i, 0)) for _ in acts]
            + [pl.BlockSpec(item.shape, fixed) for item in items],
            out_specs=[
                pl.BlockSpec((rows, shape.shape[1]), lambda i, spot: (i, 0)) if split
                else pl.BlockSpec(shape.shape, fixed)
                for shape, split in zip(shapes, outs)
            ],
        ),
        out_shape=shapes,
        compiler_params=pltpu.CompilerParams(vmem_limit_bytes=VMEM_LIMIT),
    )(spots, *acts, *items)


def outer_kernel(pairs_of, block_ref, *refs):
    out_ref = refs[-1]
    n = len(pairs_of)
    grads = refs[4 * n : -1]
    width = refs[0].shape[1]
    for a in range(4):

        @pl.when(pl.program_id(0) // 2 == a)
        def _():
            taken = 0
            for i, count in enumerate(pairs_of):
                start = 0
                for grad in grads[taken : taken + count]:
                    wide = grad.shape[1]
                    out_ref[i * width : (i + 1) * width, start : start + wide] = dot(
                        refs[4 * i + a][...], grad[...], TN
                    ).astype(BF16)
                    start += wide
                taken += count


def outer(blocks, *terms):
    total, own = terms[0][0][0].shape
    width = own // 2
    specs, args = [], []
    for acts, _ in terms:
        for a, act in enumerate(acts):
            specs.append(
                pl.BlockSpec((total, width), lambda i, _, a=a: (0, jnp.clip(i - 2 * a, 0, 1)))
            )
            args.append(act)
    for _, grads in terms:
        for grad in grads:
            specs.append(pl.BlockSpec(grad.shape, lambda i, _: (0, 0)))
            args.append(grad)
    columns = sum(g.shape[1] for g in terms[0][1])
    rows = width * len(terms)
    return pl.pallas_call(
        functools.partial(outer_kernel, [len(grads) for _, grads in terms]),
        grid_spec=pltpu.PrefetchScalarGridSpec(
            num_scalar_prefetch=1,
            grid=(8,),
            in_specs=specs,
            out_specs=pl.BlockSpec((rows, columns), lambda i, block: (block[i], 0)),
        ),
        out_shape=shaped(8 * rows, columns, dtype=BF16),
        compiler_params=pltpu.CompilerParams(vmem_limit_bytes=VMEM_LIMIT),
    )(blocks, *args)


def project_kernel(terms, late, spot_ref, *refs):
    out_ref = refs[-1]
    total = None
    for k in range(terms):
        weight = refs[terms + k][...]
        if k < late:
            weight = jnp.where(pl.program_id(0) == spot_ref[4], refs[2 * terms + k][...], weight)
        term = dot(refs[k][...], weight, NT)
        total = term if total is None else total + term
    out_ref[...] = total.astype(out_ref.dtype)


def project(ring, spots, acts, weights, late=()):
    if not ring.on:
        return sum(dot(a, w, NT) for a, w in zip(acts, weights)).astype(BF16)
    rows, width = acts[0].shape[0], 256
    whole = lambda i, spot: (0, 0)
    return pl.pallas_call(
        functools.partial(project_kernel, len(acts), len(late)),
        grid_spec=pltpu.PrefetchScalarGridSpec(
            num_scalar_prefetch=1,
            grid=(weights[0].shape[0] // width,),
            in_specs=[pl.BlockSpec(a.shape, whole) for a in acts]
            + [pl.BlockSpec((width, w.shape[1]), lambda i, spot: (i, 0)) for w in weights]
            + [pl.BlockSpec(w.shape, whole) for w in late],
            out_specs=pl.BlockSpec((rows, width), lambda i, spot: (0, i)),
        ),
        out_shape=shaped(rows, weights[0].shape[0], dtype=BF16),
        compiler_params=pltpu.CompilerParams(vmem_limit_bytes=VMEM_LIMIT),
    )(spots, *acts, *weights, *late)


def shaped(*shape, dtype=F32):
    return jax.ShapeDtypeStruct(shape, dtype)


def call(kernel, grid, ins, outs, shapes, scratch=(), micros=5.0):
    return pl.pallas_call(
        kernel,
        grid=grid,
        in_specs=ins,
        out_specs=outs,
        out_shape=shapes,
        scratch_shapes=list(scratch),
        compiler_params=pltpu.CompilerParams(vmem_limit_bytes=VMEM_LIMIT),
        cost_estimate=pl.CostEstimate(
            flops=0, bytes_accessed=int(micros * 3.3e6), transcendentals=0
        ),
    )


def conv_back(d_conv, given, after, taps, batch, length, rows):
    width = d_conv.shape[1]
    count = length // rows
    turn = lambda b, i: (b * count + count - 1 - i, 0)
    block = pl.BlockSpec((rows, width), turn)
    total = batch * length
    return call(
        conv_back_kernel,
        (batch, count),
        [
            block,
            block,
            pl.BlockSpec((1, HALO, width), lambda b, i: (b, 0, 0)),
            pl.BlockSpec((KERNEL, width), lambda b, i: (0, 0)),
        ],
        [
            block,
            pl.BlockSpec((KERNEL, width), lambda b, i: (0, 0)),
            pl.BlockSpec((1, 1, rows), lambda b, i: (b * count + count - 1 - i, 0, 0)),
        ],
        [
            shaped(total, width, dtype=BF16),
            shaped(KERNEL, width),
            shaped(batch * count, 1, rows),
        ],
        [pltpu.VMEM((HALO, width), F32)],
        micros=8.0 * total * width / 2**20,
    )(d_conv, given, after, taps)


def body(
    tokens, norm_gain, w_z, w_x, w_bc, w_dt, conv_x, conv_bc, dt_bias, decay_rate,
    skip_gain, gate_gain, w_out, grad_out,
):
    ring = Ring(lax.axis_size("seq"))
    batch, length, own_width = tokens.shape
    model = norm_gain.shape[0] * ring.size
    total = batch * length
    inner = w_z.shape[1]
    heads = dt_bias.shape[0]
    inner_all = inner * lax.axis_size("head")
    pairs = heads // 2
    rows = min(SPAN, length)
    count = length // rows
    blocks = batch * count
    margin = KERNEL - 1
    here = lax.axis_index("head")

    slab = tokens.reshape(total, own_width)
    cot_rows = grad_out.reshape(total, own_width)
    bias_row = dt_bias.reshape(1, heads)
    rate_row = decay_rate.reshape(1, heads)
    skip_lanes = jnp.repeat(skip_gain, P_SIZE).reshape(1, inner)
    gate_f = gate_gain.astype(F32).reshape(1, inner)
    conv_xf = conv_x.astype(F32)
    conv_bcf = conv_bc.astype(F32)
    conv_w = jnp.concatenate([conv_xf, conv_bcf], axis=1)

    def edge(arrays, last):
        cut = [array.reshape(batch, length, -1) for array in arrays]
        cut = [array[:, length - margin :] if last else array[:, :margin] for array in cut]
        cut = jnp.concatenate(cut, axis=2)
        moves = [(i, i + 1) for i in range(ring.size - 1)]
        if not last:
            moves = [(b, a) for a, b in moves]
        got = lax.ppermute(cut, "seq", moves).astype(F32)
        pad = ((0, 0), (HALO - margin, 0), (0, 0)) if last else ((0, 0), (0, HALO - margin), (0, 0))
        return jnp.pad(got, pad)

    at = lambda b, i: (b * count + i, 0)
    back = lambda b, i: (b * count + count - 1 - i, 0)
    at3 = lambda b, i: (b * count + i, 0, 0)
    back3 = lambda b, i: (b * count + count - 1 - i, 0, 0)
    seq3 = lambda b, i: (b, 0, 0)
    fixed = lambda b, i: (0, 0)
    row_heads = pl.BlockSpec((1, heads), fixed)
    row_inner = pl.BlockSpec((1, inner), fixed)
    state_spec = pl.BlockSpec((1, N, inner), seq3)
    pair_flops = total * rows * inner

    block_spec = pl.BlockSpec((rows, inner), at)
    row_out = pl.BlockSpec((1, 1, rows), at3)
    c_spec = pl.BlockSpec((rows, LANES), lambda b, i: (b * count + i, inner // LANES + 1))
    head_cols = pl.BlockSpec((rows, heads), at)
    v_back = pl.BlockSpec((rows, inner + 2 * N), back)
    block_back = pl.BlockSpec((rows, inner), back)
    heads_back = pl.BlockSpec((rows, heads), back)
    bc_back = pl.BlockSpec((rows, 2 * N), back)
    def scan(x_in, bc_in, halo, dt_raw):
        conv_out, y_local, steps, cumulative, begun, offsets, left, left_w = call(
            functools.partial(scan_kernel, pairs),
            (batch, count),
            [
                pl.BlockSpec((rows, inner), at),
                pl.BlockSpec((rows, 2 * N), at),
                pl.BlockSpec((1, HALO, inner + 2 * N), seq3),
                pl.BlockSpec((rows, heads), at),
                pl.BlockSpec((KERNEL, inner + 2 * N), fixed),
                row_heads,
                row_heads,
                row_inner,
            ],
            [
                pl.BlockSpec((rows, inner + 2 * N), at),
                pl.BlockSpec((rows, inner), at),
                pl.BlockSpec((rows, heads), at),
                pl.BlockSpec((rows, heads), at),
                pl.BlockSpec((1, N, inner), at3),
                pl.BlockSpec((1, 1, inner), at3),
                state_spec,
                pl.BlockSpec((1, 1, inner), seq3),
            ],
            [
                shaped(total, inner + 2 * N),
                shaped(total, inner),
                shaped(total, heads),
                shaped(total, heads),
                shaped(blocks, N, inner),
                shaped(blocks, 1, inner),
                shaped(batch, N, inner),
                shaped(batch, 1, inner),
            ],
            [
                pltpu.VMEM((HALO, inner + 2 * N), F32),
                pltpu.VMEM((N, inner), F32),
                pltpu.VMEM((8, heads), F32),
                pltpu.VMEM((8, inner), F32),
            ],
            micros=14.5,
        )(x_in, bc_in, halo, dt_raw, conv_w, bias_row, rate_row, skip_lanes)
        return conv_out, y_local, steps, cumulative, begun, offsets, left, left_w

    own_block = model // ring.size
    act_spec = pl.BlockSpec((rows, own_block), at)
    late_spec = pl.BlockSpec((own_block, inner), fixed)
    wide_scratch = [pltpu.VMEM((rows, inner), F32), pltpu.VMEM((rows, inner), F32)]

    def gate(y_local, conv_out, came, cumulative, z_part, dm_part, late):
        return call(
            functools.partial(gate_kernel, pairs),
            (batch, count),
            [
                block_spec, c_spec, state_spec, head_cols, block_spec, block_spec, row_inner,
                act_spec, act_spec, late_spec, late_spec,
            ],
            [block_spec, pl.BlockSpec((1, 2, rows), at3)],
            [shaped(total, inner), shaped(blocks, 2, rows)],
            wide_scratch,
            micros=7.0,
        )(y_local, conv_out, came, cumulative, z_part, dm_part, gate_f, *late)

    def gate_back(dm_part, ssd, z_part, gate_scale, product, cumulative, conv_out, late):
        return call(
            functools.partial(gate_back_kernel, pairs, inner_all),
            (batch, count),
            [
                block_spec, block_spec, block_spec, row_out, row_out, row_inner, head_cols, c_spec,
                act_spec, act_spec, late_spec, late_spec,
            ],
            [block_spec, block_spec, state_spec, row_out, row_inner, block_spec],
            [
                shaped(total, inner, dtype=BF16),
                shaped(total, inner),
                shaped(batch, N, inner),
                shaped(blocks, 1, rows),
                shaped(1, inner),
                shaped(total, inner, dtype=BF16),
            ],
            wide_scratch,
            micros=9.0,
        )(dm_part, ssd, z_part, gate_scale, product, gate_f, cumulative, conv_out, *late)

    def scan_back(conv_out, d_ssd, steps, begun, offsets, came):
        du_local, dbc_local = call(
            functools.partial(scan_back_kernel, pairs),
            (batch, count),
            [
                v_back, block_back, heads_back, row_heads,
                pl.BlockSpec((1, N, inner), back3),
                pl.BlockSpec((1, 1, inner), back3),
                state_spec,
            ],
            [block_back, bc_back],
            [shaped(total, inner), shaped(total, 2 * N)],
            [pltpu.VMEM((N, inner), F32)],
            micros=18.0,
        )(conv_out, d_ssd, steps, rate_row, begun, offsets, came)
        return du_local, dbc_local

    def finish(conv_out, d_ssd, du_local, ssd, steps, cumulative, left_w, later, came, left, dbc_local, dt_raw):
        lane_head = lax.broadcasted_iota(jnp.int32, (inner, heads), 0) // P_SIZE
        picker = (lane_head == lax.broadcasted_iota(jnp.int32, (inner, heads), 1)).astype(BF16)
        at_end = jnp.exp(left_w) * came + left
        d_conv_x, d_bc_part, d_dt, g_skip, g_heads = call(
            functools.partial(finish_kernel, pairs),
            (batch, count),
            [
                v_back, block_back, block_back, block_back, heads_back, heads_back,
                pl.BlockSpec((1, 1, inner), seq3), state_spec, state_spec, bc_back, heads_back,
                row_heads, row_heads, row_inner,
                pl.BlockSpec((inner, heads), fixed),
            ],
            [
                block_back, bc_back, heads_back, row_inner,
                pl.BlockSpec((2, heads), fixed),
            ],
            [
                shaped(total, inner, dtype=BF16),
                shaped(total, 2 * N),
                shaped(total, heads, dtype=BF16),
                shaped(1, inner),
                shaped(2, heads),
            ],
            [
                pltpu.VMEM((8, heads), F32),
                pltpu.VMEM((2 * rows, inner), BF16),
                pltpu.VMEM((2 * rows, inner), BF16),
            ],
            micros=15.0,
        )(
            conv_out, d_ssd, du_local, ssd, steps, cumulative, left_w, later, at_end, dbc_local,
            dt_raw, bias_row, rate_row, skip_lanes, picker,
        )
        return d_conv_x, d_bc_part, d_dt, g_skip, g_heads

    split_pass = ring.on and batch == 2
    forth, back_pass = Passing(ring, 1, inner), Passing(ring, -1, inner)
    slope = lambda v: silu_slope(v, jax.nn.sigmoid(v))

    edge_at = inner + 2 * N
    spare = -(2 * N + heads) % LANES
    per = w_z.shape[0]
    all_in = jnp.concatenate(
        [w_x, w_bc, w_dt, jnp.zeros((w_x.shape[0], spare), BF16)], axis=1
    )
    spots, order = (ring.spots(), ring.blocks()) if ring.on else (None, None)

    def work(all_in, slab):
        own_gain = own_features(ring, norm_gain.astype(F32), own_width)
        block = all_in + 0.0 * own_gain[:1].astype(BF16)
        square = head_sum(jnp.sum(slab * slab, axis=1))
        scale = lax.rsqrt(square / model + EPS)
        own_normed = (slab * scale[:, None] * own_gain).astype(BF16)
        return ring.hop((block, block)), own_gain, scale, own_normed

    hop1, own_gain, scale, own_normed = ring.phase(work, all_in, slab)
    far = across(ring, own_normed)

    def work(hop1, own, w_z, w_out, cot_rows):
        zo_in = jnp.concatenate([w_z, w_out.T], axis=0)
        return ring.hop(hop1), beside(ring, own), zo_in, cot_rows.astype(BF16)

    hop2, near, zo_in, own_cot = ring.phase(work, hop1, own_normed, w_z, w_out, cot_rows)
    hop3 = ring.phase(ring.hop, hop2)
    hop4, both = ring.phase(
        lambda hop3, far: (ring.last_hop(hop3), corner(ring, own_normed, far)), hop3, far
    )
    normed = (both, near, far, own_normed) if ring.on else (both,)

    def work(normed, hop1, hop2, hop3, hop4, zo_in):
        moving = ring.hop((zo_in, zo_in))
        if ring.on:
            x_in, bc_in, dt_raw, x_w, rest_w = with_spots(
                in_project_kernel, spots, normed, [all_in, *hop1, *hop2, *hop3, *hop4],
                [True, True, True, False, False],
                [
                    shaped(total, inner, dtype=BF16), shaped(total, 2 * N, dtype=BF16),
                    shaped(total, all_in.shape[1] - edge_at), shaped(model, inner, dtype=BF16),
                    shaped(model, all_in.shape[1] - inner, dtype=BF16),
                ],
            )
        else:
            x_w = lax.all_gather(w_x, "seq", axis=0, tiled=True)
            rest_w = lax.all_gather(all_in[:, inner:], "seq", axis=0, tiled=True)
            rest = dot(normed[0], rest_w)
            x_in, bc_in = dot(normed[0], x_w).astype(BF16), rest[:, : 2 * N].astype(BF16)
            dt_raw = rest[:, 2 * N :]
        return moving, x_in, bc_in, dt_raw[:, :heads], x_w, rest_w, edge([x_in, bc_in], True)

    hop1, x_in, bc_in, dt_raw, x_w, rest_w, halo = ring.phase(
        work, normed, hop1, hop2, hop3, hop4, zo_in
    )

    def work(hop1, x_in, bc_in, halo, dt_raw, own_cot):
        scanned = scan(x_in, bc_in, halo, dt_raw)
        held = forth.pair(forth.begin(scanned[6], scanned[7])) if split_pass else ()
        return ring.hop(hop1), scanned, held, beside(ring, own_cot), across(ring, own_cot)

    hop2, scanned, held, near, far = ring.phase(work, hop1, x_in, bc_in, halo, dt_raw, own_cot)
    conv_out, y_local, steps, cumulative, begun, offsets, left, left_w = scanned
    first = jnp.where(here == 0, 1.0, 0.0)
    once = lax.broadcasted_iota(jnp.int32, (1, all_in.shape[1]), 1)
    once = jnp.where((once < inner) | (once >= edge_at), 1.0, first)

    def work(hop2, held, far, rest_w):
        held = forth.next_line(held) if split_pass else ()
        return ring.hop(hop2), held, corner(ring, own_cot, far), rest_w * once[:, inner:].astype(BF16)

    hop3, held, both, rest_once = ring.phase(work, hop2, held, far, rest_w)
    cot = (both, near, far, own_cot) if ring.on else (both,)

    def work(hop1, hop2, hop3, held, normed, cot):
        held = forth.further_lines(held) if split_pass else ()
        if ring.on:
            wide, weight = shaped(total, inner), shaped(model, inner, dtype=BF16)
            act = shaped(total, own_block, dtype=BF16)
            given = with_spots(
                gate_project_kernel, spots, (*normed, *cot), [zo_in, *hop1, *hop2, *hop3],
                [True, True, False, False, True, True], [wide, wide, weight, weight, act, act],
            )
        else:
            z_w = lax.all_gather(w_z, "seq", axis=0, tiled=True)
            out_w = lax.all_gather(w_out.T, "seq", axis=0, tiled=True)
            none = jnp.zeros((total, own_block), BF16)
            given = dot(normed[0], z_w), dot(cot[0], out_w), z_w, out_w, none, none
        return ring.last_hop(hop3), held, given

    hop4, held, given = ring.phase(work, hop1, hop2, hop3, held, normed, cot)
    z_part, dm_part, z_w, out_w, normed_last, cot_last = given
    if not ring.on:
        hop4 = (jnp.zeros((own_block, inner), BF16),) * 2
    late = (normed_last, cot_last, *hop4)
    came = ring.phase(
        lambda held: forth.end(held) if split_pass else states_scan(left, left_w, 1), held
    )

    ssd, square_g = gate(y_local, conv_out, came, cumulative, z_part, dm_part, late)
    square_g = head_sum(square_g)
    gate_scale = lax.rsqrt(square_g[:, 0:1] / inner_all + EPS)
    product = square_g[:, 1:2]
    d_z, d_ssd, d_left, met_z, g_gate, mixed = gate_back(
        dm_part, ssd, z_part, gate_scale, product, cumulative, conv_out, late
    )

    def work(d_left, left_w, normed, d_z, mixed, cot):
        held = back_pass.pair(back_pass.begin(d_left, left_w)) if split_pass else ()
        if ring.on:
            g_zo = outer(order, (normed, [d_z]), (cot, [mixed]))
        else:
            g_zo = (dot(normed[0], d_z, TN), dot(cot[0], mixed, TN))
        return held, g_zo

    held, g_zo = ring.phase(work, d_left, left_w, normed, d_z, mixed, cot)

    def work(held, g_zo, conv_out, d_ssd, steps, begun, offsets, came):
        sent = ring.send(g_zo)
        held = back_pass.next_line(held) if split_pass else ()
        back = scan_back(conv_out, d_ssd, steps, begun, offsets, came)
        return held, ring.add(g_zo, sent, 3), back

    held, sums, (du_local, dbc_local) = ring.phase(
        work, held, g_zo, conv_out, d_ssd, steps, begun, offsets, came
    )

    def work(held, mixed, out_w, late_w):
        held = back_pass.further_lines(held) if split_pass else ()
        return held, project(ring, spots, [mixed], [out_w], [late_w])

    held, branch = ring.phase(work, held, mixed, out_w, hop4[1])

    def work(held, branch):
        later = back_pass.end(held) if split_pass else states_scan(d_left, left_w, -1)
        return later, scatter_near(ring, branch)

    later, (out_far, out_own) = ring.phase(work, held, branch)

    def work(later, sums, g_zo, du_local, dbc_local):
        sums = ring.hop(sums)
        d_conv_x, d_bc_part, d_dt, g_skip, g_heads = finish(
            conv_out, d_ssd, du_local, ssd, steps, cumulative, left_w, later, came, left,
            dbc_local, dt_raw,
        )
        after_x = edge([d_conv_x], False)
        v_bc = conv_out[:, inner:]
        if ring.on:
            half, quarter = total // 2, total // 4
            low, high = here & 1, here >> 1
            cut = lambda a, at, n: lax.dynamic_slice_in_dim(a, at, n, 0)
            mine = cut(d_bc_part, low * half, half)
            mine = mine + swap(cut(d_bc_part, (1 - low) * half, half), "head", 1)
            given = swap(cut(mine, (1 - high) * quarter, quarter), "head", 2)
            mine = cut(mine, high * quarter, quarter) + given
            mine = (mine * slope(cut(v_bc, low * half + high * quarter, quarter))).astype(BF16)
            given = swap(mine, "head", 2)
            mine = jnp.where(
                high == 0, jnp.concatenate([mine, given], 0), jnp.concatenate([given, mine], 0)
            )
            given = swap(mine, "head", 1)
            d_conv_bc = jnp.where(
                low == 0, jnp.concatenate([mine, given], 0), jnp.concatenate([given, mine], 0)
            )
        else:
            d_conv_bc = (head_sum(d_bc_part) * slope(v_bc)).astype(BF16)
        after_bc = edge([d_conv_bc], False)
        sums = ring.add(g_zo, sums, 2)
        return sums, d_conv_x, after_x, d_conv_bc, after_bc, d_dt, g_skip, g_heads

    sums, d_conv_x, after_x, d_conv_bc, after_bc, d_dt, g_skip, g_heads = ring.phase(
        work, later, sums, g_zo, du_local, dbc_local
    )
    out_far = across(ring, out_far)

    def work(sums, g_zo, d_conv_x, after_x, d_conv_bc, after_bc, d_dt, normed):
        sums = ring.add(g_zo, ring.hop(sums), 1)
        d_x, g_conv_x, met_x = conv_back(d_conv_x, x_in, after_x, conv_xf, batch, length, rows)
        d_bc, g_conv_bc, met_bc = conv_back(
            d_conv_bc, bc_in, after_bc, conv_bcf, batch, length, rows
        )
        fill = jnp.zeros((total, spare), BF16)
        d_rest = jnp.concatenate([d_bc, d_dt, fill], axis=1)
        if ring.on:
            g_all = outer(order, (normed, [d_x, d_rest]))
        else:
            g_all = jnp.concatenate([dot(normed[0], d, TN) for d in (d_x, d_rest)], axis=1)
        met_dt = jnp.sum(d_dt.astype(F32) * dt_raw, axis=1)
        met = (met_z + met_x + first * met_bc).reshape(total) + met_dt
        return sums, d_x, d_rest, g_conv_x, g_conv_bc, met, g_all

    sums, d_x, d_rest, g_conv_x, g_conv_bc, met, g_all = ring.phase(
        work, sums, g_zo, d_conv_x, after_x, d_conv_bc, after_bc, d_dt, normed
    )
    small = jnp.concatenate(
        [
            g_conv_x.reshape(-1), g_conv_bc.reshape(-1), g_gate.reshape(-1),
            g_skip.reshape(-1), g_heads.reshape(-1),
        ]
    )

    def one_swap(array, bit):
        return array + swap(array, "seq", bit) if ring.on else array

    def work(sums, g_zo, g_all, small, d_z, d_x, d_rest, z_w, x_w, rest_once, late_w, met):
        last = ring.hop(sums)
        sent = ring.send(g_all)
        back = project(ring, spots, [d_z, d_x, d_rest], [z_w, x_w, rest_once], [late_w])
        return (
            ring.total(g_zo, last) if ring.on else [ring.total(g, None) for g in g_zo],
            ring.add(g_all, sent, 3), back, one_swap(small, 1), head_sum(met) / scale,
        )

    g_zo, sums, back_terms, small, dots = ring.phase(
        work, sums, g_zo, g_all, small, d_z, d_x, d_rest, z_w, x_w, rest_once, hop4[0], met
    )
    g_z, g_out = (g_zo[:per], g_zo[per:]) if ring.on else g_zo

    def work(sums, g_all, small, back_terms, out_far, out_own, slab):
        mixed_out = slab + scatter_sum(ring, out_far, out_own)
        return (
            ring.add(g_all, ring.hop(sums), 2), scatter_near(ring, back_terms),
            one_swap(small, 2), mixed_out,
        )

    sums, (far, d_normed), small, mixed_out = ring.phase(
        work, sums, g_all, small, back_terms, out_far, out_own, slab
    )
    far = across(ring, far)

    def work(sums, g_all, small, g_z):
        return (
            ring.add(g_all, ring.hop(sums), 1), one_swap(small, 4),
            jnp.sum(g_z * w_z.astype(F32), axis=1), g_out.T,
        )

    sums, small, met_f, g_out = ring.phase(work, sums, g_all, small, g_z)
    if not ring.on:
        small = lax.psum(small, "seq")

    def work(sums, g_all, far, d_normed, slab, dots, met_f):
        last = ring.hop(sums)
        d_normed = scatter_sum(ring, far, d_normed)
        grad_tokens = (
            cot_rows
            + (scale[:, None] * own_gain) * d_normed
            - slab * (scale * scale * scale * dots / model)[:, None]
        )
        g_all = ring.total(g_all, last)
        met_f = met_f + jnp.sum(g_all * all_in.astype(F32) * once, axis=1)
        g_gain = head_sum(met_f) / norm_gain.astype(F32)
        return (
            g_all[:, :inner], g_all[:, inner:edge_at], g_all[:, edge_at : edge_at + heads],
            grad_tokens, g_gain,
        )

    g_x, g_bc, g_dt, grad_tokens, g_gain = ring.phase(
        work, sums, g_all, far, d_normed, slab, dots, met_f
    )

    cuts = [KERNEL * inner, KERNEL * 2 * N, inner, inner, heads, heads]
    parts, start = [], 0
    for width in cuts:
        parts.append(small[start : start + width])
        start += width
    sum_x, sum_bc, sum_gate, sum_skip, sum_bias, sum_rate = parts

    return (
        mixed_out.reshape(batch, length, own_width),
        grad_tokens.reshape(batch, length, own_width),
        g_gain,
        g_z,
        g_x,
        g_bc,
        g_dt,
        sum_x.reshape(KERNEL, inner),
        sum_bc.reshape(KERNEL, 2 * N),
        sum_bias,
        sum_rate,
        jnp.sum(sum_skip.reshape(heads, P_SIZE), axis=1),
        sum_gate,
        g_out,
    )


def solution(mesh):
    in_specs = (
        P(None, "seq", "head"),
        P("seq"),
        P("seq", "head"),
        P("seq", "head"),
        P("seq", None),
        P("seq", "head"),
        P(None, "head"),
        P(),
        P("head"),
        P("head"),
        P("head"),
        P("head"),
        P("head", "seq"),
        P(None, "seq", "head"),
    )
    out_specs = (
        P(None, "seq", "head"),
        P(None, "seq", "head"),
        P("seq"),
        P("seq", "head"),
        P("seq", "head"),
        P("seq", None),
        P("seq", "head"),
        P(None, "head"),
        P(),
        P("head"),
        P("head"),
        P("head"),
        P("head"),
        P("head", "seq"),
    )
    return jax.shard_map(body, mesh=mesh, in_specs=in_specs, out_specs=out_specs, check_vma=False)
```

```python
import functools

import jax
import jax.numpy as jnp
from jax import lax
from jax.experimental import pallas as pl
from jax.experimental.pallas import tpu as pltpu
from jax.sharding import PartitionSpec as P

P_SIZE = 64
N = 128
KERNEL = 4
SPAN = 128
HALO = 8
ADD_STEPS = 2
LANES = 128
EPS = 1e-05
HIGHEST = lax.Precision.HIGHEST
F32 = jnp.float32
BF16 = jnp.bfloat16
VMEM_LIMIT = 50 * 1024 * 1024
NN = (((1,), (0,)), ((), ()))
NT = (((1,), (1,)), ((), ()))
TN = (((0,), (0,)), ((), ()))


def lasts(micros):
    return pl.CostEstimate(flops=0, bytes_accessed=int(micros * 3.3e6), transcendentals=0)


def dot(left, right, dims=NN, precision=None):
    return lax.dot_general(left, right, dims, precision=precision, preferred_element_type=F32)


def silu_slope(value, logistic):
    return logistic * (1.0 + value * (1.0 - logistic))


class Ring:
    def __init__(self, size):
        self.size = size
        self.on = size == 8 and lax.axis_size("head") == 4
        self.order = list(range(0, size, 2)) + list(range(size - 1, 0, -2))
        here = lax.axis_index("seq")
        self.line, self.side = here >> 1, here & 1
        self.place = jnp.where(self.side == 0, self.line, size - 1 - self.line)

    def spots(self):
        place = (self.place + jnp.arange(self.size, dtype=jnp.int32)) & (self.size - 1)
        side = place >> 2
        line = jnp.where(side == 1, self.size - 1 - place, place)
        bit = lax.axis_index("head") ^ line
        return 2 * jnp.where(bit == 3, 0, jnp.where(bit == 0, 3, bit)) + side

    def blocks(self):
        spot = jnp.arange(self.size, dtype=jnp.int32)
        side, bit = spot & 1, spot >> 1
        bit = jnp.where(bit == 0, 3, jnp.where(bit == 3, 0, bit))
        line = lax.axis_index("head") ^ bit
        place = jnp.where(side == 1, self.size - 1 - line, line)
        return (place - self.place) & (self.size - 1)

    def shift(self, array, by):
        order, size = self.order, self.size
        return lax.ppermute(array, "seq", [(order[i], order[(i + by) % size]) for i in range(size)])

    def hop(self, moving):
        if not self.on:
            return moving
        return self.shift(moving[0], 1), self.shift(moving[1], -1)

    def last_hop(self, moving):
        if not self.on:
            return moving
        cut = moving[0].shape[0] // 2
        return self.shift(moving[0][:cut], 1), self.shift(moving[1][cut:], -1)

    def part(self, whole, k):
        n = whole.shape[0] // self.size
        k = k % self.size
        return whole[k * n : (k + 1) * n]

    def send(self, first, second):
        return self.shift(first, 1), self.shift(second, -1)

    def add(self, whole, came, k):
        if not self.on:
            return ()
        rows, columns = whole.shape[0] // self.size, whole.shape[1]
        halves = k == self.size // 2 - 1
        steps = ADD_STEPS
        tile = rows // steps

        def kernel(a_ref, b_ref, right_ref, left_ref, out_a_ref, out_b_ref):
            right, left = right_ref[...].astype(F32), left_ref[...].astype(F32)
            if halves:
                upper = pl.program_id(0) < steps // 2
                right, left = jnp.where(upper, right, 0.0), jnp.where(upper, 0.0, left)
            out_a_ref[...] = (a_ref[...].astype(F32) + right).astype(BF16)
            out_b_ref[...] = (b_ref[...].astype(F32) + left).astype(BF16)

        block = lambda at: pl.BlockSpec((tile, columns), at)
        plain = lambda i: (i, 0)
        out = jax.ShapeDtypeStruct((rows, columns), BF16)
        return pl.pallas_call(
            kernel,
            grid=(steps,),
            in_specs=[
                block(lambda i: (steps * k + i, 0)),
                block(lambda i: (steps * (self.size - k) + i, 0)),
                block((lambda i: (jnp.minimum(i, steps // 2 - 1), 0)) if halves else plain),
                block((lambda i: (jnp.maximum(i - steps // 2, 0), 0)) if halves else plain),
            ],
            out_specs=[block(plain), block(plain)],
            out_shape=[out, out],
            compiler_params=pltpu.CompilerParams(vmem_limit_bytes=VMEM_LIMIT),
        )(whole, whole, *came)

    def phase(self, work, *args):
        if not self.on:
            return work(*args)
        shapes = jax.eval_shape(work, *args)

        def idle(*args):
            return jax.tree.map(lambda x: jnp.zeros(x.shape, x.dtype), shapes)

        return lax.cond(lax.axis_index("seq") < self.size, work, idle, *args)


def swap(array, axis, bit):
    size = lax.axis_size(axis)
    return lax.ppermute(array, axis, [(i, i ^ bit) for i in range(size)])


def head_sum(array):
    return lax.psum(array, "head")


def seq_sum(ring, array):
    if not ring.on:
        return lax.psum(array, "seq")
    bit = 1
    while bit < ring.size:
        array = array + swap(array, "seq", bit)
        bit *= 2
    return array


def own_features(ring, block, own_width):
    if not ring.on:
        whole = lax.all_gather(block, "seq", axis=0, tiled=True)
        return lax.dynamic_slice_in_dim(whole, lax.axis_index("head") * own_width, own_width)

    def fetch(flip):
        index = lambda line, side, head: (2 * line + side) * 4 + head
        return lax.ppermute(
            block,
            ("seq", "head"),
            [
                (index(head, side ^ flip, line), index(line, side, head))
                for line in range(4)
                for side in range(2)
                for head in range(4)
            ],
        )

    same, other = fetch(0), fetch(1)
    even = ring.side == 0
    return jnp.concatenate([jnp.where(even, same, other), jnp.where(even, other, same)])


def corner(ring, own, far):
    if not ring.on:
        return lax.all_gather(own, "head", axis=1, tiled=True)
    return swap(far, "head", 1)


def beside(ring, array):
    return swap(array, "head", 1) if ring.on else array


def across(ring, array):
    return swap(array, "head", 2) if ring.on else array


def scatter_near(ring, whole):
    if not ring.on:
        return whole, None
    width = whole.shape[1] // 4
    part = lambda k: whole[:, k * width : (k + 1) * width]
    far = swap(part(0), "head", 1)
    near = swap(part(1), "head", 1)
    far = (part(2).astype(F32) + far.astype(F32)).astype(BF16)
    return far, part(3).astype(F32) + near.astype(F32)


def scatter_sum(ring, far, mine):
    if not ring.on:
        return lax.psum_scatter(far, "head", scatter_dimension=1, tiled=True).astype(F32)
    return mine + far.astype(F32)


def shift_flat(array, by):
    size = lax.axis_size("seq")
    return lax.ppermute(array, "seq", [(i, i + by) for i in range(size) if 0 <= i + by < size])


def states_scan(state, log_decay, direction):
    incl_s, incl_w = state, log_decay
    excl_s, excl_w = jnp.zeros_like(state), jnp.zeros_like(log_decay)
    by = 1
    while by < lax.axis_size("seq"):
        got_s = shift_flat(incl_s.astype(BF16), by * direction).astype(F32)
        got_w = shift_flat(incl_w, by * direction)
        excl_s = jnp.exp(excl_w) * got_s + excl_s
        excl_w = excl_w + got_w
        incl_s = jnp.exp(incl_w) * got_s + incl_s
        incl_w = incl_w + got_w
        by *= 2
    return excl_s


def log_rows(log_decay):
    high = log_decay.astype(BF16).astype(F32)
    middle = (log_decay - high).astype(BF16).astype(F32)
    low = log_decay - high - middle
    row = lax.broadcasted_iota(jnp.int32, (16, log_decay.shape[1]), 0)
    parts = jnp.where(row == 0, high, jnp.where(row == 1, middle, low))
    return jnp.where(row < 3, parts, 0.0).astype(BF16)


def log_sum(rows):
    rows = rows.astype(F32)
    return rows[0:1] + rows[1:2] + rows[2:3]


def pass_begin_kernel(even_ref, lead_ref, state_ref, log_ref, keep_ref, kept_ref, send_ref):
    even = even_ref[0] == 1
    keep_ref[...] = jnp.where(even, state_ref[0], state_ref[1])
    kept_ref[...] = jnp.where(even, log_ref[0], log_ref[1])
    send_ref[:N] = jnp.where(even, state_ref[1], state_ref[0]).astype(BF16)
    send_ref[N:] = log_rows(jnp.where(even, log_ref[1], log_ref[0]))


def pass_pair_kernel(
    even_ref, lead_ref, keep_ref, kept_ref, got_ref, first_ref, d_first_ref, both_ref, pair_ref, send_ref
):
    leads = lead_ref[0] == 1
    keep, kept = keep_ref[...], kept_ref[...]
    got, gotten = got_ref[:N].astype(F32), log_sum(got_ref[N:])
    first = jnp.where(leads, keep, got)
    both = jnp.exp(jnp.where(leads, gotten, kept)) * first + jnp.where(leads, got, keep)
    first_ref[...] = first
    d_first_ref[...] = jnp.exp(jnp.where(leads, kept, gotten))
    both_ref[...] = both
    pair_ref[...] = jnp.exp(kept + gotten)
    send_ref[:N] = both.astype(BF16)
    send_ref[N:] = log_rows(kept + gotten)


def pass_line_kernel(even_ref, lead_ref, both_ref, pair_ref, got_ref, carry_ref, before_ref, send_ref):
    carry = got_ref[:N].astype(F32)
    carry_ref[...] = carry
    before_ref[...] = jnp.exp(log_sum(got_ref[N:]))
    send_ref[...] = (pair_ref[...] * carry + both_ref[...]).astype(BF16)


def pass_far_kernel(
    even_ref, lead_ref, first_ref, d_first_ref, carry_ref, before_ref, got_ref, mine_ref, send_ref
):
    leads = lead_ref[0] == 1
    carry = before_ref[...] * got_ref[...].astype(F32) + carry_ref[...]
    further = d_first_ref[...] * carry + first_ref[...]
    mine_ref[...] = jnp.where(leads, carry, further)
    send_ref[...] = jnp.where(leads, further, carry).astype(BF16)


def pass_end_kernel(even_ref, lead_ref, mine_ref, got_ref, out_ref):
    even = even_ref[0] == 1
    mine, got = mine_ref[...], got_ref[...].astype(F32)
    out_ref[0] = jnp.where(even, mine, got)
    out_ref[1] = jnp.where(even, got, mine)


class Passing:
    def __init__(self, ring, direction, inner):
        self.direction = direction
        leads = ring.side == 0 if direction > 0 else ring.side == 1
        self.flags = [jnp.where(f, 1, 0).astype(jnp.int32).reshape(1) for f in (ring.side == 0, leads)]
        row = shaped(1, inner)
        self.state, self.row = shaped(N, inner), row
        self.sent, self.sent_log = shaped(N, inner, dtype=BF16), shaped(N + 16, inner, dtype=BF16)

    def step(self, kernel, outs, *args):
        return pl.pallas_call(
            kernel,
            in_specs=[pl.BlockSpec(memory_space=pltpu.SMEM)] * 2
            + [pl.BlockSpec(memory_space=pltpu.VMEM)] * len(args),
            out_specs=jax.tree.map(lambda _: pl.BlockSpec(memory_space=pltpu.VMEM), outs),
            out_shape=outs,
            compiler_params=pltpu.CompilerParams(vmem_limit_bytes=VMEM_LIMIT),
        )(*self.flags, *args)

    def begin(self, state, log_decay):
        return self.step(pass_begin_kernel, [self.state, self.row, self.sent_log], state, log_decay)

    def pair(self, held):
        keep, kept, send = held
        got = swap(send, "seq", 1)
        outs = [self.state, self.row, self.state, self.row, self.sent_log]
        return self.step(pass_pair_kernel, outs, keep, kept, got)

    def next_line(self, held):
        first, d_first, both, pair, send = held
        got = shift_flat(send, 2 * self.direction)
        outs = [self.state, self.row, self.sent]
        return (first, d_first, *self.step(pass_line_kernel, outs, both, pair, got))

    def further_lines(self, held):
        first, d_first, carry, before, send = held
        got = shift_flat(send, 4 * self.direction)
        outs = [self.state, self.sent]
        return self.step(pass_far_kernel, outs, first, d_first, carry, before, got)

    def end(self, held):
        mine, send = held
        out = shaped(2, *self.state.shape)
        return self.step(pass_end_kernel, out, mine, swap(send, "seq", 1))


def lane_is_low(rows):
    return lax.broadcasted_iota(jnp.int32, (rows, LANES), 1) < P_SIZE


def spread(columns, j, rows):
    low = jnp.broadcast_to(columns[:, 2 * j : 2 * j + 1], (rows, LANES))
    high = jnp.broadcast_to(columns[:, 2 * j + 1 : 2 * j + 2], (rows, LANES))
    return jnp.where(lane_is_low(rows), low, high), low, high


def triangle(rows, keep):
    first = lax.broadcasted_iota(jnp.int32, (rows, rows), 0)
    second = lax.broadcasted_iota(jnp.int32, (rows, rows), 1)
    return keep(first, second)


def decays(rates, rows):
    lower = triangle(rows, lambda t, s: t >= s)
    within = dot(lower.astype(F32), rates, NN, HIGHEST)
    upper = triangle(rows, lambda s, t: s <= t).astype(F32)
    within_t = dot(rates, upper, TN, HIGHEST)
    return within, within_t, lower


def window(column, row, keep):
    rows = row.shape[1]
    return jnp.exp(jnp.where(keep, column[:, :rows] - row, -1e30))


def scan_kernel(
    pairs, x_ref, bc_ref, halo_ref, dt_ref, cw_ref, bias_ref, rate_ref, skip_ref,
    v_ref, y_ref, st_ref, wc_ref, sb_ref, wo_ref, sl_ref, we_ref,
    hal, state, off, off_l,
):
    rows = x_ref.shape[0]
    inner = pairs * LANES

    @pl.when(pl.program_id(1) == 0)
    def _():
        hal[...] = halo_ref[0]
        state[...] = jnp.zeros_like(state)
        off[...] = jnp.zeros_like(off)
        off_l[...] = jnp.zeros_like(off_l)

    def convolve(ref, at, start):
        now = ref[:, start : start + LANES].astype(F32)
        chunk = jnp.concatenate([hal[:, at : at + LANES], now], axis=0)
        hal[:, at : at + LANES] = now[rows - HALO :]
        shift = HALO - KERNEL + 1
        out = cw_ref[0:1, at : at + LANES] * chunk[shift : shift + rows]
        for k in range(1, KERNEL):
            out = out + cw_ref[k : k + 1, at : at + LANES] * chunk[shift + k : shift + k + rows]
        v_ref[:, at : at + LANES] = out
        return out * jax.nn.sigmoid(out)

    bmat = convolve(bc_ref, inner, 0)
    cmat = convolve(bc_ref, inner + LANES, LANES)
    b_half, c_half = bmat.astype(BF16), cmat.astype(BF16)
    scores = dot(cmat, bmat, NT, HIGHEST)
    steps = jax.nn.softplus(dt_ref[...] + bias_ref[...])
    rates = steps * -rate_ref[...]
    within, within_t, lower = decays(rates, rows)
    low_lanes = lane_is_low(rows)
    st_ref[...] = steps
    wc_ref[...] = off[0:1] + within
    off[0:1] = off[0:1] + within[rows - 1 : rows]
    wo_ref[0] = off_l[0:1]
    for j in range(pairs):
        at = slice(j * LANES, (j + 1) * LANES)
        x = convolve(x_ref, j * LANES, j * LANES)
        u = x * spread(steps, j, rows)[0]
        u_half = u.astype(BF16)
        grow, low, high = spread(within, j, rows)
        end = grow[rows - 1 : rows]
        a_low = (window(low, within_t[2 * j : 2 * j + 1], lower) * scores).astype(BF16)
        a_high = (window(high, within_t[2 * j + 1 : 2 * j + 2], lower) * scores).astype(BF16)
        inside = jnp.where(low_lanes, dot(a_low, u_half), dot(a_high, u_half))
        before = state[:, at]
        carried = jnp.exp(grow) * dot(c_half, before.astype(BF16))
        y_ref[:, at] = inside + carried + skip_ref[0:1, at] * x
        tail = (u * jnp.exp(end - grow)).astype(BF16)
        sb_ref[0, :, at] = before
        after = jnp.exp(end) * before + dot(b_half, tail, TN)
        state[:, at] = after
        sl_ref[0, :, at] = after
        ends = off_l[0:1, at] + end
        off_l[0:1, at] = ends
        we_ref[0, :, at] = ends


def gate_kernel(
    pairs, y_ref, vc_ref, s_ref, wc_ref, zp_ref, dmp_ref, gg_ref, na_ref, ca_ref, wz_ref, wo_ref,
    ssd_ref, sq_ref, z_ref, dm_ref
):
    rows = y_ref.shape[0]
    z_ref[...] = zp_ref[...] + dot(na_ref[...], wz_ref[...])
    dm_ref[...] = dmp_ref[...] + dot(ca_ref[...], wo_ref[...])
    vc = vc_ref[...]
    c_half = (vc * jax.nn.sigmoid(vc)).astype(BF16)
    cumulative = wc_ref[...]
    total = jnp.zeros((rows, LANES), F32)
    meet = jnp.zeros((rows, LANES), F32)
    for j in range(pairs):
        at = slice(j * LANES, (j + 1) * LANES)
        grow = jnp.exp(spread(cumulative, j, rows)[0])
        ssd = y_ref[:, at] + grow * dot(c_half, s_ref[0, :, at].astype(BF16))
        ssd_ref[:, at] = ssd
        z = z_ref[:, at]
        gated = ssd * (z * jax.nn.sigmoid(z))
        total = total + gated * gated
        meet = meet + dm_ref[:, at] * gg_ref[0:1, at] * gated
    sq_ref[0, 0:1] = jnp.sum(total.T, axis=0, keepdims=True)
    sq_ref[0, 1:2] = jnp.sum(meet.T, axis=0, keepdims=True)


def as_column(row):
    return jnp.broadcast_to(row, (LANES, row.shape[1])).T


def gate_back_kernel(
    pairs, width, dmp_ref, ssd_ref, zp_ref, gs_ref, ip_ref, gg_ref, wc_ref, vc_ref,
    na_ref, ca_ref, wz_ref, wo_ref,
    dz_ref, dy_ref, ds_ref, zz_ref, gate_ref, mixed_ref, z_ref, dm_ref,
):
    rows = dmp_ref.shape[0]
    z_ref[...] = zp_ref[...] + dot(na_ref[...], wz_ref[...])
    dm_ref[...] = dmp_ref[...] + dot(ca_ref[...], wo_ref[...])

    @pl.when(pl.program_id(1) == 0)
    def _():
        ds_ref[...] = jnp.zeros_like(ds_ref)

    @pl.when((pl.program_id(0) == 0) & (pl.program_id(1) == 0))
    def _():
        gate_ref[...] = jnp.zeros_like(gate_ref)

    scale = as_column(gs_ref[0])
    pull = as_column(gs_ref[0] * gs_ref[0] * gs_ref[0] * ip_ref[0] * (1.0 / width))
    vc = vc_ref[...]
    c_half = (vc * jax.nn.sigmoid(vc)).astype(BF16)
    cumulative = wc_ref[...]
    total = jnp.zeros((rows, LANES), F32)
    for j in range(pairs):
        at = slice(j * LANES, (j + 1) * LANES)
        z = z_ref[:, at]
        ssd = ssd_ref[:, at]
        logistic = jax.nn.sigmoid(z)
        opened = z * logistic
        gated = ssd * opened
        mixed_ref[:, at] = (gated * scale * gg_ref[0:1, at]).astype(BF16)
        scaled = scale * dm_ref[:, at]
        gate_ref[0:1, at] += jnp.sum(scaled * gated, axis=0, keepdims=True)
        d_gated = scaled * gg_ref[0:1, at] - gated * pull
        d_z = (d_gated * ssd * silu_slope(z, logistic)).astype(BF16)
        dz_ref[:, at] = d_z
        total = total + d_z.astype(F32) * z
        dy = d_gated * opened
        dy_ref[:, at] = dy
        grown = (jnp.exp(spread(cumulative, j, rows)[0]) * dy).astype(BF16)
        ds_ref[0, :, at] += dot(c_half, grown, TN)
    zz_ref[0] = jnp.sum(total.T, axis=0, keepdims=True)


def scan_back_kernel(
    pairs, v_ref, dy_ref, st_ref, rate_ref, sb_ref, wo_ref, s_ref,
    du_ref, dbc_ref, grad,
):
    rows = v_ref.shape[0]
    inner = pairs * LANES

    @pl.when(pl.program_id(1) == 0)
    def _():
        grad[...] = jnp.zeros_like(grad)

    def act(at):
        value = v_ref[:, at : at + LANES]
        return value * jax.nn.sigmoid(value)

    bmat, cmat = act(inner), act(inner + LANES)
    b_half, c_half = bmat.astype(BF16), cmat.astype(BF16)
    scores = dot(cmat, bmat, NT, HIGHEST)
    steps = st_ref[...]
    rates = steps * -rate_ref[...]
    within, within_t, lower = decays(rates, rows)
    low_lanes = lane_is_low(rows)
    d_c = jnp.zeros((rows, LANES), F32)
    d_b = jnp.zeros((rows, LANES), F32)
    d_scores = jnp.zeros((rows, rows), F32)
    none = jnp.zeros((rows, LANES), BF16)
    for j in range(pairs):
        at = slice(j * LANES, (j + 1) * LANES)
        x = act(j * LANES)
        u = x * spread(steps, j, rows)[0]
        u_half = u.astype(BF16)
        dy = dy_ref[:, at]
        dy_half = dy.astype(BF16)
        grow, low, high = spread(within, j, rows)
        end = grow[rows - 1 : rows]
        back = jnp.exp(end - grow)
        grown = (jnp.exp(grow) * dy).astype(BF16)
        begun = sb_ref[0, :, at] + jnp.exp(wo_ref[0, :, at]) * s_ref[0, :, at]
        d_c = d_c + dot(grown, begun.astype(BF16), NT)
        later = grad[:, at]
        later_half = later.astype(BF16)
        d_b = d_b + dot((u * back).astype(BF16), later_half, NT)
        w_low = window(low, within_t[2 * j : 2 * j + 1], lower)
        w_high = window(high, within_t[2 * j + 1 : 2 * j + 2], lower)
        d_scores = d_scores + w_low * dot(jnp.where(low_lanes, dy_half, none), u_half, NT)
        d_scores = d_scores + w_high * dot(jnp.where(low_lanes, none, dy_half), u_half, NT)
        a_low = (w_low * scores).astype(BF16)
        a_high = (w_high * scores).astype(BF16)
        inside = jnp.where(low_lanes, dot(a_low, dy_half, TN), dot(a_high, dy_half, TN))
        du_ref[:, at] = inside + back * dot(b_half, later_half)
        grad[:, at] = jnp.exp(end) * later + dot(c_half, grown, TN)
    d_half = d_scores.astype(BF16)
    dbc_ref[:, :LANES] = d_b + dot(d_half, c_half, TN)
    dbc_ref[:, LANES:] = d_c + dot(d_half, b_half)


def put_split(ref, at, value):
    rows = value.shape[0]
    high = value.astype(BF16)
    ref[:rows, at] = high
    ref[rows : 2 * rows, at] = (value - high.astype(F32)).astype(BF16)


def per_head(ref, picker, rows):
    both = dot(ref[: 2 * rows], picker)
    return both[:rows] + both[rows:]


def finish_kernel(
    pairs, split, v_ref, dy_ref, du_ref, ssd_ref, st_ref, wc_ref, we_ref, la_ref, se_ref, dbc_ref,
    dt_ref, bias_ref, rate_ref, skip_ref, pick_ref, at_ref,
    dcx_ref, keep_ref, send_ref, ddt_ref, dskip_ref, dhead_ref, run, moves, drives,
):
    rows = v_ref.shape[0]
    inner = pairs * LANES
    picker = pick_ref[...]

    @pl.when((pl.program_id(0) == 0) & (pl.program_id(1) == 0))
    def _():
        dskip_ref[...] = jnp.zeros_like(dskip_ref)
        dhead_ref[...] = jnp.zeros_like(dhead_ref)

    @pl.when(pl.program_id(1) == 0)
    def _():
        for j in range(pairs):
            at = slice(j * LANES, (j + 1) * LANES)
            both = jnp.sum(la_ref[0, :, at] * se_ref[0, :, at], axis=0, keepdims=True)
            put_split(moves, at, jnp.broadcast_to(both, (rows, LANES)))
        run[...] = per_head(moves, picker, rows)[0:8]

    value_b = v_ref[:, inner : inner + LANES]
    b_half = (value_b * jax.nn.sigmoid(value_b)).astype(BF16)
    steps = st_ref[...]
    cumulative = wc_ref[...]
    d_b = dbc_ref[:, :LANES]
    for j in range(pairs):
        at = slice(j * LANES, (j + 1) * LANES)
        value = v_ref[:, at]
        logistic = jax.nn.sigmoid(value)
        x = value * logistic
        wide = spread(steps, j, rows)[0]
        u = x * wide
        dy = dy_ref[:, at]
        skip = skip_ref[0:1, at]
        tail = jnp.exp(we_ref[0, :, at] - spread(cumulative, j, rows)[0])
        later = la_ref[0, :, at].astype(BF16)
        du = du_ref[:, at] + tail * dot(b_half, later)
        d_b = d_b + dot((u * tail).astype(BF16), later, NT)
        put_split(moves, at, dy * (ssd_ref[:, at] - skip * x) - u * du)
        put_split(drives, at, x * du)
        dskip_ref[0:1, at] += jnp.sum(dy * x, axis=0, keepdims=True)
        d_inner = wide * du + skip * dy
        dcx_ref[:, at] = (d_inner * silu_slope(value, logistic)).astype(BF16)
    d_c = dbc_ref[:, LANES:]
    if split:
        turn = lambda a: pltpu.roll(a, P_SIZE, 1)
        near, far = jnp.where(at_ref[1] == 0, d_b, d_c), jnp.where(at_ref[1] == 0, d_c, d_b)
        low, core = lane_is_low(rows), at_ref[0] == 0
        keep_ref[...] = jnp.where(
            core, jnp.where(low, near, turn(far)), jnp.where(low, turn(near), far)
        )
        send_ref[...] = jnp.where(
            core, jnp.where(low, turn(near), far), jnp.where(low, near, turn(far))
        )
    else:
        keep_ref[...] = d_b
        send_ref[...] = d_c
    moved = per_head(moves, picker, rows)
    driven = per_head(drives, picker, rows)
    upper = triangle(rows, lambda t, s: s >= t).astype(F32)
    d_rates = dot(upper, moved, NN, HIGHEST) + run[0:1]
    run[0:1] = d_rates[0:1]
    d_steps = driven - rate_ref[...] * d_rates
    d_raw = d_steps * jax.nn.sigmoid(dt_ref[...] + bias_ref[...])
    ddt_ref[...] = d_raw.astype(BF16)
    dhead_ref[0:1] += jnp.sum(d_raw, axis=0, keepdims=True)
    dhead_ref[1:2] -= jnp.sum(steps * d_rates, axis=0, keepdims=True)


def conv_back_kernel(d_ref, in_ref, halo_ref, cw_ref, dx_ref, gw_ref, xx_ref, hal):
    rows, width = d_ref.shape

    @pl.when((pl.program_id(0) == 0) & (pl.program_id(1) == 0))
    def _():
        gw_ref[...] = jnp.zeros_like(gw_ref)

    @pl.when(pl.program_id(1) == 0)
    def _():
        hal[...] = halo_ref[0]

    meet = jnp.zeros((rows, LANES), F32)
    for c in range(width // LANES):
        at = slice(c * LANES, (c + 1) * LANES)
        now = d_ref[:, at].astype(F32)
        chunk = jnp.concatenate([now, hal[:, at]], axis=0)
        hal[:, at] = now[:HALO]
        given = in_ref[:, at].astype(F32)
        total = jnp.zeros((rows, LANES), F32)
        for k in range(KERNEL):
            moved = chunk[KERNEL - 1 - k : KERNEL - 1 - k + rows]
            total = total + cw_ref[k : k + 1, at] * moved
            gw_ref[k : k + 1, at] += jnp.sum(given * moved, axis=0, keepdims=True)
        d_x = total.astype(BF16)
        dx_ref[:, at] = d_x
        meet = meet + d_x.astype(F32) * given
    xx_ref[0] = jnp.sum(meet.T, axis=0, keepdims=True)


def place_blocks(spot_ref, target, items, down, along=slice(None)):
    order = [0]
    for k in range(1, 4):
        order += [8 - k, k]

    rows = down.stop - down.start

    def put(k, shift, block):
        at = pl.multiple_of(spot_ref[k] * rows + shift, LANES)
        target[pl.ds(at, block.shape[0]), :] = block

    for k, item in zip(order, items):
        put(k, 0, item[down, along])
    return put


def in_project_kernel(spot_ref, *refs):
    acts, items, halves = refs[:4], refs[4:11], refs[11:13]
    x_ref, rest_ref, w_ref, r_ref = refs[13:]
    rows = items[0].shape[0]
    inner = x_ref.shape[1]

    @pl.when(pl.program_id(0) == 0)
    def _():
        for target, cut in ((w_ref, slice(0, inner)), (r_ref, slice(inner, None))):
            put = place_blocks(spot_ref, target, items, slice(0, rows), cut)
            put(4, 0, halves[0][:, cut])
            put(4, rows // 2, halves[1][:, cut])

    act = jnp.concatenate([a[...] for a in acts], axis=1)
    x_ref[...] = dot(act, w_ref[...]).astype(BF16)
    rest_ref[...] = dot(act, r_ref[...])


def gate_project_kernel(spot_ref, *refs):
    acts, cots, items = refs[:4], refs[4:8], refs[8:15]
    z_ref, dm_ref, wz_ref, wo_ref, na_ref, ca_ref = refs[15:]
    rows = items[0].shape[0] // 2
    last = spot_ref[4]

    @pl.when(pl.program_id(0) == 0)
    def _():
        for target, down in ((wz_ref, slice(0, rows)), (wo_ref, slice(rows, 2 * rows))):
            put = place_blocks(spot_ref, target, items, down)
            put(4, 0, jnp.zeros((rows, target.shape[1]), BF16))

    for i in range(8):

        @pl.when(last == i)
        def _():
            cut = slice((i % 2) * rows, (i % 2 + 1) * rows)
            na_ref[...] = acts[i // 2][:, cut]
            ca_ref[...] = cots[i // 2][:, cut]

    z_ref[...] = dot(jnp.concatenate([a[...] for a in acts], axis=1), wz_ref[...])
    dm_ref[...] = dot(jnp.concatenate([a[...] for a in cots], axis=1), wo_ref[...])


def with_spots(kernel, spots, acts, items, outs, shapes):
    total, width = acts[0].shape
    rows = min(256, total)
    fixed = lambda i, spot: (0, 0)
    return pl.pallas_call(
        kernel,
        grid_spec=pltpu.PrefetchScalarGridSpec(
            num_scalar_prefetch=1,
            grid=(total // rows,),
            in_specs=[pl.BlockSpec((rows, width), lambda i, spot: (i, 0)) for _ in acts]
            + [pl.BlockSpec(item.shape, fixed) for item in items],
            out_specs=[
                pl.BlockSpec((rows, shape.shape[1]), lambda i, spot: (i, 0)) if split
                else pl.BlockSpec(shape.shape, fixed)
                for shape, split in zip(shapes, outs)
            ],
        ),
        out_shape=shapes,
        compiler_params=pltpu.CompilerParams(vmem_limit_bytes=VMEM_LIMIT),
        cost_estimate=lasts(15.0),
    )(spots, *acts, *items)


def outer_kernel(pairs_of, far_ref, block_ref, *refs):
    out_ref = refs[-1]
    n = len(pairs_of)
    grads = refs[4 * n : -1]
    width = refs[0].shape[1]
    spot = far_ref[0] ^ (pl.program_id(0) + 1)
    for a in range(4):

        @pl.when(spot // 2 == a)
        def _():
            taken = 0
            for i, count in enumerate(pairs_of):
                start = 0
                for grad in grads[taken : taken + count]:
                    wide = grad.shape[1]
                    out_ref[i * width : (i + 1) * width, start : start + wide] = dot(
                        refs[4 * i + a][...], grad[...], TN
                    ).astype(BF16)
                    start += wide
                taken += count


def outer(far, blocks, *terms):
    total, own = terms[0][0][0].shape
    width = own // 2

    def pick(i, far, blocks, a):
        late = i + 1 > 2 * ((far[0] >> 1) ^ a)
        return 0, jnp.where(late, 1 - (far[0] & 1), far[0] & 1)

    specs, args = [], []
    for acts, _ in terms:
        for a, act in enumerate(acts):
            specs.append(pl.BlockSpec((total, width), functools.partial(pick, a=a)))
            args.append(act)
    for _, grads in terms:
        for grad in grads:
            specs.append(pl.BlockSpec(grad.shape, lambda i, far, blocks: (0, 0)))
            args.append(grad)
    columns = sum(g.shape[1] for g in terms[0][1])
    rows = width * len(terms)
    return pl.pallas_call(
        functools.partial(outer_kernel, [len(grads) for _, grads in terms]),
        grid_spec=pltpu.PrefetchScalarGridSpec(
            num_scalar_prefetch=2,
            grid=(7,),
            in_specs=specs,
            out_specs=pl.BlockSpec(
                (rows, columns), lambda i, far, blocks: (blocks[far[0] ^ (i + 1)], 0)
            ),
        ),
        out_shape=shaped(8 * rows, columns, dtype=BF16),
        compiler_params=pltpu.CompilerParams(vmem_limit_bytes=VMEM_LIMIT),
        cost_estimate=lasts(8.0 * rows * columns / 2**18),
    )(far, blocks, *args)


def outer_far(acts, grads):
    vmem = pl.BlockSpec(memory_space=pltpu.VMEM)
    columns = grads[0].shape[1] if len(acts) == 2 else sum(g.shape[1] for g in grads)
    width = acts[0].shape[1]

    def kernel(*refs):
        first, second = refs[-2:]
        given = refs[len(acts) : -2]
        if len(acts) == 2:
            first[...] = dot(refs[0][...], given[0][...], TN).astype(BF16)
            second[...] = dot(refs[1][...], given[1][...], TN).astype(BF16)
            return
        start = 0
        for grad in given:
            wide = grad.shape[1]
            both = dot(refs[0][...], grad[...], TN).astype(BF16)
            first[:, start : start + wide] = both[: width // 2]
            second[:, start : start + wide] = both[width // 2 :]
            start += wide

    half = shaped(width if len(acts) == 2 else width // 2, columns, dtype=BF16)
    return pl.pallas_call(
        kernel,
        in_specs=[vmem] * (len(acts) + len(grads)),
        out_specs=[vmem, vmem],
        out_shape=[half, half],
        compiler_params=pltpu.CompilerParams(vmem_limit_bytes=VMEM_LIMIT),
    )(*acts, *grads)


def project_kernel(terms, late, spot_ref, *refs):
    out_ref = refs[-1]
    total = None
    for k in range(terms):
        weight = refs[terms + k][...]
        if k < late:
            weight = jnp.where(pl.program_id(0) == spot_ref[4], refs[2 * terms + k][...], weight)
        term = dot(refs[k][...], weight, NT)
        total = term if total is None else total + term
    out_ref[...] = total.astype(out_ref.dtype)


def project(ring, spots, acts, weights, late=()):
    if not ring.on:
        return sum(dot(a, w, NT) for a, w in zip(acts, weights)).astype(BF16)
    rows, width = acts[0].shape[0], 256
    whole = lambda i, spot: (0, 0)
    return pl.pallas_call(
        functools.partial(project_kernel, len(acts), len(late)),
        grid_spec=pltpu.PrefetchScalarGridSpec(
            num_scalar_prefetch=1,
            grid=(weights[0].shape[0] // width,),
            in_specs=[pl.BlockSpec(a.shape, whole) for a in acts]
            + [pl.BlockSpec((width, w.shape[1]), lambda i, spot: (i, 0)) for w in weights]
            + [pl.BlockSpec(w.shape, whole) for w in late],
            out_specs=pl.BlockSpec((rows, width), lambda i, spot: (0, i)),
        ),
        out_shape=shaped(rows, weights[0].shape[0], dtype=BF16),
        compiler_params=pltpu.CompilerParams(vmem_limit_bytes=VMEM_LIMIT),
        cost_estimate=lasts(7.0 * sum(a.shape[1] for a in acts) / 1024),
    )(spots, *acts, *weights, *late)


def block_total(refs, cut):
    return sum(ref[cut].astype(F32) for ref in refs)


def total_zo_kernel(own_ref, right_ref, left_ref, w_ref, gz_ref, go_ref, met_ref):
    refs = own_ref, right_ref, left_ref
    rows = w_ref.shape[0]
    g_z = block_total(refs, slice(0, rows))
    gz_ref[...] = g_z
    go_ref[...] = block_total(refs, slice(rows, 2 * rows)).T
    met_ref[...] = jnp.sum(g_z * w_ref[...].astype(F32), axis=1, keepdims=True)


def total_in_kernel(own_ref, right_ref, left_ref, w_ref, met_in, gx_ref, gb_ref, gd_ref, met_ref):
    total = block_total((own_ref, right_ref, left_ref), slice(None))
    inner, heads = gx_ref.shape[1], gd_ref.shape[1]
    gx_ref[...] = total[:, :inner]
    gb_ref[...] = total[:, inner : inner + gb_ref.shape[1]]
    start = inner + gb_ref.shape[1]
    gd_ref[...] = total[:, start : start + heads]
    met = jnp.sum(total * w_ref[...].astype(F32), axis=1, keepdims=True)
    met_ref[...] = met_in[...] + met


def totals(kernel, whole, came, others, shapes):
    rows = came[0].shape[0]
    fixed = lambda i: (0, 0)
    arrays = [*came, *others]
    return pl.pallas_call(
        kernel,
        grid=(1,),
        in_specs=[pl.BlockSpec((rows, whole.shape[1]), fixed)]
        + [pl.BlockSpec(a.shape, fixed) for a in arrays],
        out_specs=[pl.BlockSpec(shape.shape, fixed) for shape in shapes],
        out_shape=shapes,
        compiler_params=pltpu.CompilerParams(vmem_limit_bytes=VMEM_LIMIT),
    )(whole, *arrays)


def shaped(*shape, dtype=F32):
    return jax.ShapeDtypeStruct(shape, dtype)


def call(kernel, grid, ins, outs, shapes, scratch=(), micros=5.0):
    return pl.pallas_call(
        kernel,
        grid=grid,
        in_specs=ins,
        out_specs=outs,
        out_shape=shapes,
        scratch_shapes=list(scratch),
        compiler_params=pltpu.CompilerParams(vmem_limit_bytes=VMEM_LIMIT),
        cost_estimate=lasts(micros),
    )


def conv_back(d_conv, given, after, taps, batch, length, rows):
    width = d_conv.shape[1]
    count = length // rows
    turn = lambda b, i: (b * count + count - 1 - i, 0)
    block = pl.BlockSpec((rows, width), turn)
    total = batch * length
    return call(
        conv_back_kernel,
        (batch, count),
        [
            block,
            block,
            pl.BlockSpec((1, HALO, width), lambda b, i: (b, 0, 0)),
            pl.BlockSpec((KERNEL, width), lambda b, i: (0, 0)),
        ],
        [
            block,
            pl.BlockSpec((KERNEL, width), lambda b, i: (0, 0)),
            pl.BlockSpec((1, 1, rows), lambda b, i: (b * count + count - 1 - i, 0, 0)),
        ],
        [
            shaped(total, width, dtype=BF16),
            shaped(KERNEL, width),
            shaped(batch * count, 1, rows),
        ],
        [pltpu.VMEM((HALO, width), F32)],
        micros=8.0 * total * width / 2**20,
    )(d_conv, given, after, taps)


def body(
    tokens, norm_gain, w_z, w_x, w_bc, w_dt, conv_x, conv_bc, dt_bias, decay_rate,
    skip_gain, gate_gain, w_out, grad_out,
):
    ring = Ring(lax.axis_size("seq"))
    batch, length, own_width = tokens.shape
    model = norm_gain.shape[0] * ring.size
    total = batch * length
    inner = w_z.shape[1]
    heads = dt_bias.shape[0]
    inner_all = inner * lax.axis_size("head")
    pairs = heads // 2
    rows = min(SPAN, length)
    count = length // rows
    blocks = batch * count
    margin = KERNEL - 1
    here = lax.axis_index("head")

    slab = tokens.reshape(total, own_width)
    cot_rows = grad_out.reshape(total, own_width)
    bias_row = dt_bias.reshape(1, heads)
    rate_row = decay_rate.reshape(1, heads)
    skip_lanes = jnp.repeat(skip_gain, P_SIZE).reshape(1, inner)
    gate_f = gate_gain.astype(F32).reshape(1, inner)
    conv_xf = conv_x.astype(F32)
    conv_bcf = conv_bc.astype(F32)
    conv_w = jnp.concatenate([conv_xf, conv_bcf], axis=1)

    def edge(arrays, last):
        cut = [array.reshape(batch, length, -1) for array in arrays]
        cut = [array[:, length - margin :] if last else array[:, :margin] for array in cut]
        cut = jnp.concatenate(cut, axis=2)
        moves = [(i, i + 1) for i in range(ring.size - 1)]
        if not last:
            moves = [(b, a) for a, b in moves]
        got = lax.ppermute(cut, "seq", moves).astype(F32)
        pad = ((0, 0), (HALO - margin, 0), (0, 0)) if last else ((0, 0), (0, HALO - margin), (0, 0))
        return jnp.pad(got, pad)

    at = lambda b, i: (b * count + i, 0)
    back = lambda b, i: (b * count + count - 1 - i, 0)
    at3 = lambda b, i: (b * count + i, 0, 0)
    back3 = lambda b, i: (b * count + count - 1 - i, 0, 0)
    seq3 = lambda b, i: (b, 0, 0)
    fixed = lambda b, i: (0, 0)
    row_heads = pl.BlockSpec((1, heads), fixed)
    row_inner = pl.BlockSpec((1, inner), fixed)
    state_spec = pl.BlockSpec((1, N, inner), seq3)
    pair_flops = total * rows * inner

    block_spec = pl.BlockSpec((rows, inner), at)
    row_out = pl.BlockSpec((1, 1, rows), at3)
    c_spec = pl.BlockSpec((rows, LANES), lambda b, i: (b * count + i, inner // LANES + 1))
    head_cols = pl.BlockSpec((rows, heads), at)
    v_back = pl.BlockSpec((rows, inner + 2 * N), back)
    block_back = pl.BlockSpec((rows, inner), back)
    heads_back = pl.BlockSpec((rows, heads), back)
    bc_back = pl.BlockSpec((rows, 2 * N), back)
    def scan(x_in, bc_in, halo, dt_raw):
        conv_out, y_local, steps, cumulative, begun, offsets, left, left_w = call(
            functools.partial(scan_kernel, pairs),
            (batch, count),
            [
                pl.BlockSpec((rows, inner), at),
                pl.BlockSpec((rows, 2 * N), at),
                pl.BlockSpec((1, HALO, inner + 2 * N), seq3),
                pl.BlockSpec((rows, heads), at),
                pl.BlockSpec((KERNEL, inner + 2 * N), fixed),
                row_heads,
                row_heads,
                row_inner,
            ],
            [
                pl.BlockSpec((rows, inner + 2 * N), at),
                pl.BlockSpec((rows, inner), at),
                pl.BlockSpec((rows, heads), at),
                pl.BlockSpec((rows, heads), at),
                pl.BlockSpec((1, N, inner), at3),
                pl.BlockSpec((1, 1, inner), at3),
                state_spec,
                pl.BlockSpec((1, 1, inner), seq3),
            ],
            [
                shaped(total, inner + 2 * N),
                shaped(total, inner),
                shaped(total, heads),
                shaped(total, heads),
                shaped(blocks, N, inner),
                shaped(blocks, 1, inner),
                shaped(batch, N, inner),
                shaped(batch, 1, inner),
            ],
            [
                pltpu.VMEM((HALO, inner + 2 * N), F32),
                pltpu.VMEM((N, inner), F32),
                pltpu.VMEM((8, heads), F32),
                pltpu.VMEM((8, inner), F32),
            ],
            micros=14.5,
        )(x_in, bc_in, halo, dt_raw, conv_w, bias_row, rate_row, skip_lanes)
        return conv_out, y_local, steps, cumulative, begun, offsets, left, left_w

    own_block = model // ring.size
    act_spec = pl.BlockSpec((rows, own_block), at)
    late_spec = pl.BlockSpec((own_block, inner), fixed)
    wide_scratch = [pltpu.VMEM((rows, inner), F32), pltpu.VMEM((rows, inner), F32)]

    def gate(y_local, conv_out, came, cumulative, z_part, dm_part, late):
        return call(
            functools.partial(gate_kernel, pairs),
            (batch, count),
            [
                block_spec, c_spec, state_spec, head_cols, block_spec, block_spec, row_inner,
                act_spec, act_spec, late_spec, late_spec,
            ],
            [block_spec, pl.BlockSpec((1, 2, rows), at3)],
            [shaped(total, inner), shaped(blocks, 2, rows)],
            wide_scratch,
            micros=7.0,
        )(y_local, conv_out, came, cumulative, z_part, dm_part, gate_f, *late)

    def gate_back(dm_part, ssd, z_part, gate_scale, product, cumulative, conv_out, late):
        return call(
            functools.partial(gate_back_kernel, pairs, inner_all),
            (batch, count),
            [
                block_spec, block_spec, block_spec, row_out, row_out, row_inner, head_cols, c_spec,
                act_spec, act_spec, late_spec, late_spec,
            ],
            [block_spec, block_spec, state_spec, row_out, row_inner, block_spec],
            [
                shaped(total, inner, dtype=BF16),
                shaped(total, inner),
                shaped(batch, N, inner),
                shaped(blocks, 1, rows),
                shaped(1, inner),
                shaped(total, inner, dtype=BF16),
            ],
            wide_scratch,
            micros=9.0,
        )(dm_part, ssd, z_part, gate_scale, product, gate_f, cumulative, conv_out, *late)

    def scan_back(conv_out, d_ssd, steps, begun, offsets, came):
        du_local, dbc_local = call(
            functools.partial(scan_back_kernel, pairs),
            (batch, count),
            [
                v_back, block_back, heads_back, row_heads,
                pl.BlockSpec((1, N, inner), back3),
                pl.BlockSpec((1, 1, inner), back3),
                state_spec,
            ],
            [block_back, bc_back],
            [shaped(total, inner), shaped(total, 2 * N)],
            [pltpu.VMEM((N, inner), F32)],
            micros=18.0,
        )(conv_out, d_ssd, steps, rate_row, begun, offsets, came)
        return du_local, dbc_local

    def finish(conv_out, d_ssd, du_local, ssd, steps, cumulative, left_w, later, came, left, dbc_local, dt_raw):
        lane_head = lax.broadcasted_iota(jnp.int32, (inner, heads), 0) // P_SIZE
        picker = (lane_head == lax.broadcasted_iota(jnp.int32, (inner, heads), 1)).astype(BF16)
        at_end = jnp.exp(left_w) * came + left
        d_conv_x, d_bc_keep, d_bc_send, d_dt, g_skip, g_heads = call(
            functools.partial(finish_kernel, pairs, ring.on),
            (batch, count),
            [
                v_back, block_back, block_back, block_back, heads_back, heads_back,
                pl.BlockSpec((1, 1, inner), seq3), state_spec, state_spec, bc_back, heads_back,
                row_heads, row_heads, row_inner,
                pl.BlockSpec((inner, heads), fixed), pl.BlockSpec(memory_space=pltpu.SMEM),
            ],
            [
                block_back, pl.BlockSpec((rows, LANES), back), pl.BlockSpec((rows, LANES), back),
                heads_back, row_inner,
                pl.BlockSpec((2, heads), fixed),
            ],
            [
                shaped(total, inner, dtype=BF16),
                shaped(total, LANES),
                shaped(total, LANES),
                shaped(total, heads, dtype=BF16),
                shaped(1, inner),
                shaped(2, heads),
            ],
            [
                pltpu.VMEM((8, heads), F32),
                pltpu.VMEM((2 * rows, inner), BF16),
                pltpu.VMEM((2 * rows, inner), BF16),
            ],
            micros=15.0,
        )(
            conv_out, d_ssd, du_local, ssd, steps, cumulative, left_w, later, at_end, dbc_local,
            dt_raw, bias_row, rate_row, skip_lanes, picker,
            jnp.stack([here & 1, here >> 1]).astype(jnp.int32),
        )
        return d_conv_x, d_bc_keep, d_bc_send, d_dt, g_skip, g_heads

    split_pass = ring.on and batch == 2
    forth, back_pass = Passing(ring, 1, inner), Passing(ring, -1, inner)
    slope = lambda v: silu_slope(v, jax.nn.sigmoid(v))

    group = 2 * N // 4 if ring.on else 2 * N
    edge_at = inner + group
    spare = -(group + heads) % LANES
    per = w_z.shape[0]
    own_columns = lambda a: lax.dynamic_slice_in_dim(a, here * group, group, 1) if ring.on else a
    all_in = jnp.concatenate(
        [w_x, own_columns(w_bc), w_dt, jnp.zeros((w_x.shape[0], spare), BF16)], axis=1
    )

    def by_group(pieces):
        own, near, far, both = pieces
        return [
            jnp.where(
                here == g, own, jnp.where(here == g ^ 1, near, jnp.where(here == g ^ 2, far, both))
            )
            for g in range(4)
        ]

    def gather_groups(own):
        far = swap(own, "head", 2)
        return by_group([own, swap(own, "head", 1), far, swap(far, "head", 1)])

    def fold(a):
        return jnp.concatenate([a[: total // 2], a[total // 2 :]], axis=1)

    def unfold(a):
        n = a.shape[1] // 2
        return jnp.concatenate([a[:, :n], a[:, n:]], axis=0)
    spots, order = (ring.spots(), ring.blocks()) if ring.on else (None, None)

    def work(all_in, slab):
        own_gain = own_features(ring, norm_gain.astype(F32), own_width)
        square = head_sum(jnp.sum(slab * slab, axis=1))
        scale = lax.rsqrt(square / model + EPS)
        own_normed = (slab * scale[:, None] * own_gain).astype(BF16)
        return ring.hop((all_in, all_in)), own_gain, scale, own_normed

    hop1, own_gain, scale, own_normed = ring.phase(work, all_in, slab)
    far = across(ring, own_normed)

    def work(hop1, own, w_z, w_out, cot_rows):
        zo_in = jnp.concatenate([w_z, w_out.T], axis=0)
        return ring.hop(hop1), beside(ring, own), zo_in, cot_rows.astype(BF16)

    hop2, near, zo_in, own_cot = ring.phase(work, hop1, own_normed, w_z, w_out, cot_rows)
    hop3 = ring.phase(ring.hop, hop2)
    hop4, both = ring.phase(
        lambda hop3, far: (ring.last_hop(hop3), corner(ring, own_normed, far)), hop3, far
    )
    normed = (both, near, far, own_normed) if ring.on else (both,)

    def project_in(normed, hop1, hop2, hop3, hop4):
        if ring.on:
            x_in, rest, x_w, rest_w = with_spots(
                in_project_kernel, spots, normed, [all_in, *hop1, *hop2, *hop3, *hop4],
                [True, True, False, False],
                [
                    shaped(total, inner, dtype=BF16), shaped(total, all_in.shape[1] - inner),
                    shaped(model, inner, dtype=BF16),
                    shaped(model, all_in.shape[1] - inner, dtype=BF16),
                ],
            )
            groups = gather_groups(fold(rest[:, :group]).astype(BF16))
            bc_in = jnp.concatenate([unfold(piece) for piece in groups], axis=1)
        else:
            x_w = lax.all_gather(w_x, "seq", axis=0, tiled=True)
            rest_w = lax.all_gather(all_in[:, inner:], "seq", axis=0, tiled=True)
            rest = dot(normed[0], rest_w)
            x_in, bc_in = dot(normed[0], x_w).astype(BF16), rest[:, :group].astype(BF16)
        bc_own = jnp.pad(rest[:, :group].astype(BF16), ((0, 0), (0, -group % LANES)))
        return x_in, bc_in, bc_own, rest[:, group : group + heads], x_w, rest_w

    def work(normed, hop1, hop2, hop3, hop4, zo_in):
        return ring.hop((zo_in, zo_in)), ring.phase(project_in, normed, hop1, hop2, hop3, hop4)

    hop1, (x_in, bc_in, bc_own, dt_raw, x_w, rest_w) = ring.phase(
        work, normed, hop1, hop2, hop3, hop4, zo_in
    )
    halo = ring.phase(lambda x_in, bc_in: edge([x_in, bc_in], True), x_in, bc_in)

    def work(hop1, x_in, bc_in, halo, dt_raw, own_cot):
        scanned = scan(x_in, bc_in, halo, dt_raw)
        held = forth.pair(forth.begin(scanned[6], scanned[7])) if split_pass else ()
        return ring.hop(hop1), scanned, held, beside(ring, own_cot), across(ring, own_cot)

    hop2, scanned, held, near, far = ring.phase(work, hop1, x_in, bc_in, halo, dt_raw, own_cot)
    conv_out, y_local, steps, cumulative, begun, offsets, left, left_w = scanned
    def work(hop2, held, far, conv_out):
        held = forth.next_line(held) if split_pass else ()
        value = conv_out[:, inner:]
        if ring.on:
            value = [value[:, g * group : (g + 1) * group] for g in range(4)]
            value = jnp.where(
                here < 2, jnp.where(here == 0, value[0], value[1]),
                jnp.where(here == 2, value[2], value[3]),
            )
        return ring.hop(hop2), held, corner(ring, own_cot, far), slope(value)

    hop3, held, both, own_slope = ring.phase(work, hop2, held, far, conv_out)
    cot = (both, near, far, own_cot) if ring.on else (both,)

    def work(hop1, hop2, hop3, held, normed, cot):
        held = forth.further_lines(held) if split_pass else ()
        if ring.on:
            wide, weight = shaped(total, inner), shaped(model, inner, dtype=BF16)
            act = shaped(total, own_block, dtype=BF16)
            given = with_spots(
                gate_project_kernel, spots, (*normed, *cot), [zo_in, *hop1, *hop2, *hop3],
                [True, True, False, False, True, True], [wide, wide, weight, weight, act, act],
            )
        else:
            z_w = lax.all_gather(w_z, "seq", axis=0, tiled=True)
            out_w = lax.all_gather(w_out.T, "seq", axis=0, tiled=True)
            none = jnp.zeros((total, own_block), BF16)
            given = dot(normed[0], z_w), dot(cot[0], out_w), z_w, out_w, none, none
        return ring.last_hop(hop3), held, given

    hop4, held, given = ring.phase(work, hop1, hop2, hop3, held, normed, cot)
    z_part, dm_part, z_w, out_w, normed_last, cot_last = given
    if not ring.on:
        hop4 = (jnp.zeros((own_block, inner), BF16),) * 2
    late = (normed_last, cot_last, *hop4)
    came = ring.phase(
        lambda held: forth.end(held) if split_pass else states_scan(left, left_w, 1), held
    )

    ssd, square_g = gate(y_local, conv_out, came, cumulative, z_part, dm_part, late)
    square_g = head_sum(square_g)
    gate_scale = lax.rsqrt(square_g[:, 0:1] / inner_all + EPS)
    product = square_g[:, 1:2]
    d_z, d_ssd, d_left, met_z, g_gate, mixed = gate_back(
        dm_part, ssd, z_part, gate_scale, product, cumulative, conv_out, late
    )

    far_spot = spots[4:5] if ring.on else None

    def work(d_left, left_w, normed, d_z, mixed, cot, normed_last, cot_last):
        held = back_pass.pair(back_pass.begin(d_left, left_w)) if split_pass else ()
        if ring.on:
            sums = ring.send(*outer_far([normed_last, cot_last], [d_z, mixed]))
            g_zo = outer(far_spot, order, (normed, [d_z]), (cot, [mixed]))
            return held, ring.add(g_zo, sums, 3), g_zo
        return held, (), (dot(normed[0], d_z, TN), dot(cot[0], mixed, TN))

    held, sums, g_zo = ring.phase(
        work, d_left, left_w, normed, d_z, mixed, cot, normed_last, cot_last
    )

    def work(held, sums, conv_out, d_ssd, steps, begun, offsets, came):
        sums = ring.hop(sums)
        held = back_pass.next_line(held) if split_pass else ()
        return held, sums, scan_back(conv_out, d_ssd, steps, begun, offsets, came)

    held, sums, (du_local, dbc_local) = ring.phase(
        work, held, sums, conv_out, d_ssd, steps, begun, offsets, came
    )

    def work(held, sums, g_zo, mixed, out_w, late_w):
        held = back_pass.further_lines(held) if split_pass else ()
        branch = project(ring, spots, [mixed], [out_w], [late_w])
        return held, ring.add(g_zo, sums, 2), branch

    held, sums, branch = ring.phase(work, held, sums, g_zo, mixed, out_w, hop4[1])

    def work(held, branch):
        later = back_pass.end(held) if split_pass else states_scan(d_left, left_w, -1)
        return later, scatter_near(ring, branch)

    later, (out_far, out_own) = ring.phase(work, held, branch)

    def work(later, sums, du_local, dbc_local):
        sums = ring.hop(sums)
        d_conv_x, mine, send, d_dt, g_skip, g_heads = finish(
            conv_out, d_ssd, du_local, ssd, steps, cumulative, left_w, later, came, left,
            dbc_local, dt_raw,
        )
        after_x = edge([d_conv_x], False)
        if ring.on:
            mine = mine + swap(send, "head", 1)
        else:
            mine = jnp.concatenate([mine, send], axis=1)
        return sums, d_conv_x, after_x, mine, d_dt, g_skip, g_heads

    sums, d_conv_x, after_x, mine, d_dt, g_skip, g_heads = ring.phase(
        work, later, sums, du_local, dbc_local
    )

    share = 1.0 if ring.on else jnp.where(here == 0, 1.0, 0.0)

    def work(mine, sums, g_zo, own_slope):
        if ring.on:
            mine = mine[:, :group] + unfold(swap(fold(mine[:, group:]), "head", 2))
        else:
            mine = head_sum(mine)
        d_conv_bc = jnp.pad((mine * own_slope).astype(BF16), ((0, 0), (0, -group % LANES)))
        return d_conv_bc, edge([d_conv_bc], False), ring.add(g_zo, sums, 1)

    d_conv_bc, after_bc, sums = ring.phase(work, mine, sums, g_zo, own_slope)
    own_taps = jnp.pad(own_columns(conv_bcf), ((0, 0), (0, -group % LANES)))

    def work(
        sums, g_zo, d_conv_bc, after_bc, d_conv_x, after_x, d_dt, normed, normed_last, out_far
    ):
        d_x, g_conv_x, met_x = conv_back(d_conv_x, x_in, after_x, conv_xf, batch, length, rows)
        d_bc, g_conv_bc, met_bc = conv_back(
            d_conv_bc, bc_own, after_bc, own_taps, batch, length, rows
        )
        fill = jnp.zeros((total, spare), BF16)
        d_rest = jnp.concatenate([d_bc[:, :group], d_dt, fill], axis=1)
        last = ring.hop(sums)
        if ring.on:
            sums = ring.send(*outer_far([normed_last], [d_x, d_rest]))
            g_all = outer(far_spot, order, (normed, [d_x, d_rest]))
            sums = ring.add(g_all, sums, 3)
        else:
            sums = ()
            g_all = jnp.concatenate([dot(normed[0], d, TN) for d in (d_x, d_rest)], axis=1)
        met_dt = jnp.sum(d_dt.astype(F32) * dt_raw, axis=1)
        met = (met_z + met_x + share * met_bc).reshape(total) + met_dt
        return (
            last, sums, d_x, d_rest, g_conv_x, g_conv_bc, met, g_all, across(ring, out_far),
        )

    last, sums, d_x, d_rest, g_conv_x, g_conv_bc, met, g_all, out_far = ring.phase(
        work, sums, g_zo, d_conv_bc, after_bc, d_conv_x, after_x, d_dt, normed, normed_last, out_far
    )
    g_conv_bc = g_conv_bc[:, :group]
    if ring.on:
        none = jnp.zeros((KERNEL, 2 * N), F32)
        g_conv_bc = lax.dynamic_update_slice(none, g_conv_bc, (0, here * group))
    small = jnp.concatenate(
        [
            g_conv_x.reshape(-1), g_conv_bc.reshape(-1), g_gate.reshape(-1),
            g_skip.reshape(-1), g_heads.reshape(-1),
        ]
    )

    def one_swap(array, bit):
        return array + swap(array, "seq", bit) if ring.on else array

    def work(sums, small, d_z, d_x, d_rest, z_w, x_w, rest_w, late_w, met):
        sums = ring.hop(sums)
        met = met + swap(met, "head", 1) if ring.on else head_sum(met)
        if not ring.on:
            columns = lax.broadcasted_iota(jnp.int32, (1, rest_w.shape[1]), 1)
            rest_w = jnp.where((columns < group) & (here > 0), 0.0, rest_w.astype(F32)).astype(BF16)
        back = project(ring, spots, [d_z, d_x, d_rest], [z_w, x_w, rest_w], [late_w])
        return sums, back, one_swap(small, 1), met

    sums, back_terms, small, met = ring.phase(
        work, sums, small, d_z, d_x, d_rest, z_w, x_w, rest_w, hop4[0], met
    )

    def work(sums, g_all, back_terms, met):
        far, d_normed = scatter_near(ring, back_terms)
        met = met + swap(met, "head", 2) if ring.on else met
        return ring.add(g_all, sums, 2), far, d_normed, met / scale

    sums, far, d_normed, dots = ring.phase(work, sums, g_all, back_terms, met)

    def work(sums, g_all, small, far, out_far, out_own, slab, g_zo, last):
        far = across(ring, far)
        mixed_out = slab + scatter_sum(ring, out_far, out_own)
        block, column = shaped(per, inner), shaped(per, 1)
        if ring.on:
            g_z, g_out, met_f = totals(
                total_zo_kernel, g_zo, last, [w_z], [block, shaped(inner, per), column]
            )
        else:
            g_z, g_out = (
                lax.psum_scatter(g.astype(BF16), "seq", scatter_dimension=0, tiled=True).astype(F32)
                for g in g_zo
            )
            g_out, met_f = g_out.T, jnp.sum(g_z * w_z.astype(F32), axis=1, keepdims=True)
        return (
            ring.add(g_all, ring.hop(sums), 1), far, one_swap(small, 2), mixed_out,
            g_z, g_out, met_f,
        )

    sums, far, small, mixed_out, g_z, g_out, met_f = ring.phase(
        work, sums, g_all, small, far, out_far, out_own, slab, g_zo, last
    )

    def work(sums, g_all, far, d_normed, slab, dots, met_f, small):
        last = ring.hop(sums)
        small = one_swap(small, 4)
        d_normed = scatter_sum(ring, far, d_normed)
        grad_tokens = (
            cot_rows
            + (scale[:, None] * own_gain) * d_normed
            - slab * (scale * scale * scale * dots / model)[:, None]
        )
        shapes = [shaped(per, inner), shaped(per, group), shaped(per, heads), shaped(per, 1)]
        if ring.on:
            g_x, g_bc, g_dt, met_f = totals(
                total_in_kernel, g_all, last, [all_in, met_f], shapes
            )
            g_bc = jnp.concatenate(gather_groups(g_bc), axis=1)
        else:
            g = lax.psum_scatter(g_all.astype(BF16), "seq", scatter_dimension=0, tiled=True)
            g = g.astype(F32)
            g_x, g_bc, g_dt = g[:, :inner], g[:, inner:edge_at], g[:, edge_at : edge_at + heads]
            columns = lax.broadcasted_iota(jnp.int32, (1, g.shape[1]), 1)
            once = jnp.where((columns >= inner) & (columns < edge_at), share, 1.0)
            met_f = met_f + jnp.sum(g * all_in.astype(F32) * once, axis=1, keepdims=True)
            small = lax.psum(small, "seq")
        maps = small[KERNEL * inner : KERNEL * (inner + 2 * N)]
        both = head_sum(jnp.concatenate([met_f[:, 0], maps if ring.on else maps * (1.0 / lax.axis_size("head"))]))
        g_gain = both[:per] / norm_gain.astype(F32)
        return g_x, g_bc, g_dt, grad_tokens, g_gain, small, both[per:]

    g_x, g_bc, g_dt, grad_tokens, g_gain, small, sum_bc = ring.phase(
        work, sums, g_all, far, d_normed, slab, dots, met_f, small
    )
    cuts = [KERNEL * inner, KERNEL * 2 * N, inner, inner, heads, heads]
    parts, start = [], 0
    for width in cuts:
        parts.append(small[start : start + width])
        start += width
    sum_x, _, sum_gate, sum_skip, sum_bias, sum_rate = parts

    return (
        mixed_out.reshape(batch, length, own_width),
        grad_tokens.reshape(batch, length, own_width),
        g_gain,
        g_z,
        g_x,
        g_bc,
        g_dt,
        sum_x.reshape(KERNEL, inner),
        sum_bc.reshape(KERNEL, 2 * N),
        sum_bias,
        sum_rate,
        jnp.sum(sum_skip.reshape(heads, P_SIZE), axis=1),
        sum_gate,
        g_out,
    )


def solution(mesh):
    in_specs = (
        P(None, "seq", "head"),
        P("seq"),
        P("seq", "head"),
        P("seq", "head"),
        P("seq", None),
        P("seq", "head"),
        P(None, "head"),
        P(),
        P("head"),
        P("head"),
        P("head"),
        P("head"),
        P("head", "seq"),
        P(None, "seq", "head"),
    )
    out_specs = (
        P(None, "seq", "head"),
        P(None, "seq", "head"),
        P("seq"),
        P("seq", "head"),
        P("seq", "head"),
        P("seq", None),
        P("seq", "head"),
        P(None, "head"),
        P(),
        P("head"),
        P("head"),
        P("head"),
        P("head"),
        P("head", "seq"),
    )
    return jax.shard_map(body, mesh=mesh, in_specs=in_specs, out_specs=out_specs, check_vma=False)
```

```python
import functools

import jax
import jax.numpy as jnp
from jax import lax
from jax.experimental import pallas as pl
from jax.experimental.pallas import tpu as pltpu
from jax.sharding import PartitionSpec as P

P_SIZE = 64
N = 128
KERNEL = 4
SPAN = 128
HALO = 8
ADD_STEPS = 2
LANES = 128
EPS = 1e-05
HIGHEST = lax.Precision.HIGHEST
F32 = jnp.float32
BF16 = jnp.bfloat16
VMEM_LIMIT = 50 * 1024 * 1024
NN = (((1,), (0,)), ((), ()))
NT = (((1,), (1,)), ((), ()))
TN = (((0,), (0,)), ((), ()))


def lasts(micros):
    return pl.CostEstimate(flops=0, bytes_accessed=int(micros * 3.3e6), transcendentals=0)


def dot(left, right, dims=NN, precision=None):
    return lax.dot_general(left, right, dims, precision=precision, preferred_element_type=F32)


def silu_slope(value, logistic):
    return logistic * (1.0 + value * (1.0 - logistic))


class Ring:
    def __init__(self, size):
        self.size = size
        self.on = size == 8 and lax.axis_size("head") == 4
        self.order = list(range(0, size, 2)) + list(range(size - 1, 0, -2))
        here = lax.axis_index("seq")
        self.line, self.side = here >> 1, here & 1
        self.place = jnp.where(self.side == 0, self.line, size - 1 - self.line)

    def spots(self):
        place = (self.place + jnp.arange(self.size, dtype=jnp.int32)) & (self.size - 1)
        side = place >> 2
        line = jnp.where(side == 1, self.size - 1 - place, place)
        bit = lax.axis_index("head") ^ line
        return 2 * jnp.where(bit == 3, 0, jnp.where(bit == 0, 3, bit)) + side

    def blocks(self):
        spot = jnp.arange(self.size, dtype=jnp.int32)
        side, bit = spot & 1, spot >> 1
        bit = jnp.where(bit == 0, 3, jnp.where(bit == 3, 0, bit))
        line = lax.axis_index("head") ^ bit
        place = jnp.where(side == 1, self.size - 1 - line, line)
        return (place - self.place) & (self.size - 1)

    def shift(self, array, by):
        order, size = self.order, self.size
        return lax.ppermute(array, "seq", [(order[i], order[(i + by) % size]) for i in range(size)])

    def hop(self, moving):
        if not self.on:
            return moving
        return self.shift(moving[0], 1), self.shift(moving[1], -1)

    def last_hop(self, moving):
        if not self.on:
            return moving
        cut = moving[0].shape[0] // 2
        return self.shift(moving[0][:cut], 1), self.shift(moving[1][cut:], -1)

    def part(self, whole, k):
        n = whole.shape[0] // self.size
        k = k % self.size
        return whole[k * n : (k + 1) * n]

    def send(self, first, second):
        return self.shift(first, 1), self.shift(second, -1)

    def add(self, whole, came, k):
        if not self.on:
            return ()
        rows, columns = 2 * came[0].shape[0] if k == 3 else came[0].shape[0], whole.shape[1]
        halves = k == self.size // 2 - 1
        steps = ADD_STEPS
        tile = rows // steps

        def kernel(a_ref, b_ref, right_ref, left_ref, out_a_ref, out_b_ref):
            right, left = right_ref[...].astype(F32), left_ref[...].astype(F32)
            if halves:
                upper = pl.program_id(0) < steps // 2
                right, left = jnp.where(upper, right, 0.0), jnp.where(upper, 0.0, left)
            out_a_ref[...] = (a_ref[...].astype(F32) + right).astype(BF16)
            out_b_ref[...] = (b_ref[...].astype(F32) + left).astype(BF16)

        block = lambda at: pl.BlockSpec((tile, columns), at)
        plain = lambda i: (i, 0)
        out = jax.ShapeDtypeStruct((rows, columns), BF16)
        return pl.pallas_call(
            kernel,
            grid=(steps,),
            in_specs=[
                block(lambda i: (steps * k + i, 0)),
                block(lambda i: (steps * (self.size - k) + i, 0)),
                block((lambda i: (jnp.minimum(i, steps // 2 - 1), 0)) if halves else plain),
                block((lambda i: (jnp.maximum(i - steps // 2, 0), 0)) if halves else plain),
            ],
            out_specs=[block(plain), block(plain)],
            out_shape=[out, out],
            compiler_params=pltpu.CompilerParams(vmem_limit_bytes=VMEM_LIMIT),
        )(whole, whole, *came)

    def phase(self, work, *args):
        if not self.on:
            return work(*args)
        shapes = jax.eval_shape(work, *args)

        def idle(*args):
            return jax.tree.map(lambda x: jnp.zeros(x.shape, x.dtype), shapes)

        return lax.cond(lax.axis_index("seq") < self.size, work, idle, *args)


def swap(array, axis, bit):
    size = lax.axis_size(axis)
    return lax.ppermute(array, axis, [(i, i ^ bit) for i in range(size)])


def head_sum(array):
    return lax.psum(array, "head")


def seq_sum(ring, array):
    if not ring.on:
        return lax.psum(array, "seq")
    bit = 1
    while bit < ring.size:
        array = array + swap(array, "seq", bit)
        bit *= 2
    return array


def own_features(ring, block, own_width):
    if not ring.on:
        whole = lax.all_gather(block, "seq", axis=0, tiled=True)
        return lax.dynamic_slice_in_dim(whole, lax.axis_index("head") * own_width, own_width)

    def fetch(flip):
        index = lambda line, side, head: (2 * line + side) * 4 + head
        return lax.ppermute(
            block,
            ("seq", "head"),
            [
                (index(head, side ^ flip, line), index(line, side, head))
                for line in range(4)
                for side in range(2)
                for head in range(4)
            ],
        )

    same, other = fetch(0), fetch(1)
    even = ring.side == 0
    return jnp.concatenate([jnp.where(even, same, other), jnp.where(even, other, same)])


def corner(ring, own, far):
    if not ring.on:
        return lax.all_gather(own, "head", axis=1, tiled=True)
    return swap(far, "head", 1)


def beside(ring, array):
    return swap(array, "head", 1) if ring.on else array


def across(ring, array):
    return swap(array, "head", 2) if ring.on else array


def scatter_near(ring, whole):
    if not ring.on:
        return whole, None
    width = whole.shape[1] // 4
    part = lambda k: whole[:, k * width : (k + 1) * width]
    far = swap(part(0), "head", 1)
    near = swap(part(1), "head", 1)
    far = (part(2).astype(F32) + far.astype(F32)).astype(BF16)
    return far, part(3).astype(F32) + near.astype(F32)


def scatter_sum(ring, far, mine):
    if not ring.on:
        return lax.psum_scatter(far, "head", scatter_dimension=1, tiled=True).astype(F32)
    return mine + far.astype(F32)


def shift_flat(array, by):
    size = lax.axis_size("seq")
    return lax.ppermute(array, "seq", [(i, i + by) for i in range(size) if 0 <= i + by < size])


def states_scan(state, log_decay, direction):
    incl_s, incl_w = state, log_decay
    excl_s, excl_w = jnp.zeros_like(state), jnp.zeros_like(log_decay)
    by = 1
    while by < lax.axis_size("seq"):
        got_s = shift_flat(incl_s.astype(BF16), by * direction).astype(F32)
        got_w = shift_flat(incl_w, by * direction)
        excl_s = jnp.exp(excl_w) * got_s + excl_s
        excl_w = excl_w + got_w
        incl_s = jnp.exp(incl_w) * got_s + incl_s
        incl_w = incl_w + got_w
        by *= 2
    return excl_s


def log_rows(log_decay):
    high = log_decay.astype(BF16).astype(F32)
    middle = (log_decay - high).astype(BF16).astype(F32)
    low = log_decay - high - middle
    row = lax.broadcasted_iota(jnp.int32, (16, log_decay.shape[1]), 0)
    parts = jnp.where(row == 0, high, jnp.where(row == 1, middle, low))
    return jnp.where(row < 3, parts, 0.0).astype(BF16)


def log_sum(rows):
    rows = rows.astype(F32)
    return rows[0:1] + rows[1:2] + rows[2:3]


def pass_begin_kernel(even_ref, lead_ref, state_ref, log_ref, keep_ref, kept_ref, send_ref):
    even = even_ref[0] == 1
    keep_ref[...] = jnp.where(even, state_ref[0], state_ref[1])
    kept_ref[...] = jnp.where(even, log_ref[0], log_ref[1])
    send_ref[:N] = jnp.where(even, state_ref[1], state_ref[0]).astype(BF16)
    send_ref[N:] = log_rows(jnp.where(even, log_ref[1], log_ref[0]))


def pass_pair_kernel(
    even_ref, lead_ref, keep_ref, kept_ref, got_ref, first_ref, d_first_ref, both_ref, pair_ref, send_ref
):
    leads = lead_ref[0] == 1
    keep, kept = keep_ref[...], kept_ref[...]
    got, gotten = got_ref[:N].astype(F32), log_sum(got_ref[N:])
    first = jnp.where(leads, keep, got)
    both = jnp.exp(jnp.where(leads, gotten, kept)) * first + jnp.where(leads, got, keep)
    first_ref[...] = first
    d_first_ref[...] = jnp.exp(jnp.where(leads, kept, gotten))
    both_ref[...] = both
    pair_ref[...] = jnp.exp(kept + gotten)
    send_ref[:N] = both.astype(BF16)
    send_ref[N:] = log_rows(kept + gotten)


def pass_line_kernel(even_ref, lead_ref, both_ref, pair_ref, got_ref, carry_ref, before_ref, send_ref):
    carry = got_ref[:N].astype(F32)
    carry_ref[...] = carry
    before_ref[...] = jnp.exp(log_sum(got_ref[N:]))
    send_ref[...] = (pair_ref[...] * carry + both_ref[...]).astype(BF16)


def pass_far_kernel(
    even_ref, lead_ref, first_ref, d_first_ref, carry_ref, before_ref, got_ref, mine_ref, send_ref
):
    leads = lead_ref[0] == 1
    carry = before_ref[...] * got_ref[...].astype(F32) + carry_ref[...]
    further = d_first_ref[...] * carry + first_ref[...]
    mine_ref[...] = jnp.where(leads, carry, further)
    send_ref[...] = jnp.where(leads, further, carry).astype(BF16)


def pass_end_kernel(even_ref, lead_ref, mine_ref, got_ref, out_ref):
    even = even_ref[0] == 1
    mine, got = mine_ref[...], got_ref[...].astype(F32)
    out_ref[0] = jnp.where(even, mine, got)
    out_ref[1] = jnp.where(even, got, mine)


class Passing:
    def __init__(self, ring, direction, inner):
        self.direction = direction
        leads = ring.side == 0 if direction > 0 else ring.side == 1
        self.flags = [jnp.where(f, 1, 0).astype(jnp.int32).reshape(1) for f in (ring.side == 0, leads)]
        row = shaped(1, inner)
        self.state, self.row = shaped(N, inner), row
        self.sent, self.sent_log = shaped(N, inner, dtype=BF16), shaped(N + 16, inner, dtype=BF16)

    def step(self, kernel, outs, *args):
        return pl.pallas_call(
            kernel,
            in_specs=[pl.BlockSpec(memory_space=pltpu.SMEM)] * 2
            + [pl.BlockSpec(memory_space=pltpu.VMEM)] * len(args),
            out_specs=jax.tree.map(lambda _: pl.BlockSpec(memory_space=pltpu.VMEM), outs),
            out_shape=outs,
            compiler_params=pltpu.CompilerParams(vmem_limit_bytes=VMEM_LIMIT),
        )(*self.flags, *args)

    def begin(self, state, log_decay):
        return self.step(pass_begin_kernel, [self.state, self.row, self.sent_log], state, log_decay)

    def pair(self, held):
        keep, kept, send = held
        got = swap(send, "seq", 1)
        outs = [self.state, self.row, self.state, self.row, self.sent_log]
        return self.step(pass_pair_kernel, outs, keep, kept, got)

    def next_line(self, held):
        first, d_first, both, pair, send = held
        got = shift_flat(send, 2 * self.direction)
        outs = [self.state, self.row, self.sent]
        return (first, d_first, *self.step(pass_line_kernel, outs, both, pair, got))

    def further_lines(self, held):
        first, d_first, carry, before, send = held
        got = shift_flat(send, 4 * self.direction)
        outs = [self.state, self.sent]
        return self.step(pass_far_kernel, outs, first, d_first, carry, before, got)

    def end(self, held):
        mine, send = held
        out = shaped(2, *self.state.shape)
        return self.step(pass_end_kernel, out, mine, swap(send, "seq", 1))


def lane_is_low(rows):
    return lax.broadcasted_iota(jnp.int32, (rows, LANES), 1) < P_SIZE


def spread(columns, j, rows):
    low = jnp.broadcast_to(columns[:, 2 * j : 2 * j + 1], (rows, LANES))
    high = jnp.broadcast_to(columns[:, 2 * j + 1 : 2 * j + 2], (rows, LANES))
    return jnp.where(lane_is_low(rows), low, high), low, high


def triangle(rows, keep):
    first = lax.broadcasted_iota(jnp.int32, (rows, rows), 0)
    second = lax.broadcasted_iota(jnp.int32, (rows, rows), 1)
    return keep(first, second)


def decays(rates, rows):
    lower = triangle(rows, lambda t, s: t >= s)
    within = dot(lower.astype(F32), rates, NN, HIGHEST)
    upper = triangle(rows, lambda s, t: s <= t).astype(F32)
    within_t = dot(rates, upper, TN, HIGHEST)
    return within, within_t, lower


def window(column, row, keep):
    rows = row.shape[1]
    return jnp.exp(jnp.where(keep, column[:, :rows] - row, -1e30))


def scan_kernel(
    pairs, x_ref, bc_ref, halo_ref, dt_ref, cw_ref, bias_ref, rate_ref, skip_ref,
    v_ref, y_ref, st_ref, wc_ref, sb_ref, wo_ref, sl_ref, we_ref,
    hal, state, off, off_l,
):
    rows = x_ref.shape[0]
    inner = pairs * LANES

    @pl.when(pl.program_id(1) == 0)
    def _():
        hal[...] = halo_ref[0]
        state[...] = jnp.zeros_like(state)
        off[...] = jnp.zeros_like(off)
        off_l[...] = jnp.zeros_like(off_l)

    def convolve(ref, at, start):
        now = ref[:, start : start + LANES].astype(F32)
        chunk = jnp.concatenate([hal[:, at : at + LANES], now], axis=0)
        hal[:, at : at + LANES] = now[rows - HALO :]
        shift = HALO - KERNEL + 1
        out = cw_ref[0:1, at : at + LANES] * chunk[shift : shift + rows]
        for k in range(1, KERNEL):
            out = out + cw_ref[k : k + 1, at : at + LANES] * chunk[shift + k : shift + k + rows]
        v_ref[:, at : at + LANES] = out
        return out * jax.nn.sigmoid(out)

    bmat = convolve(bc_ref, inner, 0)
    cmat = convolve(bc_ref, inner + LANES, LANES)
    b_half, c_half = bmat.astype(BF16), cmat.astype(BF16)
    scores = dot(cmat, bmat, NT, HIGHEST)
    steps = jax.nn.softplus(dt_ref[...] + bias_ref[...])
    rates = steps * -rate_ref[...]
    within, within_t, lower = decays(rates, rows)
    low_lanes = lane_is_low(rows)
    st_ref[...] = steps
    wc_ref[...] = off[0:1] + within
    off[0:1] = off[0:1] + within[rows - 1 : rows]
    wo_ref[0] = off_l[0:1]
    for j in range(pairs):
        at = slice(j * LANES, (j + 1) * LANES)
        x = convolve(x_ref, j * LANES, j * LANES)
        u = x * spread(steps, j, rows)[0]
        u_half = u.astype(BF16)
        grow, low, high = spread(within, j, rows)
        end = grow[rows - 1 : rows]
        a_low = (window(low, within_t[2 * j : 2 * j + 1], lower) * scores).astype(BF16)
        a_high = (window(high, within_t[2 * j + 1 : 2 * j + 2], lower) * scores).astype(BF16)
        inside = jnp.where(low_lanes, dot(a_low, u_half), dot(a_high, u_half))
        before = state[:, at]
        carried = jnp.exp(grow) * dot(c_half, before.astype(BF16))
        y_ref[:, at] = inside + carried + skip_ref[0:1, at] * x
        tail = (u * jnp.exp(end - grow)).astype(BF16)
        sb_ref[0, :, at] = before
        after = jnp.exp(end) * before + dot(b_half, tail, TN)
        state[:, at] = after
        sl_ref[0, :, at] = after
        ends = off_l[0:1, at] + end
        off_l[0:1, at] = ends
        we_ref[0, :, at] = ends


def gate_kernel(
    pairs, y_ref, vc_ref, s_ref, wc_ref, zp_ref, dmp_ref, gg_ref, na_ref, ca_ref, wz_ref, wo_ref,
    ssd_ref, sq_ref, z_ref, dm_ref
):
    rows = y_ref.shape[0]
    z_ref[...] = zp_ref[...] + dot(na_ref[...], wz_ref[...])
    dm_ref[...] = dmp_ref[...] + dot(ca_ref[...], wo_ref[...])
    vc = vc_ref[...]
    c_half = (vc * jax.nn.sigmoid(vc)).astype(BF16)
    cumulative = wc_ref[...]
    total = jnp.zeros((rows, LANES), F32)
    meet = jnp.zeros((rows, LANES), F32)
    for j in range(pairs):
        at = slice(j * LANES, (j + 1) * LANES)
        grow = jnp.exp(spread(cumulative, j, rows)[0])
        ssd = y_ref[:, at] + grow * dot(c_half, s_ref[0, :, at].astype(BF16))
        ssd_ref[:, at] = ssd
        z = z_ref[:, at]
        gated = ssd * (z * jax.nn.sigmoid(z))
        total = total + gated * gated
        meet = meet + dm_ref[:, at] * gg_ref[0:1, at] * gated
    sq_ref[0, 0:1] = jnp.sum(total.T, axis=0, keepdims=True)
    sq_ref[0, 1:2] = jnp.sum(meet.T, axis=0, keepdims=True)


def as_column(row):
    return jnp.broadcast_to(row, (LANES, row.shape[1])).T


def gate_back_kernel(
    pairs, width, dmp_ref, ssd_ref, zp_ref, gs_ref, ip_ref, gg_ref, wc_ref, vc_ref,
    na_ref, ca_ref, wz_ref, wo_ref,
    dz_ref, dy_ref, ds_ref, zz_ref, gate_ref, mixed_ref, z_ref, dm_ref,
):
    rows = dmp_ref.shape[0]
    z_ref[...] = zp_ref[...] + dot(na_ref[...], wz_ref[...])
    dm_ref[...] = dmp_ref[...] + dot(ca_ref[...], wo_ref[...])

    @pl.when(pl.program_id(1) == 0)
    def _():
        ds_ref[...] = jnp.zeros_like(ds_ref)

    @pl.when((pl.program_id(0) == 0) & (pl.program_id(1) == 0))
    def _():
        gate_ref[...] = jnp.zeros_like(gate_ref)

    scale = as_column(gs_ref[0])
    pull = as_column(gs_ref[0] * gs_ref[0] * gs_ref[0] * ip_ref[0] * (1.0 / width))
    vc = vc_ref[...]
    c_half = (vc * jax.nn.sigmoid(vc)).astype(BF16)
    cumulative = wc_ref[...]
    total = jnp.zeros((rows, LANES), F32)
    for j in range(pairs):
        at = slice(j * LANES, (j + 1) * LANES)
        z = z_ref[:, at]
        ssd = ssd_ref[:, at]
        logistic = jax.nn.sigmoid(z)
        opened = z * logistic
        gated = ssd * opened
        mixed_ref[:, at] = (gated * scale * gg_ref[0:1, at]).astype(BF16)
        scaled = scale * dm_ref[:, at]
        gate_ref[0:1, at] += jnp.sum(scaled * gated, axis=0, keepdims=True)
        d_gated = scaled * gg_ref[0:1, at] - gated * pull
        d_z = (d_gated * ssd * silu_slope(z, logistic)).astype(BF16)
        dz_ref[:, at] = d_z
        total = total + d_z.astype(F32) * z
        dy = d_gated * opened
        dy_ref[:, at] = dy
        grown = (jnp.exp(spread(cumulative, j, rows)[0]) * dy).astype(BF16)
        ds_ref[0, :, at] += dot(c_half, grown, TN)
    zz_ref[0] = jnp.sum(total.T, axis=0, keepdims=True)


def scan_back_kernel(
    pairs, v_ref, dy_ref, st_ref, rate_ref, sb_ref, wo_ref, s_ref,
    du_ref, dbc_ref, grad,
):
    rows = v_ref.shape[0]
    inner = pairs * LANES

    @pl.when(pl.program_id(1) == 0)
    def _():
        grad[...] = jnp.zeros_like(grad)

    def act(at):
        value = v_ref[:, at : at + LANES]
        return value * jax.nn.sigmoid(value)

    bmat, cmat = act(inner), act(inner + LANES)
    b_half, c_half = bmat.astype(BF16), cmat.astype(BF16)
    scores = dot(cmat, bmat, NT, HIGHEST)
    steps = st_ref[...]
    rates = steps * -rate_ref[...]
    within, within_t, lower = decays(rates, rows)
    low_lanes = lane_is_low(rows)
    d_c = jnp.zeros((rows, LANES), F32)
    d_b = jnp.zeros((rows, LANES), F32)
    d_scores = jnp.zeros((rows, rows), F32)
    none = jnp.zeros((rows, LANES), BF16)
    for j in range(pairs):
        at = slice(j * LANES, (j + 1) * LANES)
        x = act(j * LANES)
        u = x * spread(steps, j, rows)[0]
        u_half = u.astype(BF16)
        dy = dy_ref[:, at]
        dy_half = dy.astype(BF16)
        grow, low, high = spread(within, j, rows)
        end = grow[rows - 1 : rows]
        back = jnp.exp(end - grow)
        grown = (jnp.exp(grow) * dy).astype(BF16)
        begun = sb_ref[0, :, at] + jnp.exp(wo_ref[0, :, at]) * s_ref[0, :, at]
        d_c = d_c + dot(grown, begun.astype(BF16), NT)
        later = grad[:, at]
        later_half = later.astype(BF16)
        d_b = d_b + dot((u * back).astype(BF16), later_half, NT)
        w_low = window(low, within_t[2 * j : 2 * j + 1], lower)
        w_high = window(high, within_t[2 * j + 1 : 2 * j + 2], lower)
        d_scores = d_scores + w_low * dot(jnp.where(low_lanes, dy_half, none), u_half, NT)
        d_scores = d_scores + w_high * dot(jnp.where(low_lanes, none, dy_half), u_half, NT)
        a_low = (w_low * scores).astype(BF16)
        a_high = (w_high * scores).astype(BF16)
        inside = jnp.where(low_lanes, dot(a_low, dy_half, TN), dot(a_high, dy_half, TN))
        du_ref[:, at] = inside + back * dot(b_half, later_half)
        grad[:, at] = jnp.exp(end) * later + dot(c_half, grown, TN)
    d_half = d_scores.astype(BF16)
    dbc_ref[:, :LANES] = d_b + dot(d_half, c_half, TN)
    dbc_ref[:, LANES:] = d_c + dot(d_half, b_half)


def put_split(ref, at, value):
    rows = value.shape[0]
    high = value.astype(BF16)
    ref[:rows, at] = high
    ref[rows : 2 * rows, at] = (value - high.astype(F32)).astype(BF16)


def per_head(ref, picker, rows):
    both = dot(ref[: 2 * rows], picker)
    return both[:rows] + both[rows:]


def finish_kernel(
    pairs, split, v_ref, dy_ref, du_ref, ssd_ref, st_ref, wc_ref, we_ref, la_ref, se_ref, dbc_ref,
    dt_ref, bias_ref, rate_ref, skip_ref, pick_ref, at_ref,
    dcx_ref, keep_ref, send_ref, ddt_ref, dskip_ref, dhead_ref, run, moves, drives,
):
    rows = v_ref.shape[0]
    inner = pairs * LANES
    picker = pick_ref[...]

    @pl.when((pl.program_id(0) == 0) & (pl.program_id(1) == 0))
    def _():
        dskip_ref[...] = jnp.zeros_like(dskip_ref)
        dhead_ref[...] = jnp.zeros_like(dhead_ref)

    @pl.when(pl.program_id(1) == 0)
    def _():
        for j in range(pairs):
            at = slice(j * LANES, (j + 1) * LANES)
            both = jnp.sum(la_ref[0, :, at] * se_ref[0, :, at], axis=0, keepdims=True)
            put_split(moves, at, jnp.broadcast_to(both, (rows, LANES)))
        run[...] = per_head(moves, picker, rows)[0:8]

    value_b = v_ref[:, inner : inner + LANES]
    b_half = (value_b * jax.nn.sigmoid(value_b)).astype(BF16)
    steps = st_ref[...]
    cumulative = wc_ref[...]
    d_b = dbc_ref[:, :LANES]
    for j in range(pairs):
        at = slice(j * LANES, (j + 1) * LANES)
        value = v_ref[:, at]
        logistic = jax.nn.sigmoid(value)
        x = value * logistic
        wide = spread(steps, j, rows)[0]
        u = x * wide
        dy = dy_ref[:, at]
        skip = skip_ref[0:1, at]
        tail = jnp.exp(we_ref[0, :, at] - spread(cumulative, j, rows)[0])
        later = la_ref[0, :, at].astype(BF16)
        du = du_ref[:, at] + tail * dot(b_half, later)
        d_b = d_b + dot((u * tail).astype(BF16), later, NT)
        put_split(moves, at, dy * (ssd_ref[:, at] - skip * x) - u * du)
        put_split(drives, at, x * du)
        dskip_ref[0:1, at] += jnp.sum(dy * x, axis=0, keepdims=True)
        d_inner = wide * du + skip * dy
        dcx_ref[:, at] = (d_inner * silu_slope(value, logistic)).astype(BF16)
    d_c = dbc_ref[:, LANES:]
    if split:
        turn = lambda a: pltpu.roll(a, P_SIZE, 1)
        near, far = jnp.where(at_ref[1] == 0, d_b, d_c), jnp.where(at_ref[1] == 0, d_c, d_b)
        low, core = lane_is_low(rows), at_ref[0] == 0
        keep_ref[...] = jnp.where(
            core, jnp.where(low, near, turn(far)), jnp.where(low, turn(near), far)
        )
        send_ref[...] = jnp.where(
            core, jnp.where(low, turn(near), far), jnp.where(low, near, turn(far))
        )
    else:
        keep_ref[...] = d_b
        send_ref[...] = d_c
    moved = per_head(moves, picker, rows)
    driven = per_head(drives, picker, rows)
    upper = triangle(rows, lambda t, s: s >= t).astype(F32)
    d_rates = dot(upper, moved, NN, HIGHEST) + run[0:1]
    run[0:1] = d_rates[0:1]
    d_steps = driven - rate_ref[...] * d_rates
    d_raw = d_steps * jax.nn.sigmoid(dt_ref[...] + bias_ref[...])
    ddt_ref[...] = d_raw.astype(BF16)
    dhead_ref[0:1] += jnp.sum(d_raw, axis=0, keepdims=True)
    dhead_ref[1:2] -= jnp.sum(steps * d_rates, axis=0, keepdims=True)


def conv_back_kernel(d_ref, in_ref, halo_ref, cw_ref, dx_ref, gw_ref, xx_ref, hal):
    rows, width = d_ref.shape

    @pl.when((pl.program_id(0) == 0) & (pl.program_id(1) == 0))
    def _():
        gw_ref[...] = jnp.zeros_like(gw_ref)

    @pl.when(pl.program_id(1) == 0)
    def _():
        hal[...] = halo_ref[0]

    meet = jnp.zeros((rows, LANES), F32)
    for c in range(width // LANES):
        at = slice(c * LANES, (c + 1) * LANES)
        now = d_ref[:, at].astype(F32)
        chunk = jnp.concatenate([now, hal[:, at]], axis=0)
        hal[:, at] = now[:HALO]
        given = in_ref[:, at].astype(F32)
        total = jnp.zeros((rows, LANES), F32)
        for k in range(KERNEL):
            moved = chunk[KERNEL - 1 - k : KERNEL - 1 - k + rows]
            total = total + cw_ref[k : k + 1, at] * moved
            gw_ref[k : k + 1, at] += jnp.sum(given * moved, axis=0, keepdims=True)
        d_x = total.astype(BF16)
        dx_ref[:, at] = d_x
        meet = meet + d_x.astype(F32) * given
    xx_ref[0] = jnp.sum(meet.T, axis=0, keepdims=True)


def place_blocks(spot_ref, target, items, down, along=slice(None)):
    order = [0]
    for k in range(1, 4):
        order += [8 - k, k]

    rows = down.stop - down.start

    def put(k, shift, block):
        at = pl.multiple_of(spot_ref[k] * rows + shift, LANES)
        target[pl.ds(at, block.shape[0]), :] = block

    for k, item in zip(order, items):
        put(k, 0, item[down, along])
    return put


def in_project_kernel(spot_ref, *refs):
    acts, items, halves = refs[:4], refs[4:11], refs[11:13]
    x_ref, rest_ref, w_ref, r_ref = refs[13:]
    rows = items[0].shape[0]
    inner = x_ref.shape[1]

    @pl.when(pl.program_id(0) == 0)
    def _():
        for target, cut in ((w_ref, slice(0, inner)), (r_ref, slice(inner, None))):
            put = place_blocks(spot_ref, target, items, slice(0, rows), cut)
            put(4, 0, halves[0][:, cut])
            put(4, rows // 2, halves[1][:, cut])

    act = jnp.concatenate([a[...] for a in acts], axis=1)
    x_ref[...] = dot(act, w_ref[...]).astype(BF16)
    rest_ref[...] = dot(act, r_ref[...])


LATE = (4, 3, 5)


def gate_project_kernel(spot_ref, *refs):
    acts, cots, items = refs[:4], refs[4:8], refs[8:13]
    z_ref, dm_ref, wz_ref, wo_ref, na_ref, ca_ref = refs[13:]
    rows = items[0].shape[0] // 2

    @pl.when(pl.program_id(0) == 0)
    def _():
        for target, down in ((wz_ref, slice(0, rows)), (wo_ref, slice(rows, 2 * rows))):
            put = place_blocks(spot_ref, target, items, down)
            for k in LATE:
                put(k, 0, jnp.zeros((rows, target.shape[1]), BF16))

    for n, k in enumerate(LATE):
        to = slice(n * rows, (n + 1) * rows)
        for i in range(8):

            @pl.when(spot_ref[k] == i)
            def _():
                cut = slice((i % 2) * rows, (i % 2 + 1) * rows)
                na_ref[:, to] = acts[i // 2][:, cut]
                ca_ref[:, to] = cots[i // 2][:, cut]

    z_ref[...] = dot(jnp.concatenate([a[...] for a in acts], axis=1), wz_ref[...])
    dm_ref[...] = dot(jnp.concatenate([a[...] for a in cots], axis=1), wo_ref[...])


def gate_more_kernel(spot_ref, z_ref, dm_ref, na_ref, ca_ref, five_ref, three_ref, z_out, dm_out):
    rows = five_ref.shape[0] // 2
    one, two = slice(rows, 2 * rows), slice(2 * rows, 3 * rows)
    z_out[...] = z_ref[...] + (
        dot(na_ref[:, one], three_ref[:rows]) + dot(na_ref[:, two], five_ref[:rows])
    )
    dm_out[...] = dm_ref[...] + (
        dot(ca_ref[:, one], three_ref[rows:]) + dot(ca_ref[:, two], five_ref[rows:])
    )


def with_spots(kernel, spots, acts, items, outs, shapes):
    total = acts[0].shape[0]
    rows = min(256, total)
    fixed = lambda i, spot: (0, 0)
    return pl.pallas_call(
        kernel,
        grid_spec=pltpu.PrefetchScalarGridSpec(
            num_scalar_prefetch=1,
            grid=(total // rows,),
            in_specs=[pl.BlockSpec((rows, act.shape[1]), lambda i, spot: (i, 0)) for act in acts]
            + [pl.BlockSpec(item.shape, fixed) for item in items],
            out_specs=[
                pl.BlockSpec((rows, shape.shape[1]), lambda i, spot: (i, 0)) if split
                else pl.BlockSpec(shape.shape, fixed)
                for shape, split in zip(shapes, outs)
            ],
        ),
        out_shape=shapes,
        compiler_params=pltpu.CompilerParams(vmem_limit_bytes=VMEM_LIMIT),
        cost_estimate=lasts(15.0),
    )(spots, *acts, *items)


def outer_kernel(pairs_of, far_ref, block_ref, *refs):
    out_ref = refs[-1]
    n = len(pairs_of)
    grads = refs[4 * n : -1]
    width = refs[0].shape[1]
    spot = far_ref[0] ^ (pl.program_id(0) + 1)
    for a in range(4):

        @pl.when(spot // 2 == a)
        def _():
            taken = 0
            for i, count in enumerate(pairs_of):
                start = 0
                for grad in grads[taken : taken + count]:
                    wide = grad.shape[1]
                    out_ref[i * width : (i + 1) * width, start : start + wide] = dot(
                        refs[4 * i + a][...], grad[...], TN
                    ).astype(BF16)
                    start += wide
                taken += count


def outer(far, blocks, *terms):
    total, own = terms[0][0][0].shape
    width = own // 2

    def pick(i, far, blocks, a):
        late = i + 1 > 2 * ((far[0] >> 1) ^ a)
        return 0, jnp.where(late, 1 - (far[0] & 1), far[0] & 1)

    specs, args = [], []
    for acts, _ in terms:
        for a, act in enumerate(acts):
            specs.append(pl.BlockSpec((total, width), functools.partial(pick, a=a)))
            args.append(act)
    for _, grads in terms:
        for grad in grads:
            specs.append(pl.BlockSpec(grad.shape, lambda i, far, blocks: (0, 0)))
            args.append(grad)
    columns = sum(g.shape[1] for g in terms[0][1])
    rows = width * len(terms)
    return pl.pallas_call(
        functools.partial(outer_kernel, [len(grads) for _, grads in terms]),
        grid_spec=pltpu.PrefetchScalarGridSpec(
            num_scalar_prefetch=2,
            grid=(7,),
            in_specs=specs,
            out_specs=pl.BlockSpec(
                (rows, columns), lambda i, far, blocks: (blocks[far[0] ^ (i + 1)], 0)
            ),
        ),
        out_shape=shaped(8 * rows, columns, dtype=BF16),
        compiler_params=pltpu.CompilerParams(vmem_limit_bytes=VMEM_LIMIT),
        cost_estimate=lasts(8.0 * rows * columns / 2**18),
    )(far, blocks, *args)


def outer_far(acts, grads):
    columns = grads[0].shape[1] if len(acts) == 2 else sum(g.shape[1] for g in grads)
    total, width = acts[0].shape[0], acts[0].shape[1] // len(LATE)
    first_block = pl.BlockSpec((total, width), lambda i: (0, 0))
    whole = lambda a: pl.BlockSpec(a.shape, lambda i: (0, 0))

    def kernel(*refs):
        first, second = refs[-2:]
        given = refs[len(acts) : -2]
        if len(acts) == 2:
            first[...] = dot(refs[0][...], given[0][...], TN).astype(BF16)
            second[...] = dot(refs[1][...], given[1][...], TN).astype(BF16)
            return
        start = 0
        for grad in given:
            wide = grad.shape[1]
            both = dot(refs[0][...], grad[...], TN).astype(BF16)
            first[:, start : start + wide] = both[: width // 2]
            second[:, start : start + wide] = both[width // 2 :]
            start += wide

    half = shaped(width if len(acts) == 2 else width // 2, columns, dtype=BF16)
    return pl.pallas_call(
        kernel,
        grid=(1,),
        in_specs=[first_block] * len(acts) + [whole(grad) for grad in grads],
        out_specs=[whole(half), whole(half)],
        out_shape=[half, half],
        compiler_params=pltpu.CompilerParams(vmem_limit_bytes=VMEM_LIMIT),
    )(*acts, *grads)


def project_kernel(terms, late, spot_ref, *refs):
    out_ref = refs[-1]
    total = None
    for k in range(terms):
        weight = refs[terms + k][...]
        if k == 0:
            for n in range(late):
                here = pl.program_id(0) == spot_ref[LATE[n]]
                weight = jnp.where(here, refs[2 * terms + n][...], weight)
        term = dot(refs[k][...], weight, NT)
        total = term if total is None else total + term
    out_ref[...] = total.astype(out_ref.dtype)


def project(ring, spots, acts, weights, late, second):
    if not ring.on:
        return sum(dot(a, w, NT) for a, w in zip(acts, weights)).astype(BF16)
    rows, width = acts[0].shape[0], 256
    whole = lambda i, spot: (0, 0)
    half = lambda i, spot: (second, 0)
    return pl.pallas_call(
        functools.partial(project_kernel, len(acts), len(late)),
        grid_spec=pltpu.PrefetchScalarGridSpec(
            num_scalar_prefetch=1,
            grid=(weights[0].shape[0] // width,),
            in_specs=[pl.BlockSpec(a.shape, whole) for a in acts]
            + [pl.BlockSpec((width, w.shape[1]), lambda i, spot: (i, 0)) for w in weights]
            + [
                pl.BlockSpec((width, w.shape[1]), half if w.shape[0] > width else whole)
                for w in late
            ],
            out_specs=pl.BlockSpec((rows, width), lambda i, spot: (0, i)),
        ),
        out_shape=shaped(rows, weights[0].shape[0], dtype=BF16),
        compiler_params=pltpu.CompilerParams(vmem_limit_bytes=VMEM_LIMIT),
        cost_estimate=lasts(7.0 * sum(a.shape[1] for a in acts) / 1024),
    )(spots, *acts, *weights, *late)


def block_total(refs, cut):
    return sum(ref[cut].astype(F32) for ref in refs)


def total_zo_kernel(own_ref, right_ref, left_ref, w_ref, gz_ref, go_ref, met_ref):
    refs = own_ref, right_ref, left_ref
    rows = w_ref.shape[0]
    g_z = block_total(refs, slice(0, rows))
    gz_ref[...] = g_z
    go_ref[...] = block_total(refs, slice(rows, 2 * rows)).T
    met_ref[...] = jnp.sum(g_z * w_ref[...].astype(F32), axis=1, keepdims=True)


def total_in_kernel(own_ref, right_ref, left_ref, w_ref, met_in, gx_ref, gb_ref, gd_ref, met_ref):
    total = block_total((own_ref, right_ref, left_ref), slice(None))
    inner, heads = gx_ref.shape[1], gd_ref.shape[1]
    gx_ref[...] = total[:, :inner]
    gb_ref[...] = total[:, inner : inner + gb_ref.shape[1]]
    start = inner + gb_ref.shape[1]
    gd_ref[...] = total[:, start : start + heads]
    met = jnp.sum(total * w_ref[...].astype(F32), axis=1, keepdims=True)
    met_ref[...] = met_in[...] + met


def totals(kernel, whole, came, others, shapes):
    rows = came[0].shape[0]
    fixed = lambda i: (0, 0)
    arrays = [*came, *others]
    return pl.pallas_call(
        kernel,
        grid=(1,),
        in_specs=[pl.BlockSpec((rows, whole.shape[1]), fixed)]
        + [pl.BlockSpec(a.shape, fixed) for a in arrays],
        out_specs=[pl.BlockSpec(shape.shape, fixed) for shape in shapes],
        out_shape=shapes,
        compiler_params=pltpu.CompilerParams(vmem_limit_bytes=VMEM_LIMIT),
    )(whole, *arrays)


def shaped(*shape, dtype=F32):
    return jax.ShapeDtypeStruct(shape, dtype)


def call(kernel, grid, ins, outs, shapes, scratch=(), micros=5.0):
    return pl.pallas_call(
        kernel,
        grid=grid,
        in_specs=ins,
        out_specs=outs,
        out_shape=shapes,
        scratch_shapes=list(scratch),
        compiler_params=pltpu.CompilerParams(vmem_limit_bytes=VMEM_LIMIT),
        cost_estimate=lasts(micros),
    )


def conv_back(d_conv, given, after, taps, batch, length, rows):
    width = d_conv.shape[1]
    count = length // rows
    turn = lambda b, i: (b * count + count - 1 - i, 0)
    block = pl.BlockSpec((rows, width), turn)
    total = batch * length
    return call(
        conv_back_kernel,
        (batch, count),
        [
            block,
            block,
            pl.BlockSpec((1, HALO, width), lambda b, i: (b, 0, 0)),
            pl.BlockSpec((KERNEL, width), lambda b, i: (0, 0)),
        ],
        [
            block,
            pl.BlockSpec((KERNEL, width), lambda b, i: (0, 0)),
            pl.BlockSpec((1, 1, rows), lambda b, i: (b * count + count - 1 - i, 0, 0)),
        ],
        [
            shaped(total, width, dtype=BF16),
            shaped(KERNEL, width),
            shaped(batch * count, 1, rows),
        ],
        [pltpu.VMEM((HALO, width), F32)],
        micros=8.0 * total * width / 2**20,
    )(d_conv, given, after, taps)


def body(
    tokens, norm_gain, w_z, w_x, w_bc, w_dt, conv_x, conv_bc, dt_bias, decay_rate,
    skip_gain, gate_gain, w_out, grad_out,
):
    ring = Ring(lax.axis_size("seq"))
    batch, length, own_width = tokens.shape
    model = norm_gain.shape[0] * ring.size
    total = batch * length
    inner = w_z.shape[1]
    heads = dt_bias.shape[0]
    inner_all = inner * lax.axis_size("head")
    pairs = heads // 2
    rows = min(SPAN, length)
    count = length // rows
    blocks = batch * count
    margin = KERNEL - 1
    here = lax.axis_index("head")

    slab = tokens.reshape(total, own_width)
    cot_rows = grad_out.reshape(total, own_width)
    bias_row = dt_bias.reshape(1, heads)
    rate_row = decay_rate.reshape(1, heads)
    skip_lanes = jnp.repeat(skip_gain, P_SIZE).reshape(1, inner)
    gate_f = gate_gain.astype(F32).reshape(1, inner)
    conv_xf = conv_x.astype(F32)
    conv_bcf = conv_bc.astype(F32)
    conv_w = jnp.concatenate([conv_xf, conv_bcf], axis=1)

    def edge(arrays, last):
        cut = [array.reshape(batch, length, -1) for array in arrays]
        cut = [array[:, length - margin :] if last else array[:, :margin] for array in cut]
        cut = jnp.concatenate(cut, axis=2)
        moves = [(i, i + 1) for i in range(ring.size - 1)]
        if not last:
            moves = [(b, a) for a, b in moves]
        got = lax.ppermute(cut, "seq", moves).astype(F32)
        pad = ((0, 0), (HALO - margin, 0), (0, 0)) if last else ((0, 0), (0, HALO - margin), (0, 0))
        return jnp.pad(got, pad)

    at = lambda b, i: (b * count + i, 0)
    back = lambda b, i: (b * count + count - 1 - i, 0)
    at3 = lambda b, i: (b * count + i, 0, 0)
    back3 = lambda b, i: (b * count + count - 1 - i, 0, 0)
    seq3 = lambda b, i: (b, 0, 0)
    fixed = lambda b, i: (0, 0)
    row_heads = pl.BlockSpec((1, heads), fixed)
    row_inner = pl.BlockSpec((1, inner), fixed)
    state_spec = pl.BlockSpec((1, N, inner), seq3)
    pair_flops = total * rows * inner

    block_spec = pl.BlockSpec((rows, inner), at)
    row_out = pl.BlockSpec((1, 1, rows), at3)
    c_spec = pl.BlockSpec((rows, LANES), lambda b, i: (b * count + i, inner // LANES + 1))
    head_cols = pl.BlockSpec((rows, heads), at)
    v_back = pl.BlockSpec((rows, inner + 2 * N), back)
    block_back = pl.BlockSpec((rows, inner), back)
    heads_back = pl.BlockSpec((rows, heads), back)
    bc_back = pl.BlockSpec((rows, 2 * N), back)
    def scan(x_in, bc_in, halo, dt_raw):
        conv_out, y_local, steps, cumulative, begun, offsets, left, left_w = call(
            functools.partial(scan_kernel, pairs),
            (batch, count),
            [
                pl.BlockSpec((rows, inner), at),
                pl.BlockSpec((rows, 2 * N), at),
                pl.BlockSpec((1, HALO, inner + 2 * N), seq3),
                pl.BlockSpec((rows, heads), at),
                pl.BlockSpec((KERNEL, inner + 2 * N), fixed),
                row_heads,
                row_heads,
                row_inner,
            ],
            [
                pl.BlockSpec((rows, inner + 2 * N), at),
                pl.BlockSpec((rows, inner), at),
                pl.BlockSpec((rows, heads), at),
                pl.BlockSpec((rows, heads), at),
                pl.BlockSpec((1, N, inner), at3),
                pl.BlockSpec((1, 1, inner), at3),
                state_spec,
                pl.BlockSpec((1, 1, inner), seq3),
            ],
            [
                shaped(total, inner + 2 * N),
                shaped(total, inner),
                shaped(total, heads),
                shaped(total, heads),
                shaped(blocks, N, inner),
                shaped(blocks, 1, inner),
                shaped(batch, N, inner),
                shaped(batch, 1, inner),
            ],
            [
                pltpu.VMEM((HALO, inner + 2 * N), F32),
                pltpu.VMEM((N, inner), F32),
                pltpu.VMEM((8, heads), F32),
                pltpu.VMEM((8, inner), F32),
            ],
            micros=14.5,
        )(x_in, bc_in, halo, dt_raw, conv_w, bias_row, rate_row, skip_lanes)
        return conv_out, y_local, steps, cumulative, begun, offsets, left, left_w

    own_block = model // ring.size
    g_rows = min(256, length)
    g_count = length // g_rows
    g_at = lambda b, i: (b * g_count + i, 0)
    g_at3 = lambda b, i: (b * g_count + i, 0, 0)
    g_block, g_row = pl.BlockSpec((g_rows, inner), g_at), pl.BlockSpec((1, 1, g_rows), g_at3)
    g_c = pl.BlockSpec((g_rows, LANES), lambda b, i: (b * g_count + i, inner // LANES + 1))
    g_heads_spec = pl.BlockSpec((g_rows, heads), g_at)
    act_spec = pl.BlockSpec((g_rows, own_block), g_at)
    late_spec = pl.BlockSpec((own_block, inner), fixed)
    wide_scratch = [pltpu.VMEM((g_rows, inner), F32), pltpu.VMEM((g_rows, inner), F32)]

    def gate(y_local, conv_out, came, cumulative, z_part, dm_part, late):
        return call(
            functools.partial(gate_kernel, pairs),
            (batch, g_count),
            [
                g_block, g_c, state_spec, g_heads_spec, g_block, g_block, row_inner,
                act_spec, act_spec, late_spec, late_spec,
            ],
            [g_block, pl.BlockSpec((1, 2, g_rows), g_at3)],
            [shaped(total, inner), shaped(batch * g_count, 2, g_rows)],
            wide_scratch,
            micros=7.0,
        )(y_local, conv_out, came, cumulative, z_part, dm_part, gate_f, *late)

    def gate_back(dm_part, ssd, z_part, gate_scale, product, cumulative, conv_out, late):
        return call(
            functools.partial(gate_back_kernel, pairs, inner_all),
            (batch, g_count),
            [
                g_block, g_block, g_block, g_row, g_row, row_inner, g_heads_spec, g_c,
                act_spec, act_spec, late_spec, late_spec,
            ],
            [g_block, g_block, state_spec, g_row, row_inner, g_block],
            [
                shaped(total, inner, dtype=BF16),
                shaped(total, inner),
                shaped(batch, N, inner),
                shaped(batch * g_count, 1, g_rows),
                shaped(1, inner),
                shaped(total, inner, dtype=BF16),
            ],
            wide_scratch,
            micros=9.0,
        )(dm_part, ssd, z_part, gate_scale, product, gate_f, cumulative, conv_out, *late)

    def scan_back(conv_out, d_ssd, steps, begun, offsets, came):
        du_local, dbc_local = call(
            functools.partial(scan_back_kernel, pairs),
            (batch, count),
            [
                v_back, block_back, heads_back, row_heads,
                pl.BlockSpec((1, N, inner), back3),
                pl.BlockSpec((1, 1, inner), back3),
                state_spec,
            ],
            [block_back, bc_back],
            [shaped(total, inner), shaped(total, 2 * N)],
            [pltpu.VMEM((N, inner), F32)],
            micros=18.0,
        )(conv_out, d_ssd, steps, rate_row, begun, offsets, came)
        return du_local, dbc_local

    def finish(conv_out, d_ssd, du_local, ssd, steps, cumulative, left_w, later, at_end, dbc_local, dt_raw):
        f_back = lambda b, i: (b * g_count + g_count - 1 - i, 0)
        f_spec = lambda width: pl.BlockSpec((g_rows, width), f_back)
        f_v, f_block, f_heads = f_spec(inner + 2 * N), f_spec(inner), f_spec(heads)
        f_maps, f_lanes = f_spec(2 * N), f_spec(LANES)
        lane_head = lax.broadcasted_iota(jnp.int32, (inner, heads), 0) // P_SIZE
        picker = (lane_head == lax.broadcasted_iota(jnp.int32, (inner, heads), 1)).astype(BF16)
        d_conv_x, d_bc_keep, d_bc_send, d_dt, g_skip, g_heads = call(
            functools.partial(finish_kernel, pairs, ring.on),
            (batch, g_count),
            [
                f_v, f_block, f_block, f_block, f_heads, f_heads,
                pl.BlockSpec((1, 1, inner), seq3), state_spec, state_spec, f_maps, f_heads,
                row_heads, row_heads, row_inner,
                pl.BlockSpec((inner, heads), fixed), pl.BlockSpec(memory_space=pltpu.SMEM),
            ],
            [
                f_block, f_lanes, f_lanes, f_heads, row_inner,
                pl.BlockSpec((2, heads), fixed),
            ],
            [
                shaped(total, inner, dtype=BF16),
                shaped(total, LANES),
                shaped(total, LANES),
                shaped(total, heads, dtype=BF16),
                shaped(1, inner),
                shaped(2, heads),
            ],
            [
                pltpu.VMEM((8, heads), F32),
                pltpu.VMEM((2 * g_rows, inner), BF16),
                pltpu.VMEM((2 * g_rows, inner), BF16),
            ],
            micros=15.0,
        )(
            conv_out, d_ssd, du_local, ssd, steps, cumulative, left_w, later, at_end, dbc_local,
            dt_raw, bias_row, rate_row, skip_lanes, picker,
            jnp.stack([here & 1, here >> 1]).astype(jnp.int32),
        )
        return d_conv_x, d_bc_keep, d_bc_send, d_dt, g_skip, g_heads

    split_pass = ring.on and batch == 2
    forth, back_pass = Passing(ring, 1, inner), Passing(ring, -1, inner)
    slope = lambda v: silu_slope(v, jax.nn.sigmoid(v))

    group = 2 * N // 4 if ring.on else 2 * N
    edge_at = inner + group
    spare = -(group + heads) % LANES
    per = w_z.shape[0]
    own_columns = lambda a: lax.dynamic_slice_in_dim(a, here * group, group, 1) if ring.on else a
    all_in = jnp.concatenate(
        [w_x, own_columns(w_bc), w_dt, jnp.zeros((w_x.shape[0], spare), BF16)], axis=1
    )

    def by_group(pieces):
        own, near, far, both = pieces
        return [
            jnp.where(
                here == g, own, jnp.where(here == g ^ 1, near, jnp.where(here == g ^ 2, far, both))
            )
            for g in range(4)
        ]

    def gather_groups(own):
        far = swap(own, "head", 2)
        return by_group([own, swap(own, "head", 1), far, swap(far, "head", 1)])

    def fold(a):
        return jnp.concatenate([a[: total // 2], a[total // 2 :]], axis=1)

    def unfold(a):
        n = a.shape[1] // 2
        return jnp.concatenate([a[:, :n], a[:, n:]], axis=0)
    spots, order = (ring.spots(), ring.blocks()) if ring.on else (None, None)

    def work(all_in, slab):
        own_gain = own_features(ring, norm_gain.astype(F32), own_width)
        square = head_sum(jnp.sum(slab * slab, axis=1))
        scale = lax.rsqrt(square / model + EPS)
        own_normed = (slab * scale[:, None] * own_gain).astype(BF16)
        return ring.hop((all_in, all_in)), own_gain, scale, own_normed

    hop1, own_gain, scale, own_normed = ring.phase(work, all_in, slab)
    far = across(ring, own_normed)

    def work(hop1, own, w_z, w_out, cot_rows):
        zo_in = jnp.concatenate([w_z, w_out.T], axis=0)
        hop2 = ring.hop(hop1)
        return hop2, ring.hop(hop2), beside(ring, own), zo_in, cot_rows.astype(BF16)

    hop2, hop3, near, zo_in, own_cot = ring.phase(work, hop1, own_normed, w_z, w_out, cot_rows)
    hop4, both = ring.phase(
        lambda hop3, far: (ring.last_hop(hop3), corner(ring, own_normed, far)), hop3, far
    )
    normed = (both, near, far, own_normed) if ring.on else (both,)

    def project_in(normed, hop1, hop2, hop3, hop4):
        if ring.on:
            x_in, rest, x_w, rest_w = with_spots(
                in_project_kernel, spots, normed, [all_in, *hop1, *hop2, *hop3, *hop4],
                [True, True, False, False],
                [
                    shaped(total, inner, dtype=BF16), shaped(total, all_in.shape[1] - inner),
                    shaped(model, inner, dtype=BF16),
                    shaped(model, all_in.shape[1] - inner, dtype=BF16),
                ],
            )
            groups = gather_groups(fold(rest[:, :group]).astype(BF16))
            bc_in = jnp.concatenate([unfold(piece) for piece in groups], axis=1)
        else:
            x_w = lax.all_gather(w_x, "seq", axis=0, tiled=True)
            rest_w = lax.all_gather(all_in[:, inner:], "seq", axis=0, tiled=True)
            rest = dot(normed[0], rest_w)
            x_in, bc_in = dot(normed[0], x_w).astype(BF16), rest[:, :group].astype(BF16)
        bc_own = jnp.pad(rest[:, :group].astype(BF16), ((0, 0), (0, -group % LANES)))
        return x_in, bc_in, bc_own, rest[:, group : group + heads], x_w, rest_w

    def work(normed, hop1, hop2, hop3, hop4, zo_in):
        return ring.hop((zo_in, zo_in)), ring.phase(project_in, normed, hop1, hop2, hop3, hop4)

    hop1, (x_in, bc_in, bc_own, dt_raw, x_w, rest_w) = ring.phase(
        work, normed, hop1, hop2, hop3, hop4, zo_in
    )
    halo = ring.phase(lambda x_in, bc_in: edge([x_in, bc_in], True), x_in, bc_in)

    def work(hop1, x_in, bc_in, halo, dt_raw, own_cot):
        scanned = scan(x_in, bc_in, halo, dt_raw)
        held = forth.pair(forth.begin(scanned[6], scanned[7])) if split_pass else ()
        return ring.hop(hop1), scanned, held, beside(ring, own_cot), across(ring, own_cot)

    hop2, scanned, held, near, far = ring.phase(work, hop1, x_in, bc_in, halo, dt_raw, own_cot)
    conv_out, y_local, steps, cumulative, begun, offsets, left, left_w = scanned
    def work(hop1, hop2, held, far, conv_out, normed):
        moving = ring.hop(hop2)
        value = conv_out[:, inner:]
        if not ring.on:
            z_w = lax.all_gather(w_z, "seq", axis=0, tiled=True)
            out_w = lax.all_gather(w_out.T, "seq", axis=0, tiled=True)
            cot = (corner(ring, own_cot, far),)
            none = jnp.zeros((total, own_block), BF16)
            given = dot(normed[0], z_w), dot(cot[0], out_w), z_w, out_w, none, none
            return moving, held, cot, given, slope(value)
        value = [value[:, g * group : (g + 1) * group] for g in range(4)]
        value = jnp.where(
            here < 2, jnp.where(here == 0, value[0], value[1]),
            jnp.where(here == 2, value[2], value[3]),
        )
        both = ring.phase(lambda far: corner(ring, own_cot, far), far)
        wide, weight = shaped(total, inner), shaped(model, inner, dtype=BF16)
        act = shaped(total, len(LATE) * own_block, dtype=BF16)
        given = with_spots(
            gate_project_kernel, spots, (*normed, both, near, far, own_cot), [zo_in, *hop1, *hop2],
            [True, True, False, False, True, True], [wide, wide, weight, weight, act, act],
        )
        held = forth.next_line(held) if split_pass else ()
        return moving, held, both, given, slope(value)

    hop3, held, cot, given, own_slope = ring.phase(
        work, hop1, hop2, held, far, conv_out, normed
    )
    if ring.on:
        cot = (cot, near, far, own_cot)
    z_part, dm_part, z_w, out_w, normed_late, cot_late = given

    def work(hop3, held, z_part, dm_part, normed_late, cot_late):
        held = forth.further_lines(held) if split_pass else ()
        if ring.on:
            wide = shaped(total, inner)
            z_part, dm_part = with_spots(
                gate_more_kernel, spots, (z_part, dm_part, normed_late, cot_late), hop3,
                [True, True], [wide, wide],
            )
        came = forth.end(held) if split_pass else states_scan(left, left_w, 1)
        return ring.last_hop(hop3), came, z_part, dm_part

    hop4, came, z_part, dm_part = ring.phase(
        work, hop3, held, z_part, dm_part, normed_late, cot_late
    )
    if not ring.on:
        hop4 = (jnp.zeros((own_block, inner), BF16),) * 2
    late = (normed_late, cot_late, *hop4)
    late_z, late_out = ([half, hop3[1], hop3[0]] if ring.on else [] for half in hop4)

    ssd, square_g = gate(y_local, conv_out, came, cumulative, z_part, dm_part, late)
    square_g = head_sum(square_g)
    gate_scale = lax.rsqrt(square_g[:, 0:1] / inner_all + EPS)
    product = square_g[:, 1:2]
    d_z, d_ssd, d_left, met_z, g_gate, mixed = gate_back(
        dm_part, ssd, z_part, gate_scale, product, cumulative, conv_out, late
    )

    far_spot = spots[4:5] if ring.on else None

    def work(d_left, left_w, normed, d_z, mixed, cot, normed_late, cot_late):
        held = back_pass.pair(back_pass.begin(d_left, left_w)) if split_pass else ()
        if ring.on:
            sums = ring.send(*outer_far([normed_late, cot_late], [d_z, mixed]))
            g_zo = outer(far_spot, order, (normed, [d_z]), (cot, [mixed]))
            return held, ring.add(g_zo, sums, 3), g_zo
        return held, (), (dot(normed[0], d_z, TN), dot(cot[0], mixed, TN))

    held, sums, g_zo = ring.phase(
        work, d_left, left_w, normed, d_z, mixed, cot, normed_late, cot_late
    )

    def work(held, sums, conv_out, d_ssd, steps, begun, offsets, came):
        sums = ring.hop(sums)
        held = back_pass.next_line(held) if split_pass else ()
        at_end = jnp.exp(left_w) * came + left
        return held, sums, scan_back(conv_out, d_ssd, steps, begun, offsets, came), at_end

    held, sums, (du_local, dbc_local), at_end = ring.phase(
        work, held, sums, conv_out, d_ssd, steps, begun, offsets, came
    )

    def work(held, sums, g_zo, mixed, out_w, late_out):
        held = back_pass.further_lines(held) if split_pass else ()
        branch = project(ring, spots, [mixed], [out_w], late_out, 1)
        return held, ring.add(g_zo, sums, 2), branch

    held, sums, branch = ring.phase(work, held, sums, g_zo, mixed, out_w, late_out)

    def work(held, branch):
        later = back_pass.end(held) if split_pass else states_scan(d_left, left_w, -1)
        return later, scatter_near(ring, branch)

    later, (out_far, out_own) = ring.phase(work, held, branch)

    def work(later, sums, du_local, dbc_local):
        sums = ring.hop(sums)
        d_conv_x, mine, send, d_dt, g_skip, g_heads = finish(
            conv_out, d_ssd, du_local, ssd, steps, cumulative, left_w, later, at_end,
            dbc_local, dt_raw,
        )
        after_x = edge([d_conv_x], False)
        if ring.on:
            mine = mine + swap(send, "head", 1)
        else:
            mine = jnp.concatenate([mine, send], axis=1)
        return sums, d_conv_x, after_x, mine, d_dt, g_skip, g_heads

    sums, d_conv_x, after_x, mine, d_dt, g_skip, g_heads = ring.phase(
        work, later, sums, du_local, dbc_local
    )

    share = 1.0 if ring.on else jnp.where(here == 0, 1.0, 0.0)

    def work(mine, sums, g_zo, own_slope):
        if ring.on:
            mine = mine[:, :group] + unfold(swap(fold(mine[:, group:]), "head", 2))
        else:
            mine = head_sum(mine)
        d_conv_bc = jnp.pad((mine * own_slope).astype(BF16), ((0, 0), (0, -group % LANES)))
        return d_conv_bc, edge([d_conv_bc], False), ring.add(g_zo, sums, 1)

    d_conv_bc, after_bc, sums = ring.phase(work, mine, sums, g_zo, own_slope)
    own_taps = jnp.pad(own_columns(conv_bcf), ((0, 0), (0, -group % LANES)))

    def work(
        sums, g_zo, d_conv_bc, after_bc, d_conv_x, after_x, d_dt, normed, normed_late, out_far
    ):
        d_x, g_conv_x, met_x = conv_back(d_conv_x, x_in, after_x, conv_xf, batch, length, g_rows)
        d_bc, g_conv_bc, met_bc = conv_back(
            d_conv_bc, bc_own, after_bc, own_taps, batch, length, g_rows
        )
        fill = jnp.zeros((total, spare), BF16)
        d_rest = jnp.concatenate([d_bc[:, :group], d_dt, fill], axis=1)
        last = ring.hop(sums)
        if ring.on:
            sums = ring.send(*outer_far([normed_late], [d_x, d_rest]))
            g_all = outer(far_spot, order, (normed, [d_x, d_rest]))
            sums = ring.add(g_all, sums, 3)
        else:
            sums = ()
            g_all = jnp.concatenate([dot(normed[0], d, TN) for d in (d_x, d_rest)], axis=1)
        met_dt = jnp.sum(d_dt.astype(F32) * dt_raw, axis=1)
        met = met_z.reshape(total) + (met_x + share * met_bc).reshape(total) + met_dt
        return (
            last, sums, d_x, d_rest, g_conv_x, g_conv_bc, met, g_all, across(ring, out_far),
        )

    last, sums, d_x, d_rest, g_conv_x, g_conv_bc, met, g_all, out_far = ring.phase(
        work, sums, g_zo, d_conv_bc, after_bc, d_conv_x, after_x, d_dt, normed, normed_late, out_far
    )
    g_conv_bc = g_conv_bc[:, :group]
    if ring.on:
        none = jnp.zeros((KERNEL, 2 * N), F32)
        g_conv_bc = lax.dynamic_update_slice(none, g_conv_bc, (0, here * group))
    small = jnp.concatenate(
        [
            g_conv_x.reshape(-1), g_conv_bc.reshape(-1), g_gate.reshape(-1),
            g_skip.reshape(-1), g_heads.reshape(-1),
        ]
    )

    def one_swap(array, bit):
        return array + swap(array, "seq", bit) if ring.on else array

    def work(sums, small, d_z, d_x, d_rest, z_w, x_w, rest_w, late_z, met):
        sums = ring.hop(sums)
        met = met + swap(met, "head", 1) if ring.on else head_sum(met)
        if not ring.on:
            columns = lax.broadcasted_iota(jnp.int32, (1, rest_w.shape[1]), 1)
            rest_w = jnp.where((columns < group) & (here > 0), 0.0, rest_w.astype(F32)).astype(BF16)
        back = project(ring, spots, [d_z, d_x, d_rest], [z_w, x_w, rest_w], late_z, 0)
        return sums, back, one_swap(small, 1), met

    sums, back_terms, small, met = ring.phase(
        work, sums, small, d_z, d_x, d_rest, z_w, x_w, rest_w, late_z, met
    )

    def work(sums, g_all, back_terms, met):
        far, d_normed = scatter_near(ring, back_terms)
        met = met + swap(met, "head", 2) if ring.on else met
        return ring.add(g_all, sums, 2), far, d_normed, met / scale

    sums, far, d_normed, dots = ring.phase(work, sums, g_all, back_terms, met)

    def third(sums, g_all, small, out_far, out_own, g_zo, last):
        mixed_out = slab + scatter_sum(ring, out_far, out_own)
        block, column = shaped(per, inner), shaped(per, 1)
        if ring.on:
            g_z, g_out, met_f = totals(
                total_zo_kernel, g_zo, last, [w_z], [block, shaped(inner, per), column]
            )
        else:
            g_z, g_out = (
                lax.psum_scatter(g.astype(BF16), "seq", scatter_dimension=0, tiled=True).astype(F32)
                for g in g_zo
            )
            g_out, met_f = g_out.T, jnp.sum(g_z * w_z.astype(F32), axis=1, keepdims=True)
        sums = ring.add(g_all, ring.hop(sums), 1)
        small = one_swap(one_swap(small, 2), 4) if ring.on else lax.psum(small, "seq")
        parts, start = [], 0
        for width in [KERNEL * inner, KERNEL * 2 * N, inner, inner, heads, heads]:
            parts.append(small[start : start + width])
            start += width
        return sums, parts, mixed_out, g_z, g_out, met_f

    def fourth(sums, g_all, met_f, sum_bc):
        last = ring.hop(sums)
        shapes = [shaped(per, inner), shaped(per, group), shaped(per, heads), shaped(per, 1)]
        if ring.on:
            g_x, g_bc, g_dt, met_f = totals(
                total_in_kernel, g_all, last, [all_in, met_f], shapes
            )
            g_bc = jnp.concatenate(gather_groups(g_bc), axis=1)
        else:
            g = lax.psum_scatter(g_all.astype(BF16), "seq", scatter_dimension=0, tiled=True)
            g = g.astype(F32)
            g_x, g_bc, g_dt = g[:, :inner], g[:, inner:edge_at], g[:, edge_at : edge_at + heads]
            columns = lax.broadcasted_iota(jnp.int32, (1, g.shape[1]), 1)
            once = jnp.where((columns >= inner) & (columns < edge_at), share, 1.0)
            met_f = met_f + jnp.sum(g * all_in.astype(F32) * once, axis=1, keepdims=True)
            sum_bc = sum_bc * (1.0 / lax.axis_size("head"))
        both = head_sum(jnp.concatenate([met_f[:, 0], sum_bc]))
        g_gain = both[:per] / norm_gain.astype(F32)
        return g_x, g_bc, g_dt, g_gain, both[per:]

    def work(sums, g_all, small, far, d_normed, dots, out_far, out_own, g_zo, last):
        far = across(ring, far)
        sums, parts, *given = third(sums, g_all, small, out_far, out_own, g_zo, last)
        ends = fourth(sums, g_all, given[-1], parts[1])
        d_normed = scatter_sum(ring, far, d_normed)
        grad_tokens = (
            cot_rows
            + (scale[:, None] * own_gain) * d_normed
            - slab * (scale * scale * scale * dots / model)[:, None]
        )
        return parts, given, ends, grad_tokens

    parts, (mixed_out, g_z, g_out, _), ends, grad_tokens = ring.phase(
        work, sums, g_all, small, far, d_normed, dots, out_far, out_own, g_zo, last
    )
    sum_x, _, sum_gate, sum_skip, sum_bias, sum_rate = parts
    g_x, g_bc, g_dt, g_gain, sum_bc = ends

    return (
        mixed_out.reshape(batch, length, own_width),
        grad_tokens.reshape(batch, length, own_width),
        g_gain,
        g_z,
        g_x,
        g_bc,
        g_dt,
        sum_x.reshape(KERNEL, inner),
        sum_bc.reshape(KERNEL, 2 * N),
        sum_bias,
        sum_rate,
        jnp.sum(sum_skip.reshape(heads, P_SIZE), axis=1),
        sum_gate,
        g_out,
    )


def solution(mesh):
    in_specs = (
        P(None, "seq", "head"),
        P("seq"),
        P("seq", "head"),
        P("seq", "head"),
        P("seq", None),
        P("seq", "head"),
        P(None, "head"),
        P(),
        P("head"),
        P("head"),
        P("head"),
        P("head"),
        P("head", "seq"),
        P(None, "seq", "head"),
    )
    out_specs = (
        P(None, "seq", "head"),
        P(None, "seq", "head"),
        P("seq"),
        P("seq", "head"),
        P("seq", "head"),
        P("seq", None),
        P("seq", "head"),
        P(None, "head"),
        P(),
        P("head"),
        P("head"),
        P("head"),
        P("head"),
        P("head", "seq"),
    )
    return jax.shard_map(body, mesh=mesh, in_specs=in_specs, out_specs=out_specs, check_vma=False)
```

```python
import functools

import jax
import jax.numpy as jnp
from jax import lax
from jax.experimental import pallas as pl
from jax.experimental.pallas import tpu as pltpu
from jax.sharding import PartitionSpec as P

P_SIZE = 64
N = 128
KERNEL = 4
SPAN = 128
HALO = 8
ADD_STEPS = 2
LANES = 128
EPS = 1e-05
HIGHEST = lax.Precision.HIGHEST
F32 = jnp.float32
BF16 = jnp.bfloat16
VMEM_LIMIT = 50 * 1024 * 1024
NN = (((1,), (0,)), ((), ()))
NT = (((1,), (1,)), ((), ()))
TN = (((0,), (0,)), ((), ()))


def lasts(micros):
    return pl.CostEstimate(flops=0, bytes_accessed=int(micros * 3.3e6), transcendentals=0)


def dot(left, right, dims=NN, precision=None):
    return lax.dot_general(left, right, dims, precision=precision, preferred_element_type=F32)


def silu_slope(value, logistic):
    return logistic * (1.0 + value * (1.0 - logistic))


class Ring:
    def __init__(self, size):
        self.size = size
        self.on = size == 8 and lax.axis_size("head") == 4
        self.order = list(range(0, size, 2)) + list(range(size - 1, 0, -2))
        here = lax.axis_index("seq")
        self.line, self.side = here >> 1, here & 1
        self.place = jnp.where(self.side == 0, self.line, size - 1 - self.line)

    def spots(self):
        place = (self.place + jnp.arange(self.size, dtype=jnp.int32)) & (self.size - 1)
        side = place >> 2
        line = jnp.where(side == 1, self.size - 1 - place, place)
        bit = lax.axis_index("head") ^ line
        return 2 * jnp.where(bit == 3, 0, jnp.where(bit == 0, 3, bit)) + side

    def blocks(self):
        spot = jnp.arange(self.size, dtype=jnp.int32)
        side, bit = spot & 1, spot >> 1
        bit = jnp.where(bit == 0, 3, jnp.where(bit == 3, 0, bit))
        line = lax.axis_index("head") ^ bit
        place = jnp.where(side == 1, self.size - 1 - line, line)
        return (place - self.place) & (self.size - 1)

    def shift(self, array, by):
        order, size = self.order, self.size
        return lax.ppermute(array, "seq", [(order[i], order[(i + by) % size]) for i in range(size)])

    def hop(self, moving):
        if not self.on:
            return moving
        return self.shift(moving[0], 1), self.shift(moving[1], -1)

    def last_hop(self, moving):
        if not self.on:
            return moving
        cut = moving[0].shape[0] // 2
        return self.shift(moving[0][:cut], 1), self.shift(moving[1][cut:], -1)

    def part(self, whole, k):
        n = whole.shape[0] // self.size
        k = k % self.size
        return whole[k * n : (k + 1) * n]

    def send(self, first, second):
        return self.shift(first, 1), self.shift(second, -1)

    def add(self, whole, came, k):
        if not self.on:
            return ()
        rows, columns = 2 * came[0].shape[0] if k == 3 else came[0].shape[0], whole.shape[1]
        halves = k == self.size // 2 - 1
        steps = ADD_STEPS
        tile = rows // steps

        def kernel(a_ref, b_ref, right_ref, left_ref, out_a_ref, out_b_ref):
            right, left = right_ref[...].astype(F32), left_ref[...].astype(F32)
            if halves:
                upper = pl.program_id(0) < steps // 2
                right, left = jnp.where(upper, right, 0.0), jnp.where(upper, 0.0, left)
            out_a_ref[...] = (a_ref[...].astype(F32) + right).astype(BF16)
            out_b_ref[...] = (b_ref[...].astype(F32) + left).astype(BF16)

        block = lambda at: pl.BlockSpec((tile, columns), at)
        plain = lambda i: (i, 0)
        out = jax.ShapeDtypeStruct((rows, columns), BF16)
        return pl.pallas_call(
            kernel,
            grid=(steps,),
            in_specs=[
                block(lambda i: (steps * k + i, 0)),
                block(lambda i: (steps * (self.size - k) + i, 0)),
                block((lambda i: (jnp.minimum(i, steps // 2 - 1), 0)) if halves else plain),
                block((lambda i: (jnp.maximum(i - steps // 2, 0), 0)) if halves else plain),
            ],
            out_specs=[block(plain), block(plain)],
            out_shape=[out, out],
            compiler_params=pltpu.CompilerParams(vmem_limit_bytes=VMEM_LIMIT),
        )(whole, whole, *came)

    def phase(self, work, *args):
        if not self.on:
            return work(*args)
        shapes = jax.eval_shape(work, *args)

        def idle(*args):
            return jax.tree.map(lambda x: jnp.zeros(x.shape, x.dtype), shapes)

        return lax.cond(lax.axis_index("seq") < self.size, work, idle, *args)


def swap(array, axis, bit):
    size = lax.axis_size(axis)
    return lax.ppermute(array, axis, [(i, i ^ bit) for i in range(size)])


def head_sum(array):
    return lax.psum(array, "head")


def seq_sum(ring, array):
    if not ring.on:
        return lax.psum(array, "seq")
    bit = 1
    while bit < ring.size:
        array = array + swap(array, "seq", bit)
        bit *= 2
    return array


def own_features(ring, block, own_width):
    if not ring.on:
        whole = lax.all_gather(block, "seq", axis=0, tiled=True)
        return lax.dynamic_slice_in_dim(whole, lax.axis_index("head") * own_width, own_width)

    def fetch(flip):
        index = lambda line, side, head: (2 * line + side) * 4 + head
        return lax.ppermute(
            block,
            ("seq", "head"),
            [
                (index(head, side ^ flip, line), index(line, side, head))
                for line in range(4)
                for side in range(2)
                for head in range(4)
            ],
        )

    same, other = fetch(0), fetch(1)
    even = ring.side == 0
    return jnp.concatenate([jnp.where(even, same, other), jnp.where(even, other, same)])


def corner(ring, own, far):
    if not ring.on:
        return lax.all_gather(own, "head", axis=1, tiled=True)
    return swap(far, "head", 1)


def beside(ring, array):
    return swap(array, "head", 1) if ring.on else array


def across(ring, array):
    return swap(array, "head", 2) if ring.on else array


def scatter_near(ring, whole):
    if not ring.on:
        return whole, None
    width = whole.shape[1] // 4
    part = lambda k: whole[:, k * width : (k + 1) * width]
    far = swap(part(0), "head", 1)
    near = swap(part(1), "head", 1)
    far = (part(2).astype(F32) + far.astype(F32)).astype(BF16)
    return far, part(3).astype(F32) + near.astype(F32)


def scatter_sum(ring, far, mine):
    if not ring.on:
        return lax.psum_scatter(far, "head", scatter_dimension=1, tiled=True).astype(F32)
    return mine + far.astype(F32)


def shift_flat(array, by):
    size = lax.axis_size("seq")
    return lax.ppermute(array, "seq", [(i, i + by) for i in range(size) if 0 <= i + by < size])


def states_scan(state, log_decay, direction):
    incl_s, incl_w = state, log_decay
    excl_s, excl_w = jnp.zeros_like(state), jnp.zeros_like(log_decay)
    by = 1
    while by < lax.axis_size("seq"):
        got_s = shift_flat(incl_s.astype(BF16), by * direction).astype(F32)
        got_w = shift_flat(incl_w, by * direction)
        excl_s = jnp.exp(excl_w) * got_s + excl_s
        excl_w = excl_w + got_w
        incl_s = jnp.exp(incl_w) * got_s + incl_s
        incl_w = incl_w + got_w
        by *= 2
    return excl_s


def log_rows(log_decay):
    high = log_decay.astype(BF16).astype(F32)
    middle = (log_decay - high).astype(BF16).astype(F32)
    low = log_decay - high - middle
    row = lax.broadcasted_iota(jnp.int32, (16, log_decay.shape[1]), 0)
    parts = jnp.where(row == 0, high, jnp.where(row == 1, middle, low))
    return jnp.where(row < 3, parts, 0.0).astype(BF16)


def log_sum(rows):
    rows = rows.astype(F32)
    return rows[0:1] + rows[1:2] + rows[2:3]


def pass_begin_kernel(even_ref, lead_ref, state_ref, log_ref, keep_ref, kept_ref, send_ref):
    even = even_ref[0] == 1
    keep_ref[...] = jnp.where(even, state_ref[0], state_ref[1])
    kept_ref[...] = jnp.where(even, log_ref[0], log_ref[1])
    send_ref[:N] = jnp.where(even, state_ref[1], state_ref[0]).astype(BF16)
    send_ref[N:] = log_rows(jnp.where(even, log_ref[1], log_ref[0]))


def pass_pair_kernel(
    even_ref, lead_ref, keep_ref, kept_ref, got_ref, first_ref, d_first_ref, both_ref, pair_ref, send_ref
):
    leads = lead_ref[0] == 1
    keep, kept = keep_ref[...], kept_ref[...]
    got, gotten = got_ref[:N].astype(F32), log_sum(got_ref[N:])
    first = jnp.where(leads, keep, got)
    both = jnp.exp(jnp.where(leads, gotten, kept)) * first + jnp.where(leads, got, keep)
    first_ref[...] = first
    d_first_ref[...] = jnp.exp(jnp.where(leads, kept, gotten))
    both_ref[...] = both
    pair_ref[...] = jnp.exp(kept + gotten)
    send_ref[:N] = both.astype(BF16)
    send_ref[N:] = log_rows(kept + gotten)


def pass_line_kernel(even_ref, lead_ref, both_ref, pair_ref, got_ref, carry_ref, before_ref, send_ref):
    carry = got_ref[:N].astype(F32)
    carry_ref[...] = carry
    before_ref[...] = jnp.exp(log_sum(got_ref[N:]))
    send_ref[...] = (pair_ref[...] * carry + both_ref[...]).astype(BF16)


def pass_far_kernel(
    even_ref, lead_ref, first_ref, d_first_ref, carry_ref, before_ref, got_ref, mine_ref, send_ref
):
    leads = lead_ref[0] == 1
    carry = before_ref[...] * got_ref[...].astype(F32) + carry_ref[...]
    further = d_first_ref[...] * carry + first_ref[...]
    mine_ref[...] = jnp.where(leads, carry, further)
    send_ref[...] = jnp.where(leads, further, carry).astype(BF16)


def pass_end_kernel(even_ref, lead_ref, mine_ref, got_ref, out_ref):
    even = even_ref[0] == 1
    mine, got = mine_ref[...], got_ref[...].astype(F32)
    out_ref[0] = jnp.where(even, mine, got)
    out_ref[1] = jnp.where(even, got, mine)


class Passing:
    def __init__(self, ring, direction, inner):
        self.direction = direction
        leads = ring.side == 0 if direction > 0 else ring.side == 1
        self.flags = [jnp.where(f, 1, 0).astype(jnp.int32).reshape(1) for f in (ring.side == 0, leads)]
        row = shaped(1, inner)
        self.state, self.row = shaped(N, inner), row
        self.sent, self.sent_log = shaped(N, inner, dtype=BF16), shaped(N + 16, inner, dtype=BF16)

    def step(self, kernel, outs, *args):
        return pl.pallas_call(
            kernel,
            in_specs=[pl.BlockSpec(memory_space=pltpu.SMEM)] * 2
            + [pl.BlockSpec(memory_space=pltpu.VMEM)] * len(args),
            out_specs=jax.tree.map(lambda _: pl.BlockSpec(memory_space=pltpu.VMEM), outs),
            out_shape=outs,
            compiler_params=pltpu.CompilerParams(vmem_limit_bytes=VMEM_LIMIT),
        )(*self.flags, *args)

    def begin(self, state, log_decay):
        return self.step(pass_begin_kernel, [self.state, self.row, self.sent_log], state, log_decay)

    def pair(self, held):
        keep, kept, send = held
        got = swap(send, "seq", 1)
        outs = [self.state, self.row, self.state, self.row, self.sent_log]
        return self.step(pass_pair_kernel, outs, keep, kept, got)

    def next_line(self, held):
        first, d_first, both, pair, send = held
        got = shift_flat(send, 2 * self.direction)
        outs = [self.state, self.row, self.sent]
        return (first, d_first, *self.step(pass_line_kernel, outs, both, pair, got))

    def further_lines(self, held):
        first, d_first, carry, before, send = held
        got = shift_flat(send, 4 * self.direction)
        outs = [self.state, self.sent]
        return self.step(pass_far_kernel, outs, first, d_first, carry, before, got)

    def end(self, held):
        mine, send = held
        out = shaped(2, *self.state.shape)
        return self.step(pass_end_kernel, out, mine, swap(send, "seq", 1))


def lane_is_low(rows):
    return lax.broadcasted_iota(jnp.int32, (rows, LANES), 1) < P_SIZE


def spread(columns, j, rows):
    low = jnp.broadcast_to(columns[:, 2 * j : 2 * j + 1], (rows, LANES))
    high = jnp.broadcast_to(columns[:, 2 * j + 1 : 2 * j + 2], (rows, LANES))
    return jnp.where(lane_is_low(rows), low, high), low, high


def triangle(rows, keep):
    first = lax.broadcasted_iota(jnp.int32, (rows, rows), 0)
    second = lax.broadcasted_iota(jnp.int32, (rows, rows), 1)
    return keep(first, second)


def decays(rates, rows):
    lower = triangle(rows, lambda t, s: t >= s)
    within = dot(lower.astype(F32), rates, NN, HIGHEST)
    upper = triangle(rows, lambda s, t: s <= t).astype(F32)
    within_t = dot(rates, upper, TN, HIGHEST)
    return within, within_t, lower


def window(column, row, keep):
    rows = row.shape[1]
    return jnp.exp(jnp.where(keep, column[:, :rows] - row, -1e30))


def scan_kernel(
    pairs, x_ref, bc_ref, halo_ref, dt_ref, cw_ref, bias_ref, rate_ref, skip_ref,
    v_ref, y_ref, st_ref, wc_ref, sb_ref, wo_ref, sl_ref, we_ref,
    hal, state, off, off_l,
):
    rows = x_ref.shape[0]
    inner = pairs * LANES

    @pl.when(pl.program_id(1) == 0)
    def _():
        hal[...] = halo_ref[0]
        state[...] = jnp.zeros_like(state)
        off[...] = jnp.zeros_like(off)
        off_l[...] = jnp.zeros_like(off_l)

    def convolve(ref, at, start):
        now = ref[:, start : start + LANES].astype(F32)
        chunk = jnp.concatenate([hal[:, at : at + LANES], now], axis=0)
        hal[:, at : at + LANES] = now[rows - HALO :]
        shift = HALO - KERNEL + 1
        out = cw_ref[0:1, at : at + LANES] * chunk[shift : shift + rows]
        for k in range(1, KERNEL):
            out = out + cw_ref[k : k + 1, at : at + LANES] * chunk[shift + k : shift + k + rows]
        v_ref[:, at : at + LANES] = out
        return out * jax.nn.sigmoid(out)

    bmat = convolve(bc_ref, inner, 0)
    cmat = convolve(bc_ref, inner + LANES, LANES)
    b_half, c_half = bmat.astype(BF16), cmat.astype(BF16)
    scores = dot(cmat, bmat, NT, HIGHEST)
    steps = jax.nn.softplus(dt_ref[...] + bias_ref[...])
    rates = steps * -rate_ref[...]
    within, within_t, lower = decays(rates, rows)
    low_lanes = lane_is_low(rows)
    st_ref[...] = steps
    wc_ref[...] = off[0:1] + within
    off[0:1] = off[0:1] + within[rows - 1 : rows]
    wo_ref[0] = off_l[0:1]
    for j in range(pairs):
        at = slice(j * LANES, (j + 1) * LANES)
        x = convolve(x_ref, j * LANES, j * LANES)
        u = x * spread(steps, j, rows)[0]
        u_half = u.astype(BF16)
        grow, low, high = spread(within, j, rows)
        end = grow[rows - 1 : rows]
        a_low = (window(low, within_t[2 * j : 2 * j + 1], lower) * scores).astype(BF16)
        a_high = (window(high, within_t[2 * j + 1 : 2 * j + 2], lower) * scores).astype(BF16)
        inside = jnp.where(low_lanes, dot(a_low, u_half), dot(a_high, u_half))
        before = state[:, at]
        carried = jnp.exp(grow) * dot(c_half, before.astype(BF16))
        y_ref[:, at] = inside + carried + skip_ref[0:1, at] * x
        tail = (u * jnp.exp(end - grow)).astype(BF16)
        sb_ref[0, :, at] = before
        after = jnp.exp(end) * before + dot(b_half, tail, TN)
        state[:, at] = after
        sl_ref[0, :, at] = after
        ends = off_l[0:1, at] + end
        off_l[0:1, at] = ends
        we_ref[0, :, at] = ends


def gate_kernel(
    pairs, y_ref, vc_ref, s_ref, wc_ref, zp_ref, dmp_ref, gg_ref, na_ref, ca_ref, wz_ref, wo_ref,
    ssd_ref, sq_ref, z_ref, dm_ref
):
    rows = y_ref.shape[0]
    z_ref[...] = zp_ref[...] + dot(na_ref[...], wz_ref[...])
    dm_ref[...] = dmp_ref[...] + dot(ca_ref[...], wo_ref[...])
    vc = vc_ref[...]
    c_half = (vc * jax.nn.sigmoid(vc)).astype(BF16)
    cumulative = wc_ref[...]
    total = jnp.zeros((rows, LANES), F32)
    meet = jnp.zeros((rows, LANES), F32)
    for j in range(pairs):
        at = slice(j * LANES, (j + 1) * LANES)
        grow = jnp.exp(spread(cumulative, j, rows)[0])
        ssd = y_ref[:, at] + grow * dot(c_half, s_ref[0, :, at].astype(BF16))
        ssd_ref[:, at] = ssd
        z = z_ref[:, at]
        gated = ssd * (z * jax.nn.sigmoid(z))
        total = total + gated * gated
        meet = meet + dm_ref[:, at] * gg_ref[0:1, at] * gated
    sq_ref[0, 0:1] = jnp.sum(total.T, axis=0, keepdims=True)
    sq_ref[0, 1:2] = jnp.sum(meet.T, axis=0, keepdims=True)


def as_column(row):
    return jnp.broadcast_to(row, (LANES, row.shape[1])).T


def gate_back_kernel(
    pairs, width, dmp_ref, ssd_ref, zp_ref, gs_ref, ip_ref, gg_ref, wc_ref, vc_ref,
    na_ref, ca_ref, wz_ref, wo_ref,
    dz_ref, dy_ref, ds_ref, zz_ref, gate_ref, mixed_ref, z_ref, dm_ref,
):
    rows = dmp_ref.shape[0]
    z_ref[...] = zp_ref[...] + dot(na_ref[...], wz_ref[...])
    dm_ref[...] = dmp_ref[...] + dot(ca_ref[...], wo_ref[...])

    @pl.when(pl.program_id(1) == 0)
    def _():
        ds_ref[...] = jnp.zeros_like(ds_ref)

    @pl.when((pl.program_id(0) == 0) & (pl.program_id(1) == 0))
    def _():
        gate_ref[...] = jnp.zeros_like(gate_ref)

    scale = as_column(gs_ref[0])
    pull = as_column(gs_ref[0] * gs_ref[0] * gs_ref[0] * ip_ref[0] * (1.0 / width))
    vc = vc_ref[...]
    c_half = (vc * jax.nn.sigmoid(vc)).astype(BF16)
    cumulative = wc_ref[...]
    total = jnp.zeros((rows, LANES), F32)
    for j in range(pairs):
        at = slice(j * LANES, (j + 1) * LANES)
        z = z_ref[:, at]
        ssd = ssd_ref[:, at]
        logistic = jax.nn.sigmoid(z)
        opened = z * logistic
        gated = ssd * opened
        mixed_ref[:, at] = (gated * scale * gg_ref[0:1, at]).astype(BF16)
        scaled = scale * dm_ref[:, at]
        gate_ref[0:1, at] += jnp.sum(scaled * gated, axis=0, keepdims=True)
        d_gated = scaled * gg_ref[0:1, at] - gated * pull
        d_z = (d_gated * ssd * silu_slope(z, logistic)).astype(BF16)
        dz_ref[:, at] = d_z
        total = total + d_z.astype(F32) * z
        dy = d_gated * opened
        dy_ref[:, at] = dy
        grown = (jnp.exp(spread(cumulative, j, rows)[0]) * dy).astype(BF16)
        ds_ref[0, :, at] += dot(c_half, grown, TN)
    zz_ref[0] = jnp.sum(total.T, axis=0, keepdims=True)


def scan_back_kernel(
    pairs, v_ref, dy_ref, st_ref, rate_ref, sb_ref, wo_ref, s_ref,
    du_ref, dbc_ref, grad,
):
    rows = v_ref.shape[0]
    inner = pairs * LANES

    @pl.when(pl.program_id(1) == 0)
    def _():
        grad[...] = jnp.zeros_like(grad)

    def act(at):
        value = v_ref[:, at : at + LANES]
        return value * jax.nn.sigmoid(value)

    bmat, cmat = act(inner), act(inner + LANES)
    b_half, c_half = bmat.astype(BF16), cmat.astype(BF16)
    scores = dot(cmat, bmat, NT, HIGHEST)
    steps = st_ref[...]
    rates = steps * -rate_ref[...]
    within, within_t, lower = decays(rates, rows)
    low_lanes = lane_is_low(rows)
    d_c = jnp.zeros((rows, LANES), F32)
    d_b = jnp.zeros((rows, LANES), F32)
    d_scores = jnp.zeros((rows, rows), F32)
    none = jnp.zeros((rows, LANES), BF16)
    for j in range(pairs):
        at = slice(j * LANES, (j + 1) * LANES)
        x = act(j * LANES)
        u = x * spread(steps, j, rows)[0]
        u_half = u.astype(BF16)
        dy = dy_ref[:, at]
        dy_half = dy.astype(BF16)
        grow, low, high = spread(within, j, rows)
        end = grow[rows - 1 : rows]
        back = jnp.exp(end - grow)
        grown = (jnp.exp(grow) * dy).astype(BF16)
        begun = sb_ref[0, :, at] + jnp.exp(wo_ref[0, :, at]) * s_ref[0, :, at]
        d_c = d_c + dot(grown, begun.astype(BF16), NT)
        later = grad[:, at]
        later_half = later.astype(BF16)
        d_b = d_b + dot((u * back).astype(BF16), later_half, NT)
        w_low = window(low, within_t[2 * j : 2 * j + 1], lower)
        w_high = window(high, within_t[2 * j + 1 : 2 * j + 2], lower)
        d_scores = d_scores + w_low * dot(jnp.where(low_lanes, dy_half, none), u_half, NT)
        d_scores = d_scores + w_high * dot(jnp.where(low_lanes, none, dy_half), u_half, NT)
        a_low = (w_low * scores).astype(BF16)
        a_high = (w_high * scores).astype(BF16)
        inside = jnp.where(low_lanes, dot(a_low, dy_half, TN), dot(a_high, dy_half, TN))
        du_ref[:, at] = inside + back * dot(b_half, later_half)
        grad[:, at] = jnp.exp(end) * later + dot(c_half, grown, TN)
    d_half = d_scores.astype(BF16)
    dbc_ref[:, :LANES] = d_b + dot(d_half, c_half, TN)
    dbc_ref[:, LANES:] = d_c + dot(d_half, b_half)


def put_split(ref, at, value):
    rows = value.shape[0]
    high = value.astype(BF16)
    ref[:rows, at] = high
    ref[rows : 2 * rows, at] = (value - high.astype(F32)).astype(BF16)


def per_head(ref, picker, rows):
    both = dot(ref[: 2 * rows], picker)
    return both[:rows] + both[rows:]


def finish_kernel(
    pairs, split, v_ref, dy_ref, du_ref, ssd_ref, st_ref, wc_ref, we_ref, la_ref, se_ref, dbc_ref,
    dt_ref, bias_ref, rate_ref, skip_ref, pick_ref, at_ref,
    dcx_ref, keep_ref, send_ref, ddt_ref, dskip_ref, dhead_ref, run, moves, drives,
):
    rows = v_ref.shape[0]
    inner = pairs * LANES
    picker = pick_ref[...]

    @pl.when((pl.program_id(0) == 0) & (pl.program_id(1) == 0))
    def _():
        dskip_ref[...] = jnp.zeros_like(dskip_ref)
        dhead_ref[...] = jnp.zeros_like(dhead_ref)

    @pl.when(pl.program_id(1) == 0)
    def _():
        for j in range(pairs):
            at = slice(j * LANES, (j + 1) * LANES)
            both = jnp.sum(la_ref[0, :, at] * se_ref[0, :, at], axis=0, keepdims=True)
            put_split(moves, at, jnp.broadcast_to(both, (rows, LANES)))
        run[...] = per_head(moves, picker, rows)[0:8]

    value_b = v_ref[:, inner : inner + LANES]
    b_half = (value_b * jax.nn.sigmoid(value_b)).astype(BF16)
    steps = st_ref[...]
    cumulative = wc_ref[...]
    d_b = dbc_ref[:, :LANES]
    for j in range(pairs):
        at = slice(j * LANES, (j + 1) * LANES)
        value = v_ref[:, at]
        logistic = jax.nn.sigmoid(value)
        x = value * logistic
        wide = spread(steps, j, rows)[0]
        u = x * wide
        dy = dy_ref[:, at]
        skip = skip_ref[0:1, at]
        tail = jnp.exp(we_ref[0, :, at] - spread(cumulative, j, rows)[0])
        later = la_ref[0, :, at].astype(BF16)
        du = du_ref[:, at] + tail * dot(b_half, later)
        d_b = d_b + dot((u * tail).astype(BF16), later, NT)
        put_split(moves, at, dy * (ssd_ref[:, at] - skip * x) - u * du)
        put_split(drives, at, x * du)
        dskip_ref[0:1, at] += jnp.sum(dy * x, axis=0, keepdims=True)
        d_inner = wide * du + skip * dy
        dcx_ref[:, at] = (d_inner * silu_slope(value, logistic)).astype(BF16)
    d_c = dbc_ref[:, LANES:]
    if split:
        turn = lambda a: pltpu.roll(a, P_SIZE, 1)
        near, far = jnp.where(at_ref[1] == 0, d_b, d_c), jnp.where(at_ref[1] == 0, d_c, d_b)
        low, core = lane_is_low(rows), at_ref[0] == 0
        keep_ref[...] = jnp.where(
            core, jnp.where(low, near, turn(far)), jnp.where(low, turn(near), far)
        )
        send_ref[...] = jnp.where(
            core, jnp.where(low, turn(near), far), jnp.where(low, near, turn(far))
        )
    else:
        keep_ref[...] = d_b
        send_ref[...] = d_c
    moved = per_head(moves, picker, rows)
    driven = per_head(drives, picker, rows)
    upper = triangle(rows, lambda t, s: s >= t).astype(F32)
    d_rates = dot(upper, moved, NN, HIGHEST) + run[0:1]
    run[0:1] = d_rates[0:1]
    d_steps = driven - rate_ref[...] * d_rates
    d_raw = d_steps * jax.nn.sigmoid(dt_ref[...] + bias_ref[...])
    ddt_ref[...] = d_raw.astype(BF16)
    dhead_ref[0:1] += jnp.sum(d_raw, axis=0, keepdims=True)
    dhead_ref[1:2] -= jnp.sum(steps * d_rates, axis=0, keepdims=True)


def conv_back_kernel(d_ref, in_ref, halo_ref, cw_ref, dx_ref, gw_ref, xx_ref, hal):
    rows, width = d_ref.shape

    @pl.when((pl.program_id(0) == 0) & (pl.program_id(1) == 0))
    def _():
        gw_ref[...] = jnp.zeros_like(gw_ref)

    @pl.when(pl.program_id(1) == 0)
    def _():
        hal[...] = halo_ref[0]

    meet = jnp.zeros((rows, LANES), F32)
    for c in range(width // LANES):
        at = slice(c * LANES, (c + 1) * LANES)
        now = d_ref[:, at].astype(F32)
        chunk = jnp.concatenate([now, hal[:, at]], axis=0)
        hal[:, at] = now[:HALO]
        given = in_ref[:, at].astype(F32)
        total = jnp.zeros((rows, LANES), F32)
        for k in range(KERNEL):
            moved = chunk[KERNEL - 1 - k : KERNEL - 1 - k + rows]
            total = total + cw_ref[k : k + 1, at] * moved
            gw_ref[k : k + 1, at] += jnp.sum(given * moved, axis=0, keepdims=True)
        d_x = total.astype(BF16)
        dx_ref[:, at] = d_x
        meet = meet + d_x.astype(F32) * given
    xx_ref[0] = jnp.sum(meet.T, axis=0, keepdims=True)


def place_blocks(spot_ref, target, items, down, along=slice(None)):
    order = [0]
    for k in range(1, 4):
        order += [8 - k, k]

    rows = down.stop - down.start

    def put(k, shift, block):
        at = pl.multiple_of(spot_ref[k] * rows + shift, LANES)
        target[pl.ds(at, block.shape[0]), :] = block

    for k, item in zip(order, items):
        put(k, 0, item[down, along])
    return put


def in_project_kernel(spot_ref, *refs):
    acts, items, halves = refs[:4], refs[4:11], refs[11:13]
    x_ref, rest_ref, w_ref, r_ref = refs[13:]
    rows = items[0].shape[0]
    inner = x_ref.shape[1]

    @pl.when(pl.program_id(0) == 0)
    def _():
        for target, cut in ((w_ref, slice(0, inner)), (r_ref, slice(inner, None))):
            put = place_blocks(spot_ref, target, items, slice(0, rows), cut)
            put(4, 0, halves[0][:, cut])
            put(4, rows // 2, halves[1][:, cut])

    act = jnp.concatenate([a[...] for a in acts], axis=1)
    x_ref[...] = dot(act, w_ref[...]).astype(BF16)
    rest_ref[...] = dot(act, r_ref[...])


LATE = (4, 3, 5)


def gate_project_kernel(spot_ref, *refs):
    acts, cots, items = refs[:4], refs[4:8], refs[8:13]
    z_ref, dm_ref, wz_ref, wo_ref, na_ref, ca_ref = refs[13:]
    rows = items[0].shape[0] // 2

    @pl.when(pl.program_id(0) == 0)
    def _():
        for target, down in ((wz_ref, slice(0, rows)), (wo_ref, slice(rows, 2 * rows))):
            put = place_blocks(spot_ref, target, items, down)
            for k in LATE:
                put(k, 0, jnp.zeros((rows, target.shape[1]), BF16))

    for n, k in enumerate(LATE):
        to = slice(n * rows, (n + 1) * rows)
        for i in range(8):

            @pl.when(spot_ref[k] == i)
            def _():
                cut = slice((i % 2) * rows, (i % 2 + 1) * rows)
                na_ref[:, to] = acts[i // 2][:, cut]
                ca_ref[:, to] = cots[i // 2][:, cut]

    z_ref[...] = dot(jnp.concatenate([a[...] for a in acts], axis=1), wz_ref[...])
    dm_ref[...] = dot(jnp.concatenate([a[...] for a in cots], axis=1), wo_ref[...])


def gate_more_kernel(spot_ref, z_ref, dm_ref, na_ref, ca_ref, five_ref, three_ref, z_out, dm_out):
    rows = five_ref.shape[0] // 2
    one, two = slice(rows, 2 * rows), slice(2 * rows, 3 * rows)
    z_out[...] = z_ref[...] + (
        dot(na_ref[:, one], three_ref[:rows]) + dot(na_ref[:, two], five_ref[:rows])
    )
    dm_out[...] = dm_ref[...] + (
        dot(ca_ref[:, one], three_ref[rows:]) + dot(ca_ref[:, two], five_ref[rows:])
    )


def with_spots(kernel, spots, acts, items, outs, shapes):
    total = acts[0].shape[0]
    rows = min(256, total)
    fixed = lambda i, spot: (0, 0)
    return pl.pallas_call(
        kernel,
        grid_spec=pltpu.PrefetchScalarGridSpec(
            num_scalar_prefetch=1,
            grid=(total // rows,),
            in_specs=[pl.BlockSpec((rows, act.shape[1]), lambda i, spot: (i, 0)) for act in acts]
            + [pl.BlockSpec(item.shape, fixed) for item in items],
            out_specs=[
                pl.BlockSpec((rows, shape.shape[1]), lambda i, spot: (i, 0)) if split
                else pl.BlockSpec(shape.shape, fixed)
                for shape, split in zip(shapes, outs)
            ],
        ),
        out_shape=shapes,
        compiler_params=pltpu.CompilerParams(vmem_limit_bytes=VMEM_LIMIT),
        cost_estimate=lasts(15.0),
    )(spots, *acts, *items)


def outer_kernel(pairs_of, far_ref, block_ref, *refs):
    out_ref = refs[-1]
    n = len(pairs_of)
    grads = refs[4 * n : -1]
    width = refs[0].shape[1]
    spot = far_ref[0] ^ (pl.program_id(0) + 1)
    for a in range(4):

        @pl.when(spot // 2 == a)
        def _():
            taken = 0
            for i, count in enumerate(pairs_of):
                start = 0
                for grad in grads[taken : taken + count]:
                    wide = grad.shape[1]
                    out_ref[i * width : (i + 1) * width, start : start + wide] = dot(
                        refs[4 * i + a][...], grad[...], TN
                    ).astype(BF16)
                    start += wide
                taken += count


def outer(far, blocks, *terms):
    total, own = terms[0][0][0].shape
    width = own // 2

    def pick(i, far, blocks, a):
        late = i + 1 > 2 * ((far[0] >> 1) ^ a)
        return 0, jnp.where(late, 1 - (far[0] & 1), far[0] & 1)

    specs, args = [], []
    for acts, _ in terms:
        for a, act in enumerate(acts):
            specs.append(pl.BlockSpec((total, width), functools.partial(pick, a=a)))
            args.append(act)
    for _, grads in terms:
        for grad in grads:
            specs.append(pl.BlockSpec(grad.shape, lambda i, far, blocks: (0, 0)))
            args.append(grad)
    columns = sum(g.shape[1] for g in terms[0][1])
    rows = width * len(terms)
    return pl.pallas_call(
        functools.partial(outer_kernel, [len(grads) for _, grads in terms]),
        grid_spec=pltpu.PrefetchScalarGridSpec(
            num_scalar_prefetch=2,
            grid=(7,),
            in_specs=specs,
            out_specs=pl.BlockSpec(
                (rows, columns), lambda i, far, blocks: (blocks[far[0] ^ (i + 1)], 0)
            ),
        ),
        out_shape=shaped(8 * rows, columns, dtype=BF16),
        compiler_params=pltpu.CompilerParams(vmem_limit_bytes=VMEM_LIMIT),
        cost_estimate=lasts(8.0 * rows * columns / 2**18),
    )(far, blocks, *args)


def outer_far(acts, grads):
    columns = grads[0].shape[1] if len(acts) == 2 else sum(g.shape[1] for g in grads)
    total, width = acts[0].shape[0], acts[0].shape[1] // len(LATE)
    first_block = pl.BlockSpec((total, width), lambda i: (0, 0))
    whole = lambda a: pl.BlockSpec(a.shape, lambda i: (0, 0))

    def kernel(*refs):
        first, second = refs[-2:]
        given = refs[len(acts) : -2]
        if len(acts) == 2:
            first[...] = dot(refs[0][...], given[0][...], TN).astype(BF16)
            second[...] = dot(refs[1][...], given[1][...], TN).astype(BF16)
            return
        start = 0
        for grad in given:
            wide = grad.shape[1]
            both = dot(refs[0][...], grad[...], TN).astype(BF16)
            first[:, start : start + wide] = both[: width // 2]
            second[:, start : start + wide] = both[width // 2 :]
            start += wide

    half = shaped(width if len(acts) == 2 else width // 2, columns, dtype=BF16)
    return pl.pallas_call(
        kernel,
        grid=(1,),
        in_specs=[first_block] * len(acts) + [whole(grad) for grad in grads],
        out_specs=[whole(half), whole(half)],
        out_shape=[half, half],
        compiler_params=pltpu.CompilerParams(vmem_limit_bytes=VMEM_LIMIT),
    )(*acts, *grads)


def project_kernel(terms, late, spot_ref, *refs):
    out_ref = refs[-1]
    total = None
    for k in range(terms):
        weight = refs[terms + k][...]
        if k == 0:
            for n in range(late):
                here = pl.program_id(0) == spot_ref[LATE[n]]
                weight = jnp.where(here, refs[2 * terms + n][...], weight)
        term = dot(refs[k][...], weight, NT)
        total = term if total is None else total + term
    out_ref[...] = total.astype(out_ref.dtype)


def project(ring, spots, acts, weights, late, second):
    if not ring.on:
        return sum(dot(a, w, NT) for a, w in zip(acts, weights)).astype(BF16)
    rows, width = acts[0].shape[0], 256
    whole = lambda i, spot: (0, 0)
    half = lambda i, spot: (second, 0)
    return pl.pallas_call(
        functools.partial(project_kernel, len(acts), len(late)),
        grid_spec=pltpu.PrefetchScalarGridSpec(
            num_scalar_prefetch=1,
            grid=(weights[0].shape[0] // width,),
            in_specs=[pl.BlockSpec(a.shape, whole) for a in acts]
            + [pl.BlockSpec((width, w.shape[1]), lambda i, spot: (i, 0)) for w in weights]
            + [
                pl.BlockSpec((width, w.shape[1]), half if w.shape[0] > width else whole)
                for w in late
            ],
            out_specs=pl.BlockSpec((rows, width), lambda i, spot: (0, i)),
        ),
        out_shape=shaped(rows, weights[0].shape[0], dtype=BF16),
        compiler_params=pltpu.CompilerParams(vmem_limit_bytes=VMEM_LIMIT),
        cost_estimate=lasts(7.0 * sum(a.shape[1] for a in acts) / 1024),
    )(spots, *acts, *weights, *late)


def block_total(refs, cut):
    return sum(ref[cut].astype(F32) for ref in refs)


def total_zo_kernel(own_ref, right_ref, left_ref, w_ref, gz_ref, go_ref, met_ref):
    refs = own_ref, right_ref, left_ref
    rows = w_ref.shape[0]
    g_z = block_total(refs, slice(0, rows))
    gz_ref[...] = g_z
    go_ref[...] = block_total(refs, slice(rows, 2 * rows)).T
    met_ref[...] = jnp.sum(g_z * w_ref[...].astype(F32), axis=1, keepdims=True)


def total_in_kernel(own_ref, right_ref, left_ref, w_ref, met_in, gx_ref, gb_ref, gd_ref, met_ref):
    total = block_total((own_ref, right_ref, left_ref), slice(None))
    inner, heads = gx_ref.shape[1], gd_ref.shape[1]
    gx_ref[...] = total[:, :inner]
    gb_ref[...] = total[:, inner : inner + gb_ref.shape[1]]
    start = inner + gb_ref.shape[1]
    gd_ref[...] = total[:, start : start + heads]
    met = jnp.sum(total * w_ref[...].astype(F32), axis=1, keepdims=True)
    met_ref[...] = met_in[...] + met


def totals(kernel, whole, came, others, shapes):
    rows = came[0].shape[0]
    fixed = lambda i: (0, 0)
    arrays = [*came, *others]
    return pl.pallas_call(
        kernel,
        grid=(1,),
        in_specs=[pl.BlockSpec((rows, whole.shape[1]), fixed)]
        + [pl.BlockSpec(a.shape, fixed) for a in arrays],
        out_specs=[pl.BlockSpec(shape.shape, fixed) for shape in shapes],
        out_shape=shapes,
        compiler_params=pltpu.CompilerParams(vmem_limit_bytes=VMEM_LIMIT),
    )(whole, *arrays)


def shaped(*shape, dtype=F32):
    return jax.ShapeDtypeStruct(shape, dtype)


def call(kernel, grid, ins, outs, shapes, scratch=(), micros=5.0):
    return pl.pallas_call(
        kernel,
        grid=grid,
        in_specs=ins,
        out_specs=outs,
        out_shape=shapes,
        scratch_shapes=list(scratch),
        compiler_params=pltpu.CompilerParams(vmem_limit_bytes=VMEM_LIMIT),
        cost_estimate=lasts(micros),
    )


def conv_back(d_conv, given, after, taps, batch, length, rows):
    width = d_conv.shape[1]
    count = length // rows
    turn = lambda b, i: (b * count + count - 1 - i, 0)
    block = pl.BlockSpec((rows, width), turn)
    total = batch * length
    return call(
        conv_back_kernel,
        (batch, count),
        [
            block,
            block,
            pl.BlockSpec((1, HALO, width), lambda b, i: (b, 0, 0)),
            pl.BlockSpec((KERNEL, width), lambda b, i: (0, 0)),
        ],
        [
            block,
            pl.BlockSpec((KERNEL, width), lambda b, i: (0, 0)),
            pl.BlockSpec((1, 1, rows), lambda b, i: (b * count + count - 1 - i, 0, 0)),
        ],
        [
            shaped(total, width, dtype=BF16),
            shaped(KERNEL, width),
            shaped(batch * count, 1, rows),
        ],
        [pltpu.VMEM((HALO, width), F32)],
        micros=8.0 * total * width / 2**20,
    )(d_conv, given, after, taps)


def body(
    tokens, norm_gain, w_z, w_x, w_bc, w_dt, conv_x, conv_bc, dt_bias, decay_rate,
    skip_gain, gate_gain, w_out, grad_out,
):
    ring = Ring(lax.axis_size("seq"))
    batch, length, own_width = tokens.shape
    model = norm_gain.shape[0] * ring.size
    total = batch * length
    inner = w_z.shape[1]
    heads = dt_bias.shape[0]
    inner_all = inner * lax.axis_size("head")
    pairs = heads // 2
    rows = min(SPAN, length)
    count = length // rows
    blocks = batch * count
    margin = KERNEL - 1
    here = lax.axis_index("head")

    slab = tokens.reshape(total, own_width)
    cot_rows = grad_out.reshape(total, own_width)
    bias_row = dt_bias.reshape(1, heads)
    rate_row = decay_rate.reshape(1, heads)
    skip_lanes = jnp.repeat(skip_gain, P_SIZE).reshape(1, inner)
    gate_f = gate_gain.astype(F32).reshape(1, inner)
    conv_xf = conv_x.astype(F32)
    conv_bcf = conv_bc.astype(F32)
    conv_w = jnp.concatenate([conv_xf, conv_bcf], axis=1)

    def edge(arrays, last):
        cut = [array.reshape(batch, length, -1) for array in arrays]
        cut = [array[:, length - margin :] if last else array[:, :margin] for array in cut]
        cut = jnp.concatenate(cut, axis=2)
        moves = [(i, i + 1) for i in range(ring.size - 1)]
        if not last:
            moves = [(b, a) for a, b in moves]
        got = lax.ppermute(cut, "seq", moves).astype(F32)
        pad = ((0, 0), (HALO - margin, 0), (0, 0)) if last else ((0, 0), (0, HALO - margin), (0, 0))
        return jnp.pad(got, pad)

    at = lambda b, i: (b * count + i, 0)
    back = lambda b, i: (b * count + count - 1 - i, 0)
    at3 = lambda b, i: (b * count + i, 0, 0)
    back3 = lambda b, i: (b * count + count - 1 - i, 0, 0)
    seq3 = lambda b, i: (b, 0, 0)
    fixed = lambda b, i: (0, 0)
    row_heads = pl.BlockSpec((1, heads), fixed)
    row_inner = pl.BlockSpec((1, inner), fixed)
    state_spec = pl.BlockSpec((1, N, inner), seq3)
    pair_flops = total * rows * inner

    block_spec = pl.BlockSpec((rows, inner), at)
    row_out = pl.BlockSpec((1, 1, rows), at3)
    c_spec = pl.BlockSpec((rows, LANES), lambda b, i: (b * count + i, inner // LANES + 1))
    head_cols = pl.BlockSpec((rows, heads), at)
    v_back = pl.BlockSpec((rows, inner + 2 * N), back)
    block_back = pl.BlockSpec((rows, inner), back)
    heads_back = pl.BlockSpec((rows, heads), back)
    bc_back = pl.BlockSpec((rows, 2 * N), back)
    def scan(x_in, bc_in, halo, dt_raw):
        conv_out, y_local, steps, cumulative, begun, offsets, left, left_w = call(
            functools.partial(scan_kernel, pairs),
            (batch, count),
            [
                pl.BlockSpec((rows, inner), at),
                pl.BlockSpec((rows, 2 * N), at),
                pl.BlockSpec((1, HALO, inner + 2 * N), seq3),
                pl.BlockSpec((rows, heads), at),
                pl.BlockSpec((KERNEL, inner + 2 * N), fixed),
                row_heads,
                row_heads,
                row_inner,
            ],
            [
                pl.BlockSpec((rows, inner + 2 * N), at),
                pl.BlockSpec((rows, inner), at),
                pl.BlockSpec((rows, heads), at),
                pl.BlockSpec((rows, heads), at),
                pl.BlockSpec((1, N, inner), at3),
                pl.BlockSpec((1, 1, inner), at3),
                state_spec,
                pl.BlockSpec((1, 1, inner), seq3),
            ],
            [
                shaped(total, inner + 2 * N),
                shaped(total, inner),
                shaped(total, heads),
                shaped(total, heads),
                shaped(blocks, N, inner),
                shaped(blocks, 1, inner),
                shaped(batch, N, inner),
                shaped(batch, 1, inner),
            ],
            [
                pltpu.VMEM((HALO, inner + 2 * N), F32),
                pltpu.VMEM((N, inner), F32),
                pltpu.VMEM((8, heads), F32),
                pltpu.VMEM((8, inner), F32),
            ],
            micros=14.5,
        )(x_in, bc_in, halo, dt_raw, conv_w, bias_row, rate_row, skip_lanes)
        return conv_out, y_local, steps, cumulative, begun, offsets, left, left_w

    own_block = model // ring.size
    g_rows = min(256, length)
    g_count = length // g_rows
    g_at = lambda b, i: (b * g_count + i, 0)
    g_at3 = lambda b, i: (b * g_count + i, 0, 0)
    g_block, g_row = pl.BlockSpec((g_rows, inner), g_at), pl.BlockSpec((1, 1, g_rows), g_at3)
    g_c = pl.BlockSpec((g_rows, LANES), lambda b, i: (b * g_count + i, inner // LANES + 1))
    g_heads_spec = pl.BlockSpec((g_rows, heads), g_at)
    act_spec = pl.BlockSpec((g_rows, own_block), g_at)
    late_spec = pl.BlockSpec((own_block, inner), fixed)
    wide_scratch = [pltpu.VMEM((g_rows, inner), F32), pltpu.VMEM((g_rows, inner), F32)]

    def gate(y_local, conv_out, came, cumulative, z_part, dm_part, late):
        return call(
            functools.partial(gate_kernel, pairs),
            (batch, g_count),
            [
                g_block, g_c, state_spec, g_heads_spec, g_block, g_block, row_inner,
                act_spec, act_spec, late_spec, late_spec,
            ],
            [g_block, pl.BlockSpec((1, 2, g_rows), g_at3)],
            [shaped(total, inner), shaped(batch * g_count, 2, g_rows)],
            wide_scratch,
            micros=7.0,
        )(y_local, conv_out, came, cumulative, z_part, dm_part, gate_f, *late)

    def gate_back(dm_part, ssd, z_part, gate_scale, product, cumulative, conv_out, late):
        return call(
            functools.partial(gate_back_kernel, pairs, inner_all),
            (batch, g_count),
            [
                g_block, g_block, g_block, g_row, g_row, row_inner, g_heads_spec, g_c,
                act_spec, act_spec, late_spec, late_spec,
            ],
            [g_block, g_block, state_spec, g_row, row_inner, g_block],
            [
                shaped(total, inner, dtype=BF16),
                shaped(total, inner),
                shaped(batch, N, inner),
                shaped(batch * g_count, 1, g_rows),
                shaped(1, inner),
                shaped(total, inner, dtype=BF16),
            ],
            wide_scratch,
            micros=9.0,
        )(dm_part, ssd, z_part, gate_scale, product, gate_f, cumulative, conv_out, *late)

    def scan_back(conv_out, d_ssd, steps, begun, offsets, came):
        du_local, dbc_local = call(
            functools.partial(scan_back_kernel, pairs),
            (batch, count),
            [
                v_back, block_back, heads_back, row_heads,
                pl.BlockSpec((1, N, inner), back3),
                pl.BlockSpec((1, 1, inner), back3),
                state_spec,
            ],
            [block_back, bc_back],
            [shaped(total, inner), shaped(total, 2 * N)],
            [pltpu.VMEM((N, inner), F32)],
            micros=18.0,
        )(conv_out, d_ssd, steps, rate_row, begun, offsets, came)
        return du_local, dbc_local

    def finish(conv_out, d_ssd, du_local, ssd, steps, cumulative, left_w, later, at_end, dbc_local, dt_raw):
        f_back = lambda b, i: (b * g_count + g_count - 1 - i, 0)
        f_spec = lambda width: pl.BlockSpec((g_rows, width), f_back)
        f_v, f_block, f_heads = f_spec(inner + 2 * N), f_spec(inner), f_spec(heads)
        f_maps, f_lanes = f_spec(2 * N), f_spec(LANES)
        lane_head = lax.broadcasted_iota(jnp.int32, (inner, heads), 0) // P_SIZE
        picker = (lane_head == lax.broadcasted_iota(jnp.int32, (inner, heads), 1)).astype(BF16)
        d_conv_x, d_bc_keep, d_bc_send, d_dt, g_skip, g_heads = call(
            functools.partial(finish_kernel, pairs, ring.on),
            (batch, g_count),
            [
                f_v, f_block, f_block, f_block, f_heads, f_heads,
                pl.BlockSpec((1, 1, inner), seq3), state_spec, state_spec, f_maps, f_heads,
                row_heads, row_heads, row_inner,
                pl.BlockSpec((inner, heads), fixed), pl.BlockSpec(memory_space=pltpu.SMEM),
            ],
            [
                f_block, f_lanes, f_lanes, f_heads, row_inner,
                pl.BlockSpec((2, heads), fixed),
            ],
            [
                shaped(total, inner, dtype=BF16),
                shaped(total, LANES),
                shaped(total, LANES),
                shaped(total, heads, dtype=BF16),
                shaped(1, inner),
                shaped(2, heads),
            ],
            [
                pltpu.VMEM((8, heads), F32),
                pltpu.VMEM((2 * g_rows, inner), BF16),
                pltpu.VMEM((2 * g_rows, inner), BF16),
            ],
            micros=15.0,
        )(
            conv_out, d_ssd, du_local, ssd, steps, cumulative, left_w, later, at_end, dbc_local,
            dt_raw, bias_row, rate_row, skip_lanes, picker,
            jnp.stack([here & 1, here >> 1]).astype(jnp.int32),
        )
        return d_conv_x, d_bc_keep, d_bc_send, d_dt, g_skip, g_heads

    split_pass = ring.on and batch == 2
    forth, back_pass = Passing(ring, 1, inner), Passing(ring, -1, inner)
    slope = lambda v: silu_slope(v, jax.nn.sigmoid(v))

    group = 2 * N // 4 if ring.on else 2 * N
    edge_at = inner + group
    spare = -(group + heads) % LANES
    per = w_z.shape[0]
    own_columns = lambda a: lax.dynamic_slice_in_dim(a, here * group, group, 1) if ring.on else a
    all_in = jnp.concatenate(
        [w_x, own_columns(w_bc), w_dt, jnp.zeros((w_x.shape[0], spare), BF16)], axis=1
    )

    def by_group(pieces):
        own, near, far, both = pieces
        return [
            jnp.where(
                here == g, own, jnp.where(here == g ^ 1, near, jnp.where(here == g ^ 2, far, both))
            )
            for g in range(4)
        ]

    def gather_groups(own):
        far = swap(own, "head", 2)
        return by_group([own, swap(own, "head", 1), far, swap(far, "head", 1)])

    def fold(a):
        return jnp.concatenate([a[: total // 2], a[total // 2 :]], axis=1)

    def unfold(a):
        n = a.shape[1] // 2
        return jnp.concatenate([a[:, :n], a[:, n:]], axis=0)
    spots, order = (ring.spots(), ring.blocks()) if ring.on else (None, None)

    def work(all_in, slab):
        own_gain = own_features(ring, norm_gain.astype(F32), own_width)
        square = head_sum(jnp.sum(slab * slab, axis=1))
        scale = lax.rsqrt(square / model + EPS)
        own_normed = (slab * scale[:, None] * own_gain).astype(BF16)
        return ring.hop((all_in, all_in)), own_gain, scale, own_normed

    hop1, own_gain, scale, own_normed = ring.phase(work, all_in, slab)
    far = across(ring, own_normed)

    def work(hop1, own, w_z, w_out, cot_rows):
        zo_in = jnp.concatenate([w_z, w_out.T], axis=0)
        hop2 = ring.hop(hop1)
        return hop2, ring.hop(hop2), beside(ring, own), zo_in, cot_rows.astype(BF16)

    hop2, hop3, near, zo_in, own_cot = ring.phase(work, hop1, own_normed, w_z, w_out, cot_rows)
    hop4, both = ring.phase(
        lambda hop3, far: (ring.last_hop(hop3), corner(ring, own_normed, far)), hop3, far
    )
    normed = (both, near, far, own_normed) if ring.on else (both,)

    def project_in(normed, hop1, hop2, hop3, hop4):
        if ring.on:
            x_in, rest, x_w, rest_w = with_spots(
                in_project_kernel, spots, normed, [all_in, *hop1, *hop2, *hop3, *hop4],
                [True, True, False, False],
                [
                    shaped(total, inner, dtype=BF16), shaped(total, all_in.shape[1] - inner),
                    shaped(model, inner, dtype=BF16),
                    shaped(model, all_in.shape[1] - inner, dtype=BF16),
                ],
            )
            groups = gather_groups(fold(rest[:, :group]).astype(BF16))
            bc_in = jnp.concatenate([unfold(piece) for piece in groups], axis=1)
        else:
            x_w = lax.all_gather(w_x, "seq", axis=0, tiled=True)
            rest_w = lax.all_gather(all_in[:, inner:], "seq", axis=0, tiled=True)
            rest = dot(normed[0], rest_w)
            x_in, bc_in = dot(normed[0], x_w).astype(BF16), rest[:, :group].astype(BF16)
        bc_own = jnp.pad(rest[:, :group].astype(BF16), ((0, 0), (0, -group % LANES)))
        return (
            x_in, bc_in, bc_own, rest[:, group : group + heads], x_w, rest_w,
            edge([x_in, bc_in], True),
        )

    def work(normed, hop1, hop2, hop3, hop4, zo_in):
        return ring.hop((zo_in, zo_in)), ring.phase(project_in, normed, hop1, hop2, hop3, hop4)

    hop1, (x_in, bc_in, bc_own, dt_raw, x_w, rest_w, halo) = ring.phase(
        work, normed, hop1, hop2, hop3, hop4, zo_in
    )

    def work(hop1, x_in, bc_in, halo, dt_raw, own_cot):
        scanned = scan(x_in, bc_in, halo, dt_raw)
        held = forth.pair(forth.begin(scanned[6], scanned[7])) if split_pass else ()
        return ring.hop(hop1), scanned, held, beside(ring, own_cot), across(ring, own_cot)

    hop2, scanned, held, near, far = ring.phase(work, hop1, x_in, bc_in, halo, dt_raw, own_cot)
    conv_out, y_local, steps, cumulative, begun, offsets, left, left_w = scanned
    def work(hop1, hop2, held, far, conv_out, normed):
        moving = ring.hop(hop2)
        value = conv_out[:, inner:]
        if not ring.on:
            z_w = lax.all_gather(w_z, "seq", axis=0, tiled=True)
            out_w = lax.all_gather(w_out.T, "seq", axis=0, tiled=True)
            cot = (corner(ring, own_cot, far),)
            none = jnp.zeros((total, own_block), BF16)
            given = dot(normed[0], z_w), dot(cot[0], out_w), z_w, out_w, none, none
            return moving, held, cot, given, slope(value)
        value = [value[:, g * group : (g + 1) * group] for g in range(4)]
        value = jnp.where(
            here < 2, jnp.where(here == 0, value[0], value[1]),
            jnp.where(here == 2, value[2], value[3]),
        )
        both = ring.phase(lambda far: corner(ring, own_cot, far), far)
        wide, weight = shaped(total, inner), shaped(model, inner, dtype=BF16)
        act = shaped(total, len(LATE) * own_block, dtype=BF16)
        given = with_spots(
            gate_project_kernel, spots, (*normed, both, near, far, own_cot), [zo_in, *hop1, *hop2],
            [True, True, False, False, True, True], [wide, wide, weight, weight, act, act],
        )
        held = forth.next_line(held) if split_pass else ()
        return moving, held, both, given, slope(value)

    hop3, held, cot, given, own_slope = ring.phase(
        work, hop1, hop2, held, far, conv_out, normed
    )
    if ring.on:
        cot = (cot, near, far, own_cot)
    z_part, dm_part, z_w, out_w, normed_late, cot_late = given

    def work(hop3, held, z_part, dm_part, normed_late, cot_late):
        held = forth.further_lines(held) if split_pass else ()
        if ring.on:
            wide = shaped(total, inner)
            z_part, dm_part = with_spots(
                gate_more_kernel, spots, (z_part, dm_part, normed_late, cot_late), hop3,
                [True, True], [wide, wide],
            )
        came = forth.end(held) if split_pass else states_scan(left, left_w, 1)
        return ring.last_hop(hop3), came, z_part, dm_part

    hop4, came, z_part, dm_part = ring.phase(
        work, hop3, held, z_part, dm_part, normed_late, cot_late
    )
    if not ring.on:
        hop4 = (jnp.zeros((own_block, inner), BF16),) * 2
    late = (normed_late, cot_late, *hop4)
    late_z, late_out = ([half, hop3[1], hop3[0]] if ring.on else [] for half in hop4)

    ssd, square_g = gate(y_local, conv_out, came, cumulative, z_part, dm_part, late)
    square_g = head_sum(square_g)
    gate_scale = lax.rsqrt(square_g[:, 0:1] / inner_all + EPS)
    product = square_g[:, 1:2]
    d_z, d_ssd, d_left, met_z, g_gate, mixed = gate_back(
        dm_part, ssd, z_part, gate_scale, product, cumulative, conv_out, late
    )

    far_spot = spots[4:5] if ring.on else None

    def work(d_left, left_w, normed, d_z, mixed, cot, normed_late, cot_late):
        held = back_pass.pair(back_pass.begin(d_left, left_w)) if split_pass else ()
        if ring.on:
            sums = ring.send(*outer_far([normed_late, cot_late], [d_z, mixed]))
            g_zo = outer(far_spot, order, (normed, [d_z]), (cot, [mixed]))
            return held, ring.add(g_zo, sums, 3), g_zo
        return held, (), (dot(normed[0], d_z, TN), dot(cot[0], mixed, TN))

    held, sums, g_zo = ring.phase(
        work, d_left, left_w, normed, d_z, mixed, cot, normed_late, cot_late
    )

    def work(held, sums, conv_out, d_ssd, steps, begun, offsets, came):
        sums = ring.hop(sums)
        held = back_pass.next_line(held) if split_pass else ()
        at_end = jnp.exp(left_w) * came + left
        return held, sums, scan_back(conv_out, d_ssd, steps, begun, offsets, came), at_end

    held, sums, (du_local, dbc_local), at_end = ring.phase(
        work, held, sums, conv_out, d_ssd, steps, begun, offsets, came
    )

    def work(held, sums, g_zo, mixed, out_w, late_out):
        held = back_pass.further_lines(held) if split_pass else ()
        branch = project(ring, spots, [mixed], [out_w], late_out, 1)
        return held, ring.add(g_zo, sums, 2), branch

    held, sums, branch = ring.phase(work, held, sums, g_zo, mixed, out_w, late_out)

    def work(held, branch):
        later = back_pass.end(held) if split_pass else states_scan(d_left, left_w, -1)
        return later, scatter_near(ring, branch)

    later, (out_far, out_own) = ring.phase(work, held, branch)

    def finish_maps(later, du_local, dbc_local, own_slope):
        d_conv_x, mine, send, d_dt, g_skip, g_heads = finish(
            conv_out, d_ssd, du_local, ssd, steps, cumulative, left_w, later, at_end,
            dbc_local, dt_raw,
        )
        if ring.on:
            mine = mine + swap(send, "head", 1)
            mine = mine[:, :group] + unfold(swap(fold(mine[:, group:]), "head", 2))
        else:
            mine = head_sum(jnp.concatenate([mine, send], axis=1))
        d_conv_bc = jnp.pad((mine * own_slope).astype(BF16), ((0, 0), (0, -group % LANES)))
        after = edge([d_conv_x, d_conv_bc], False)
        return d_conv_x, d_conv_bc, d_dt, g_skip, g_heads, after

    def work(later, sums, g_zo, du_local, dbc_local, own_slope):
        sums = ring.hop(sums)
        given = ring.phase(finish_maps, later, du_local, dbc_local, own_slope)
        return ring.add(g_zo, sums, 1), given

    sums, (d_conv_x, d_conv_bc, d_dt, g_skip, g_heads, after) = ring.phase(
        work, later, sums, g_zo, du_local, dbc_local, own_slope
    )

    share = 1.0 if ring.on else jnp.where(here == 0, 1.0, 0.0)
    after_x, after_bc = after[:, :, :inner], after[:, :, inner:]
    own_taps = jnp.pad(own_columns(conv_bcf), ((0, 0), (0, -group % LANES)))

    def work(
        sums, g_zo, d_conv_bc, after_bc, d_conv_x, after_x, d_dt, normed, normed_late, out_far
    ):
        d_x, g_conv_x, met_x = conv_back(d_conv_x, x_in, after_x, conv_xf, batch, length, g_rows)
        d_bc, g_conv_bc, met_bc = conv_back(
            d_conv_bc, bc_own, after_bc, own_taps, batch, length, g_rows
        )
        fill = jnp.zeros((total, spare), BF16)
        d_rest = jnp.concatenate([d_bc[:, :group], d_dt, fill], axis=1)
        last = ring.hop(sums)
        if ring.on:
            sums = ring.send(*outer_far([normed_late], [d_x, d_rest]))
            g_all = outer(far_spot, order, (normed, [d_x, d_rest]))
            sums = ring.add(g_all, sums, 3)
        else:
            sums = ()
            g_all = jnp.concatenate([dot(normed[0], d, TN) for d in (d_x, d_rest)], axis=1)
        met_dt = jnp.sum(d_dt.astype(F32) * dt_raw, axis=1)
        met = met_z.reshape(total) + (met_x + share * met_bc).reshape(total) + met_dt
        return (
            last, sums, d_x, d_rest, g_conv_x, g_conv_bc, met, g_all, across(ring, out_far),
        )

    last, sums, d_x, d_rest, g_conv_x, g_conv_bc, met, g_all, out_far = ring.phase(
        work, sums, g_zo, d_conv_bc, after_bc, d_conv_x, after_x, d_dt, normed, normed_late, out_far
    )
    g_conv_bc = g_conv_bc[:, :group]
    if ring.on:
        none = jnp.zeros((KERNEL, 2 * N), F32)
        g_conv_bc = lax.dynamic_update_slice(none, g_conv_bc, (0, here * group))
    small = jnp.concatenate(
        [
            g_conv_x.reshape(-1), g_conv_bc.reshape(-1), g_gate.reshape(-1),
            g_skip.reshape(-1), g_heads.reshape(-1),
        ]
    )

    def one_swap(array, bit):
        return array + swap(array, "seq", bit) if ring.on else array

    def work(sums, small, d_z, d_x, d_rest, z_w, x_w, rest_w, late_z, met):
        sums = ring.hop(sums)
        met = met + swap(met, "head", 1) if ring.on else head_sum(met)
        if not ring.on:
            columns = lax.broadcasted_iota(jnp.int32, (1, rest_w.shape[1]), 1)
            rest_w = jnp.where((columns < group) & (here > 0), 0.0, rest_w.astype(F32)).astype(BF16)
        back = project(ring, spots, [d_z, d_x, d_rest], [z_w, x_w, rest_w], late_z, 0)
        return sums, back, one_swap(small, 1), met

    sums, back_terms, small, met = ring.phase(
        work, sums, small, d_z, d_x, d_rest, z_w, x_w, rest_w, late_z, met
    )

    def work(sums, g_all, back_terms, met):
        far, d_normed = scatter_near(ring, back_terms)
        met = met + swap(met, "head", 2) if ring.on else met
        return ring.add(g_all, sums, 2), far, d_normed, met / scale

    sums, far, d_normed, dots = ring.phase(work, sums, g_all, back_terms, met)

    def third(sums, g_all, small, out_far, out_own, g_zo, last):
        mixed_out = slab + scatter_sum(ring, out_far, out_own)
        block, column = shaped(per, inner), shaped(per, 1)
        if ring.on:
            g_z, g_out, met_f = totals(
                total_zo_kernel, g_zo, last, [w_z], [block, shaped(inner, per), column]
            )
        else:
            g_z, g_out = (
                lax.psum_scatter(g.astype(BF16), "seq", scatter_dimension=0, tiled=True).astype(F32)
                for g in g_zo
            )
            g_out, met_f = g_out.T, jnp.sum(g_z * w_z.astype(F32), axis=1, keepdims=True)
        sums = ring.add(g_all, ring.hop(sums), 1)
        small = one_swap(one_swap(small, 2), 4) if ring.on else lax.psum(small, "seq")
        parts, start = [], 0
        for width in [KERNEL * inner, KERNEL * 2 * N, inner, inner, heads, heads]:
            parts.append(small[start : start + width])
            start += width
        return sums, parts, mixed_out, g_z, g_out, met_f

    def fourth(sums, g_all, met_f, sum_bc):
        last = ring.hop(sums)
        shapes = [shaped(per, inner), shaped(per, group), shaped(per, heads), shaped(per, 1)]
        if ring.on:
            g_x, g_bc, g_dt, met_f = totals(
                total_in_kernel, g_all, last, [all_in, met_f], shapes
            )
            g_bc = jnp.concatenate(gather_groups(g_bc), axis=1)
        else:
            g = lax.psum_scatter(g_all.astype(BF16), "seq", scatter_dimension=0, tiled=True)
            g = g.astype(F32)
            g_x, g_bc, g_dt = g[:, :inner], g[:, inner:edge_at], g[:, edge_at : edge_at + heads]
            columns = lax.broadcasted_iota(jnp.int32, (1, g.shape[1]), 1)
            once = jnp.where((columns >= inner) & (columns < edge_at), share, 1.0)
            met_f = met_f + jnp.sum(g * all_in.astype(F32) * once, axis=1, keepdims=True)
            sum_bc = sum_bc * (1.0 / lax.axis_size("head"))
        both = head_sum(jnp.concatenate([met_f[:, 0], sum_bc]))
        g_gain = both[:per] / norm_gain.astype(F32)
        return g_x, g_bc, g_dt, g_gain, both[per:]

    def work(sums, g_all, small, far, d_normed, dots, out_far, out_own, g_zo, last):
        far = across(ring, far)
        sums, parts, *given = third(sums, g_all, small, out_far, out_own, g_zo, last)
        ends = fourth(sums, g_all, given[-1], parts[1])
        d_normed = scatter_sum(ring, far, d_normed)
        grad_tokens = (
            cot_rows
            + (scale[:, None] * own_gain) * d_normed
            - slab * (scale * scale * scale * dots / model)[:, None]
        )
        return parts, given, ends, grad_tokens

    parts, (mixed_out, g_z, g_out, _), ends, grad_tokens = ring.phase(
        work, sums, g_all, small, far, d_normed, dots, out_far, out_own, g_zo, last
    )
    sum_x, _, sum_gate, sum_skip, sum_bias, sum_rate = parts
    g_x, g_bc, g_dt, g_gain, sum_bc = ends

    return (
        mixed_out.reshape(batch, length, own_width),
        grad_tokens.reshape(batch, length, own_width),
        g_gain,
        g_z,
        g_x,
        g_bc,
        g_dt,
        sum_x.reshape(KERNEL, inner),
        sum_bc.reshape(KERNEL, 2 * N),
        sum_bias,
        sum_rate,
        jnp.sum(sum_skip.reshape(heads, P_SIZE), axis=1),
        sum_gate,
        g_out,
    )


def solution(mesh):
    in_specs = (
        P(None, "seq", "head"),
        P("seq"),
        P("seq", "head"),
        P("seq", "head"),
        P("seq", None),
        P("seq", "head"),
        P(None, "head"),
        P(),
        P("head"),
        P("head"),
        P("head"),
        P("head"),
        P("head", "seq"),
        P(None, "seq", "head"),
    )
    out_specs = (
        P(None, "seq", "head"),
        P(None, "seq", "head"),
        P("seq"),
        P("seq", "head"),
        P("seq", "head"),
        P("seq", None),
        P("seq", "head"),
        P(None, "head"),
        P(),
        P("head"),
        P("head"),
        P("head"),
        P("head"),
        P("head", "seq"),
    )
    return jax.shard_map(body, mesh=mesh, in_specs=in_specs, out_specs=out_specs, check_vma=False)
```

```python
import functools

import jax
import jax.numpy as jnp
from jax import lax
from jax.experimental import pallas as pl
from jax.experimental.pallas import tpu as pltpu
from jax.sharding import PartitionSpec as P

P_SIZE = 64
N = 128
KERNEL = 4
SPAN = 128
HALO = 8
ADD_STEPS = 2
LANES = 128
EPS = 1e-05
HIGHEST = lax.Precision.HIGHEST
F32 = jnp.float32
BF16 = jnp.bfloat16
VMEM_LIMIT = 50 * 1024 * 1024
NN = (((1,), (0,)), ((), ()))
NT = (((1,), (1,)), ((), ()))
TN = (((0,), (0,)), ((), ()))


def lasts(micros):
    return pl.CostEstimate(flops=0, bytes_accessed=int(micros * 3.3e6), transcendentals=0)


def dot(left, right, dims=NN, precision=None):
    return lax.dot_general(left, right, dims, precision=precision, preferred_element_type=F32)


def silu_slope(value, logistic):
    return logistic * (1.0 + value * (1.0 - logistic))


class Ring:
    def __init__(self, size):
        self.size = size
        self.on = size == 8 and lax.axis_size("head") == 4
        self.order = list(range(0, size, 2)) + list(range(size - 1, 0, -2))
        here = lax.axis_index("seq")
        self.line, self.side = here >> 1, here & 1
        self.place = jnp.where(self.side == 0, self.line, size - 1 - self.line)

    def spots(self):
        place = (self.place + jnp.arange(self.size, dtype=jnp.int32)) & (self.size - 1)
        side = place >> 2
        line = jnp.where(side == 1, self.size - 1 - place, place)
        bit = lax.axis_index("head") ^ line
        return 2 * jnp.where(bit == 3, 0, jnp.where(bit == 0, 3, bit)) + side

    def blocks(self):
        spot = jnp.arange(self.size, dtype=jnp.int32)
        side, bit = spot & 1, spot >> 1
        bit = jnp.where(bit == 0, 3, jnp.where(bit == 3, 0, bit))
        line = lax.axis_index("head") ^ bit
        place = jnp.where(side == 1, self.size - 1 - line, line)
        return (place - self.place) & (self.size - 1)

    def shift(self, array, by):
        order, size = self.order, self.size
        return lax.ppermute(array, "seq", [(order[i], order[(i + by) % size]) for i in range(size)])

    def hop(self, moving):
        if not self.on:
            return moving
        return self.shift(moving[0], 1), self.shift(moving[1], -1)

    def last_hop(self, moving):
        if not self.on:
            return moving
        cut = moving[0].shape[0] // 2
        return self.shift(moving[0][:cut], 1), self.shift(moving[1][cut:], -1)

    def part(self, whole, k):
        n = whole.shape[0] // self.size
        k = k % self.size
        return whole[k * n : (k + 1) * n]

    def send(self, first, second):
        return self.shift(first, 1), self.shift(second, -1)

    def add(self, whole, came, k):
        if not self.on:
            return ()
        rows, columns = 2 * came[0].shape[0] if k == 3 else came[0].shape[0], whole.shape[1]
        halves = k == self.size // 2 - 1
        steps = ADD_STEPS
        tile = rows // steps

        def kernel(a_ref, b_ref, right_ref, left_ref, out_a_ref, out_b_ref):
            right, left = right_ref[...].astype(F32), left_ref[...].astype(F32)
            if halves:
                upper = pl.program_id(0) < steps // 2
                right, left = jnp.where(upper, right, 0.0), jnp.where(upper, 0.0, left)
            out_a_ref[...] = (a_ref[...].astype(F32) + right).astype(BF16)
            out_b_ref[...] = (b_ref[...].astype(F32) + left).astype(BF16)

        block = lambda at: pl.BlockSpec((tile, columns), at)
        plain = lambda i: (i, 0)
        out = jax.ShapeDtypeStruct((rows, columns), BF16)
        return pl.pallas_call(
            kernel,
            grid=(steps,),
            in_specs=[
                block(lambda i: (steps * k + i, 0)),
                block(lambda i: (steps * (self.size - k) + i, 0)),
                block((lambda i: (jnp.minimum(i, steps // 2 - 1), 0)) if halves else plain),
                block((lambda i: (jnp.maximum(i - steps // 2, 0), 0)) if halves else plain),
            ],
            out_specs=[block(plain), block(plain)],
            out_shape=[out, out],
            compiler_params=pltpu.CompilerParams(vmem_limit_bytes=VMEM_LIMIT),
        )(whole, whole, *came)

    def phase(self, work, *args):
        if not self.on:
            return work(*args)
        shapes = jax.eval_shape(work, *args)

        def idle(*args):
            return jax.tree.map(lambda x: jnp.zeros(x.shape, x.dtype), shapes)

        return lax.cond(lax.axis_index("seq") < self.size, work, idle, *args)


def swap(array, axis, bit):
    size = lax.axis_size(axis)
    return lax.ppermute(array, axis, [(i, i ^ bit) for i in range(size)])


def head_sum(array):
    return lax.psum(array, "head")


def seq_sum(ring, array):
    if not ring.on:
        return lax.psum(array, "seq")
    bit = 1
    while bit < ring.size:
        array = array + swap(array, "seq", bit)
        bit *= 2
    return array


def own_features(ring, block, own_width):
    if not ring.on:
        whole = lax.all_gather(block, "seq", axis=0, tiled=True)
        return lax.dynamic_slice_in_dim(whole, lax.axis_index("head") * own_width, own_width)

    def fetch(flip):
        index = lambda line, side, head: (2 * line + side) * 4 + head
        return lax.ppermute(
            block,
            ("seq", "head"),
            [
                (index(head, side ^ flip, line), index(line, side, head))
                for line in range(4)
                for side in range(2)
                for head in range(4)
            ],
        )

    same, other = fetch(0), fetch(1)
    even = ring.side == 0
    return jnp.concatenate([jnp.where(even, same, other), jnp.where(even, other, same)])


def corner(ring, own, far):
    if not ring.on:
        return lax.all_gather(own, "head", axis=1, tiled=True)
    return swap(far, "head", 1)


def beside(ring, array):
    return swap(array, "head", 1) if ring.on else array


def across(ring, array):
    return swap(array, "head", 2) if ring.on else array


def scatter_near(ring, whole):
    if not ring.on:
        return whole, None
    width = whole.shape[1] // 4
    part = lambda k: whole[:, k * width : (k + 1) * width]
    far = swap(part(0), "head", 1)
    near = swap(part(1), "head", 1)
    far = (part(2).astype(F32) + far.astype(F32)).astype(BF16)
    return far, part(3).astype(F32) + near.astype(F32)


def scatter_sum(ring, far, mine):
    if not ring.on:
        return lax.psum_scatter(far, "head", scatter_dimension=1, tiled=True).astype(F32)
    return mine + far.astype(F32)


def shift_flat(array, by):
    size = lax.axis_size("seq")
    return lax.ppermute(array, "seq", [(i, i + by) for i in range(size) if 0 <= i + by < size])


def states_scan(state, log_decay, direction):
    incl_s, incl_w = state, log_decay
    excl_s, excl_w = jnp.zeros_like(state), jnp.zeros_like(log_decay)
    by = 1
    while by < lax.axis_size("seq"):
        got_s = shift_flat(incl_s.astype(BF16), by * direction).astype(F32)
        got_w = shift_flat(incl_w, by * direction)
        excl_s = jnp.exp(excl_w) * got_s + excl_s
        excl_w = excl_w + got_w
        incl_s = jnp.exp(incl_w) * got_s + incl_s
        incl_w = incl_w + got_w
        by *= 2
    return excl_s


def log_rows(log_decay):
    high = log_decay.astype(BF16).astype(F32)
    middle = (log_decay - high).astype(BF16).astype(F32)
    low = log_decay - high - middle
    row = lax.broadcasted_iota(jnp.int32, (16, log_decay.shape[1]), 0)
    parts = jnp.where(row == 0, high, jnp.where(row == 1, middle, low))
    return jnp.where(row < 3, parts, 0.0).astype(BF16)


def log_sum(rows):
    rows = rows.astype(F32)
    return rows[0:1] + rows[1:2] + rows[2:3]


def pass_begin_kernel(even_ref, lead_ref, state_ref, log_ref, keep_ref, kept_ref, send_ref):
    even = even_ref[0] == 1
    keep_ref[...] = jnp.where(even, state_ref[0], state_ref[1])
    kept_ref[...] = jnp.where(even, log_ref[0], log_ref[1])
    send_ref[:N] = jnp.where(even, state_ref[1], state_ref[0]).astype(BF16)
    send_ref[N:] = log_rows(jnp.where(even, log_ref[1], log_ref[0]))


def pass_pair_kernel(
    even_ref, lead_ref, keep_ref, kept_ref, got_ref, first_ref, d_first_ref, both_ref, pair_ref, send_ref
):
    leads = lead_ref[0] == 1
    keep, kept = keep_ref[...], kept_ref[...]
    got, gotten = got_ref[:N].astype(F32), log_sum(got_ref[N:])
    first = jnp.where(leads, keep, got)
    both = jnp.exp(jnp.where(leads, gotten, kept)) * first + jnp.where(leads, got, keep)
    first_ref[...] = first
    d_first_ref[...] = jnp.exp(jnp.where(leads, kept, gotten))
    both_ref[...] = both
    pair_ref[...] = jnp.exp(kept + gotten)
    send_ref[:N] = both.astype(BF16)
    send_ref[N:] = log_rows(kept + gotten)


def pass_line_kernel(even_ref, lead_ref, both_ref, pair_ref, got_ref, carry_ref, before_ref, send_ref):
    carry = got_ref[:N].astype(F32)
    carry_ref[...] = carry
    before_ref[...] = jnp.exp(log_sum(got_ref[N:]))
    send_ref[...] = (pair_ref[...] * carry + both_ref[...]).astype(BF16)


def pass_far_kernel(
    even_ref, lead_ref, first_ref, d_first_ref, carry_ref, before_ref, got_ref, mine_ref, send_ref
):
    leads = lead_ref[0] == 1
    carry = before_ref[...] * got_ref[...].astype(F32) + carry_ref[...]
    further = d_first_ref[...] * carry + first_ref[...]
    mine_ref[...] = jnp.where(leads, carry, further)
    send_ref[...] = jnp.where(leads, further, carry).astype(BF16)


def pass_end_kernel(even_ref, lead_ref, mine_ref, got_ref, out_ref):
    even = even_ref[0] == 1
    mine, got = mine_ref[...], got_ref[...].astype(F32)
    out_ref[0] = jnp.where(even, mine, got)
    out_ref[1] = jnp.where(even, got, mine)


class Passing:
    def __init__(self, ring, direction, inner):
        self.direction = direction
        leads = ring.side == 0 if direction > 0 else ring.side == 1
        self.flags = [jnp.where(f, 1, 0).astype(jnp.int32).reshape(1) for f in (ring.side == 0, leads)]
        row = shaped(1, inner)
        self.state, self.row = shaped(N, inner), row
        self.sent, self.sent_log = shaped(N, inner, dtype=BF16), shaped(N + 16, inner, dtype=BF16)

    def step(self, kernel, outs, *args):
        return pl.pallas_call(
            kernel,
            in_specs=[pl.BlockSpec(memory_space=pltpu.SMEM)] * 2
            + [pl.BlockSpec(memory_space=pltpu.VMEM)] * len(args),
            out_specs=jax.tree.map(lambda _: pl.BlockSpec(memory_space=pltpu.VMEM), outs),
            out_shape=outs,
            compiler_params=pltpu.CompilerParams(vmem_limit_bytes=VMEM_LIMIT),
        )(*self.flags, *args)

    def begin(self, state, log_decay):
        return self.step(pass_begin_kernel, [self.state, self.row, self.sent_log], state, log_decay)

    def pair(self, held):
        keep, kept, send = held
        got = swap(send, "seq", 1)
        outs = [self.state, self.row, self.state, self.row, self.sent_log]
        return self.step(pass_pair_kernel, outs, keep, kept, got)

    def next_line(self, held):
        first, d_first, both, pair, send = held
        got = shift_flat(send, 2 * self.direction)
        outs = [self.state, self.row, self.sent]
        return (first, d_first, *self.step(pass_line_kernel, outs, both, pair, got))

    def further_lines(self, held):
        first, d_first, carry, before, send = held
        got = shift_flat(send, 4 * self.direction)
        outs = [self.state, self.sent]
        return self.step(pass_far_kernel, outs, first, d_first, carry, before, got)

    def end(self, held):
        mine, send = held
        out = shaped(2, *self.state.shape)
        return self.step(pass_end_kernel, out, mine, swap(send, "seq", 1))


def lane_is_low(rows):
    return lax.broadcasted_iota(jnp.int32, (rows, LANES), 1) < P_SIZE


def spread(columns, j, rows):
    low = jnp.broadcast_to(columns[:, 2 * j : 2 * j + 1], (rows, LANES))
    high = jnp.broadcast_to(columns[:, 2 * j + 1 : 2 * j + 2], (rows, LANES))
    return jnp.where(lane_is_low(rows), low, high), low, high


def triangle(rows, keep):
    first = lax.broadcasted_iota(jnp.int32, (rows, rows), 0)
    second = lax.broadcasted_iota(jnp.int32, (rows, rows), 1)
    return keep(first, second)


def decays(rates, rows):
    lower = triangle(rows, lambda t, s: t >= s)
    within = dot(lower.astype(F32), rates, NN, HIGHEST)
    upper = triangle(rows, lambda s, t: s <= t).astype(F32)
    within_t = dot(rates, upper, TN, HIGHEST)
    return within, within_t, lower


def window(column, row, keep):
    rows = row.shape[1]
    return jnp.exp(jnp.where(keep, column[:, :rows] - row, -1e30))


def scan_kernel(
    pairs, x_ref, bc_ref, halo_ref, dt_ref, cw_ref, bias_ref, rate_ref, skip_ref,
    v_ref, y_ref, st_ref, wc_ref, sb_ref, wo_ref, sl_ref, we_ref,
    hal, state, off, off_l,
):
    rows = x_ref.shape[0]
    inner = pairs * LANES

    @pl.when(pl.program_id(1) == 0)
    def _():
        hal[...] = halo_ref[0]
        state[...] = jnp.zeros_like(state)
        off[...] = jnp.zeros_like(off)
        off_l[...] = jnp.zeros_like(off_l)

    def convolve(ref, at, start):
        now = ref[:, start : start + LANES].astype(F32)
        chunk = jnp.concatenate([hal[:, at : at + LANES], now], axis=0)
        hal[:, at : at + LANES] = now[rows - HALO :]
        shift = HALO - KERNEL + 1
        out = cw_ref[0:1, at : at + LANES] * chunk[shift : shift + rows]
        for k in range(1, KERNEL):
            out = out + cw_ref[k : k + 1, at : at + LANES] * chunk[shift + k : shift + k + rows]
        v_ref[:, at : at + LANES] = out
        return out * jax.nn.sigmoid(out)

    bmat = convolve(bc_ref, inner, 0)
    cmat = convolve(bc_ref, inner + LANES, LANES)
    b_half, c_half = bmat.astype(BF16), cmat.astype(BF16)
    scores = dot(cmat, bmat, NT, HIGHEST)
    steps = jax.nn.softplus(dt_ref[...] + bias_ref[...])
    rates = steps * -rate_ref[...]
    within, within_t, lower = decays(rates, rows)
    low_lanes = lane_is_low(rows)
    st_ref[...] = steps
    wc_ref[...] = off[0:1] + within
    off[0:1] = off[0:1] + within[rows - 1 : rows]
    wo_ref[0] = off_l[0:1]
    for j in range(pairs):
        at = slice(j * LANES, (j + 1) * LANES)
        x = convolve(x_ref, j * LANES, j * LANES)
        u = x * spread(steps, j, rows)[0]
        u_half = u.astype(BF16)
        grow, low, high = spread(within, j, rows)
        end = grow[rows - 1 : rows]
        a_low = (window(low, within_t[2 * j : 2 * j + 1], lower) * scores).astype(BF16)
        a_high = (window(high, within_t[2 * j + 1 : 2 * j + 2], lower) * scores).astype(BF16)
        inside = jnp.where(low_lanes, dot(a_low, u_half), dot(a_high, u_half))
        before = state[:, at]
        carried = jnp.exp(grow) * dot(c_half, before.astype(BF16))
        y_ref[:, at] = inside + carried + skip_ref[0:1, at] * x
        tail = (u * jnp.exp(end - grow)).astype(BF16)
        sb_ref[0, :, at] = before
        after = jnp.exp(end) * before + dot(b_half, tail, TN)
        state[:, at] = after
        sl_ref[0, :, at] = after
        ends = off_l[0:1, at] + end
        off_l[0:1, at] = ends
        we_ref[0, :, at] = ends


def gate_kernel(
    pairs, y_ref, vc_ref, s_ref, wc_ref, zp_ref, dmp_ref, gg_ref, na_ref, ca_ref, wz_ref, wo_ref,
    ssd_ref, sq_ref, z_ref, dm_ref
):
    rows = y_ref.shape[0]
    z_ref[...] = zp_ref[...] + dot(na_ref[...], wz_ref[...])
    dm_ref[...] = dmp_ref[...] + dot(ca_ref[...], wo_ref[...])
    vc = vc_ref[...]
    c_half = (vc * jax.nn.sigmoid(vc)).astype(BF16)
    cumulative = wc_ref[...]
    total = jnp.zeros((rows, LANES), F32)
    meet = jnp.zeros((rows, LANES), F32)
    for j in range(pairs):
        at = slice(j * LANES, (j + 1) * LANES)
        grow = jnp.exp(spread(cumulative, j, rows)[0])
        ssd = y_ref[:, at] + grow * dot(c_half, s_ref[0, :, at].astype(BF16))
        ssd_ref[:, at] = ssd
        z = z_ref[:, at]
        gated = ssd * (z * jax.nn.sigmoid(z))
        total = total + gated * gated
        meet = meet + dm_ref[:, at] * gg_ref[0:1, at] * gated
    sq_ref[0, 0:1] = jnp.sum(total.T, axis=0, keepdims=True)
    sq_ref[0, 1:2] = jnp.sum(meet.T, axis=0, keepdims=True)


def as_column(row):
    return jnp.broadcast_to(row, (LANES, row.shape[1])).T


def gate_back_kernel(
    pairs, width, dmp_ref, ssd_ref, zp_ref, gs_ref, ip_ref, gg_ref, wc_ref, vc_ref,
    na_ref, ca_ref, wz_ref, wo_ref,
    dz_ref, dy_ref, ds_ref, zz_ref, gate_ref, mixed_ref, z_ref, dm_ref,
):
    rows = dmp_ref.shape[0]
    z_ref[...] = zp_ref[...] + dot(na_ref[...], wz_ref[...])
    dm_ref[...] = dmp_ref[...] + dot(ca_ref[...], wo_ref[...])

    @pl.when(pl.program_id(1) == 0)
    def _():
        ds_ref[...] = jnp.zeros_like(ds_ref)

    @pl.when((pl.program_id(0) == 0) & (pl.program_id(1) == 0))
    def _():
        gate_ref[...] = jnp.zeros_like(gate_ref)

    scale = as_column(gs_ref[0])
    pull = as_column(gs_ref[0] * gs_ref[0] * gs_ref[0] * ip_ref[0] * (1.0 / width))
    vc = vc_ref[...]
    c_half = (vc * jax.nn.sigmoid(vc)).astype(BF16)
    cumulative = wc_ref[...]
    total = jnp.zeros((rows, LANES), F32)
    for j in range(pairs):
        at = slice(j * LANES, (j + 1) * LANES)
        z = z_ref[:, at]
        ssd = ssd_ref[:, at]
        logistic = jax.nn.sigmoid(z)
        opened = z * logistic
        gated = ssd * opened
        mixed_ref[:, at] = (gated * scale * gg_ref[0:1, at]).astype(BF16)
        scaled = scale * dm_ref[:, at]
        gate_ref[0:1, at] += jnp.sum(scaled * gated, axis=0, keepdims=True)
        d_gated = scaled * gg_ref[0:1, at] - gated * pull
        d_z = (d_gated * ssd * silu_slope(z, logistic)).astype(BF16)
        dz_ref[:, at] = d_z
        total = total + d_z.astype(F32) * z
        dy = d_gated * opened
        dy_ref[:, at] = dy
        grown = (jnp.exp(spread(cumulative, j, rows)[0]) * dy).astype(BF16)
        ds_ref[0, :, at] += dot(c_half, grown, TN)
    zz_ref[0] = jnp.sum(total.T, axis=0, keepdims=True)


def scan_back_kernel(
    pairs, v_ref, dy_ref, st_ref, rate_ref, sb_ref, wo_ref, s_ref,
    du_ref, dbc_ref, grad,
):
    rows = v_ref.shape[0]
    inner = pairs * LANES

    @pl.when(pl.program_id(1) == 0)
    def _():
        grad[...] = jnp.zeros_like(grad)

    def act(at):
        value = v_ref[:, at : at + LANES]
        return value * jax.nn.sigmoid(value)

    bmat, cmat = act(inner), act(inner + LANES)
    b_half, c_half = bmat.astype(BF16), cmat.astype(BF16)
    scores = dot(cmat, bmat, NT, HIGHEST)
    steps = st_ref[...]
    rates = steps * -rate_ref[...]
    within, within_t, lower = decays(rates, rows)
    low_lanes = lane_is_low(rows)
    d_c = jnp.zeros((rows, LANES), F32)
    d_b = jnp.zeros((rows, LANES), F32)
    d_scores = jnp.zeros((rows, rows), F32)
    none = jnp.zeros((rows, LANES), BF16)
    for j in range(pairs):
        at = slice(j * LANES, (j + 1) * LANES)
        x = act(j * LANES)
        u = x * spread(steps, j, rows)[0]
        u_half = u.astype(BF16)
        dy = dy_ref[:, at]
        dy_half = dy.astype(BF16)
        grow, low, high = spread(within, j, rows)
        end = grow[rows - 1 : rows]
        back = jnp.exp(end - grow)
        grown = (jnp.exp(grow) * dy).astype(BF16)
        begun = sb_ref[0, :, at] + jnp.exp(wo_ref[0, :, at]) * s_ref[0, :, at]
        d_c = d_c + dot(grown, begun.astype(BF16), NT)
        later = grad[:, at]
        later_half = later.astype(BF16)
        d_b = d_b + dot((u * back).astype(BF16), later_half, NT)
        w_low = window(low, within_t[2 * j : 2 * j + 1], lower)
        w_high = window(high, within_t[2 * j + 1 : 2 * j + 2], lower)
        d_scores = d_scores + w_low * dot(jnp.where(low_lanes, dy_half, none), u_half, NT)
        d_scores = d_scores + w_high * dot(jnp.where(low_lanes, none, dy_half), u_half, NT)
        a_low = (w_low * scores).astype(BF16)
        a_high = (w_high * scores).astype(BF16)
        inside = jnp.where(low_lanes, dot(a_low, dy_half, TN), dot(a_high, dy_half, TN))
        du_ref[:, at] = inside + back * dot(b_half, later_half)
        grad[:, at] = jnp.exp(end) * later + dot(c_half, grown, TN)
    d_half = d_scores.astype(BF16)
    dbc_ref[:, :LANES] = d_b + dot(d_half, c_half, TN)
    dbc_ref[:, LANES:] = d_c + dot(d_half, b_half)


def put_split(ref, at, value):
    rows = value.shape[0]
    high = value.astype(BF16)
    ref[:rows, at] = high
    ref[rows : 2 * rows, at] = (value - high.astype(F32)).astype(BF16)


def per_head(ref, picker, rows):
    both = dot(ref[: 2 * rows], picker)
    return both[:rows] + both[rows:]


def finish_kernel(
    pairs, split, v_ref, dy_ref, du_ref, ssd_ref, st_ref, wc_ref, we_ref, la_ref, se_ref, dbc_ref,
    dt_ref, bias_ref, rate_ref, skip_ref, pick_ref, at_ref,
    dcx_ref, keep_ref, send_ref, ddt_ref, dskip_ref, dhead_ref, run, moves, drives,
):
    rows = v_ref.shape[0]
    inner = pairs * LANES
    picker = pick_ref[...]

    @pl.when((pl.program_id(0) == 0) & (pl.program_id(1) == 0))
    def _():
        dskip_ref[...] = jnp.zeros_like(dskip_ref)
        dhead_ref[...] = jnp.zeros_like(dhead_ref)

    @pl.when(pl.program_id(1) == 0)
    def _():
        for j in range(pairs):
            at = slice(j * LANES, (j + 1) * LANES)
            both = jnp.sum(la_ref[0, :, at] * se_ref[0, :, at], axis=0, keepdims=True)
            put_split(moves, at, jnp.broadcast_to(both, (rows, LANES)))
        run[...] = per_head(moves, picker, rows)[0:8]

    value_b = v_ref[:, inner : inner + LANES]
    b_half = (value_b * jax.nn.sigmoid(value_b)).astype(BF16)
    steps = st_ref[...]
    cumulative = wc_ref[...]
    d_b = dbc_ref[:, :LANES]
    for j in range(pairs):
        at = slice(j * LANES, (j + 1) * LANES)
        value = v_ref[:, at]
        logistic = jax.nn.sigmoid(value)
        x = value * logistic
        wide = spread(steps, j, rows)[0]
        u = x * wide
        dy = dy_ref[:, at]
        skip = skip_ref[0:1, at]
        tail = jnp.exp(we_ref[0, :, at] - spread(cumulative, j, rows)[0])
        later = la_ref[0, :, at].astype(BF16)
        du = du_ref[:, at] + tail * dot(b_half, later)
        d_b = d_b + dot((u * tail).astype(BF16), later, NT)
        put_split(moves, at, dy * (ssd_ref[:, at] - skip * x) - u * du)
        put_split(drives, at, x * du)
        dskip_ref[0:1, at] += jnp.sum(dy * x, axis=0, keepdims=True)
        d_inner = wide * du + skip * dy
        dcx_ref[:, at] = (d_inner * silu_slope(value, logistic)).astype(BF16)
    d_c = dbc_ref[:, LANES:]
    if split:
        turn = lambda a: pltpu.roll(a, P_SIZE, 1)
        near, far = jnp.where(at_ref[1] == 0, d_b, d_c), jnp.where(at_ref[1] == 0, d_c, d_b)
        low, core = lane_is_low(rows), at_ref[0] == 0
        keep_ref[...] = jnp.where(
            core, jnp.where(low, near, turn(far)), jnp.where(low, turn(near), far)
        )
        send_ref[...] = jnp.where(
            core, jnp.where(low, turn(near), far), jnp.where(low, near, turn(far))
        )
    else:
        keep_ref[...] = d_b
        send_ref[...] = d_c
    moved = per_head(moves, picker, rows)
    driven = per_head(drives, picker, rows)
    upper = triangle(rows, lambda t, s: s >= t).astype(F32)
    d_rates = dot(upper, moved, NN, HIGHEST) + run[0:1]
    run[0:1] = d_rates[0:1]
    d_steps = driven - rate_ref[...] * d_rates
    d_raw = d_steps * jax.nn.sigmoid(dt_ref[...] + bias_ref[...])
    ddt_ref[...] = d_raw.astype(BF16)
    dhead_ref[0:1] += jnp.sum(d_raw, axis=0, keepdims=True)
    dhead_ref[1:2] -= jnp.sum(steps * d_rates, axis=0, keepdims=True)


def conv_back_kernel(d_ref, in_ref, halo_ref, cw_ref, dx_ref, gw_ref, xx_ref, hal):
    rows, width = d_ref.shape

    @pl.when((pl.program_id(0) == 0) & (pl.program_id(1) == 0))
    def _():
        gw_ref[...] = jnp.zeros_like(gw_ref)

    @pl.when(pl.program_id(1) == 0)
    def _():
        hal[...] = halo_ref[0]

    meet = jnp.zeros((rows, LANES), F32)
    for c in range(width // LANES):
        at = slice(c * LANES, (c + 1) * LANES)
        now = d_ref[:, at].astype(F32)
        chunk = jnp.concatenate([now, hal[:, at]], axis=0)
        hal[:, at] = now[:HALO]
        given = in_ref[:, at].astype(F32)
        total = jnp.zeros((rows, LANES), F32)
        for k in range(KERNEL):
            moved = chunk[KERNEL - 1 - k : KERNEL - 1 - k + rows]
            total = total + cw_ref[k : k + 1, at] * moved
            gw_ref[k : k + 1, at] += jnp.sum(given * moved, axis=0, keepdims=True)
        d_x = total.astype(BF16)
        dx_ref[:, at] = d_x
        meet = meet + d_x.astype(F32) * given
    xx_ref[0] = jnp.sum(meet.T, axis=0, keepdims=True)


def place_blocks(spot_ref, target, items, down, along=slice(None)):
    order = [0]
    for k in range(1, 4):
        order += [8 - k, k]

    rows = down.stop - down.start

    def put(k, shift, block):
        at = pl.multiple_of(spot_ref[k] * rows + shift, LANES)
        target[pl.ds(at, block.shape[0]), :] = block

    for k, item in zip(order, items):
        put(k, 0, item[down, along])
    return put


def in_project_kernel(spot_ref, *refs):
    acts, items, halves = refs[:4], refs[4:11], refs[11:13]
    x_ref, rest_ref, w_ref, r_ref = refs[13:]
    rows = items[0].shape[0]
    inner = x_ref.shape[1]

    @pl.when(pl.program_id(0) == 0)
    def _():
        for target, cut in ((w_ref, slice(0, inner)), (r_ref, slice(inner, None))):
            put = place_blocks(spot_ref, target, items, slice(0, rows), cut)
            put(4, 0, halves[0][:, cut])
            put(4, rows // 2, halves[1][:, cut])

    act = jnp.concatenate([a[...] for a in acts], axis=1)
    x_ref[...] = dot(act, w_ref[...]).astype(BF16)
    rest_ref[...] = dot(act, r_ref[...])


LATE = (4, 3, 5)


def gate_project_kernel(spot_ref, *refs):
    acts, cots, items = refs[:4], refs[4:8], refs[8:13]
    z_ref, dm_ref, wz_ref, wo_ref, na_ref, ca_ref = refs[13:]
    rows = items[0].shape[0] // 2

    @pl.when(pl.program_id(0) == 0)
    def _():
        for target, down in ((wz_ref, slice(0, rows)), (wo_ref, slice(rows, 2 * rows))):
            put = place_blocks(spot_ref, target, items, down)
            for k in LATE:
                put(k, 0, jnp.zeros((rows, target.shape[1]), BF16))

    for n, k in enumerate(LATE):
        to = slice(n * rows, (n + 1) * rows)
        for i in range(8):

            @pl.when(spot_ref[k] == i)
            def _():
                cut = slice((i % 2) * rows, (i % 2 + 1) * rows)
                na_ref[:, to] = acts[i // 2][:, cut]
                ca_ref[:, to] = cots[i // 2][:, cut]

    z_ref[...] = dot(jnp.concatenate([a[...] for a in acts], axis=1), wz_ref[...])
    dm_ref[...] = dot(jnp.concatenate([a[...] for a in cots], axis=1), wo_ref[...])


def gate_more_kernel(spot_ref, z_ref, dm_ref, na_ref, ca_ref, five_ref, three_ref, z_out, dm_out):
    rows = five_ref.shape[0] // 2
    one, two = slice(rows, 2 * rows), slice(2 * rows, 3 * rows)
    z_out[...] = z_ref[...] + (
        dot(na_ref[:, one], three_ref[:rows]) + dot(na_ref[:, two], five_ref[:rows])
    )
    dm_out[...] = dm_ref[...] + (
        dot(ca_ref[:, one], three_ref[rows:]) + dot(ca_ref[:, two], five_ref[rows:])
    )


def with_spots(kernel, spots, acts, items, outs, shapes):
    total = acts[0].shape[0]
    rows = min(512, total)
    fixed = lambda i, spot: (0, 0)
    return pl.pallas_call(
        kernel,
        grid_spec=pltpu.PrefetchScalarGridSpec(
            num_scalar_prefetch=1,
            grid=(total // rows,),
            in_specs=[pl.BlockSpec((rows, act.shape[1]), lambda i, spot: (i, 0)) for act in acts]
            + [pl.BlockSpec(item.shape, fixed) for item in items],
            out_specs=[
                pl.BlockSpec((rows, shape.shape[1]), lambda i, spot: (i, 0)) if split
                else pl.BlockSpec(shape.shape, fixed)
                for shape, split in zip(shapes, outs)
            ],
        ),
        out_shape=shapes,
        compiler_params=pltpu.CompilerParams(vmem_limit_bytes=VMEM_LIMIT),
        cost_estimate=lasts(15.0),
    )(spots, *acts, *items)


def outer_kernel(pairs_of, far_ref, block_ref, *refs):
    out_ref = refs[-1]
    n = len(pairs_of)
    grads = refs[4 * n : -1]
    width = refs[0].shape[1]
    spot = far_ref[0] ^ (pl.program_id(0) + 1)
    for a in range(4):

        @pl.when(spot // 2 == a)
        def _():
            taken = 0
            for i, count in enumerate(pairs_of):
                start = 0
                for grad in grads[taken : taken + count]:
                    wide = grad.shape[1]
                    out_ref[i * width : (i + 1) * width, start : start + wide] = dot(
                        refs[4 * i + a][...], grad[...], TN
                    ).astype(BF16)
                    start += wide
                taken += count


def outer(far, blocks, *terms):
    total, own = terms[0][0][0].shape
    width = own // 2

    def pick(i, far, blocks, a):
        late = i + 1 > 2 * ((far[0] >> 1) ^ a)
        return 0, jnp.where(late, 1 - (far[0] & 1), far[0] & 1)

    specs, args = [], []
    for acts, _ in terms:
        for a, act in enumerate(acts):
            specs.append(pl.BlockSpec((total, width), functools.partial(pick, a=a)))
            args.append(act)
    for _, grads in terms:
        for grad in grads:
            specs.append(pl.BlockSpec(grad.shape, lambda i, far, blocks: (0, 0)))
            args.append(grad)
    columns = sum(g.shape[1] for g in terms[0][1])
    rows = width * len(terms)
    return pl.pallas_call(
        functools.partial(outer_kernel, [len(grads) for _, grads in terms]),
        grid_spec=pltpu.PrefetchScalarGridSpec(
            num_scalar_prefetch=2,
            grid=(7,),
            in_specs=specs,
            out_specs=pl.BlockSpec(
                (rows, columns), lambda i, far, blocks: (blocks[far[0] ^ (i + 1)], 0)
            ),
        ),
        out_shape=shaped(8 * rows, columns, dtype=BF16),
        compiler_params=pltpu.CompilerParams(vmem_limit_bytes=VMEM_LIMIT),
        cost_estimate=lasts(8.0 * rows * columns / 2**18),
    )(far, blocks, *args)


def outer_far(acts, grads):
    columns = grads[0].shape[1] if len(acts) == 2 else sum(g.shape[1] for g in grads)
    total, width = acts[0].shape[0], acts[0].shape[1] // len(LATE)
    first_block = pl.BlockSpec((total, width), lambda i: (0, 0))
    whole = lambda a: pl.BlockSpec(a.shape, lambda i: (0, 0))

    def kernel(*refs):
        first, second = refs[-2:]
        given = refs[len(acts) : -2]
        if len(acts) == 2:
            first[...] = dot(refs[0][...], given[0][...], TN).astype(BF16)
            second[...] = dot(refs[1][...], given[1][...], TN).astype(BF16)
            return
        start = 0
        for grad in given:
            wide = grad.shape[1]
            both = dot(refs[0][...], grad[...], TN).astype(BF16)
            first[:, start : start + wide] = both[: width // 2]
            second[:, start : start + wide] = both[width // 2 :]
            start += wide

    half = shaped(width if len(acts) == 2 else width // 2, columns, dtype=BF16)
    return pl.pallas_call(
        kernel,
        grid=(1,),
        in_specs=[first_block] * len(acts) + [whole(grad) for grad in grads],
        out_specs=[whole(half), whole(half)],
        out_shape=[half, half],
        compiler_params=pltpu.CompilerParams(vmem_limit_bytes=VMEM_LIMIT),
    )(*acts, *grads)


def project_kernel(terms, late, spot_ref, *refs):
    out_ref = refs[-1]
    total = None
    for k in range(terms):
        weight = refs[terms + k][...]
        if k == 0:
            for n in range(late):
                here = pl.program_id(0) == spot_ref[LATE[n]]
                weight = jnp.where(here, refs[2 * terms + n][...], weight)
        term = dot(refs[k][...], weight, NT)
        total = term if total is None else total + term
    out_ref[...] = total.astype(out_ref.dtype)


def project(ring, spots, acts, weights, late, second):
    if not ring.on:
        return sum(dot(a, w, NT) for a, w in zip(acts, weights)).astype(BF16)
    rows, width = acts[0].shape[0], 256
    whole = lambda i, spot: (0, 0)
    half = lambda i, spot: (second, 0)
    return pl.pallas_call(
        functools.partial(project_kernel, len(acts), len(late)),
        grid_spec=pltpu.PrefetchScalarGridSpec(
            num_scalar_prefetch=1,
            grid=(weights[0].shape[0] // width,),
            in_specs=[pl.BlockSpec(a.shape, whole) for a in acts]
            + [pl.BlockSpec((width, w.shape[1]), lambda i, spot: (i, 0)) for w in weights]
            + [
                pl.BlockSpec((width, w.shape[1]), half if w.shape[0] > width else whole)
                for w in late
            ],
            out_specs=pl.BlockSpec((rows, width), lambda i, spot: (0, i)),
        ),
        out_shape=shaped(rows, weights[0].shape[0], dtype=BF16),
        compiler_params=pltpu.CompilerParams(vmem_limit_bytes=VMEM_LIMIT),
        cost_estimate=lasts(7.0 * sum(a.shape[1] for a in acts) / 1024),
    )(spots, *acts, *weights, *late)


def block_total(refs, cut):
    return sum(ref[cut].astype(F32) for ref in refs)


def total_zo_kernel(own_ref, right_ref, left_ref, w_ref, gz_ref, go_ref, met_ref):
    refs = own_ref, right_ref, left_ref
    rows = w_ref.shape[0]
    g_z = block_total(refs, slice(0, rows))
    gz_ref[...] = g_z
    go_ref[...] = block_total(refs, slice(rows, 2 * rows)).T
    met_ref[...] = jnp.sum(g_z * w_ref[...].astype(F32), axis=1, keepdims=True)


def total_in_kernel(own_ref, right_ref, left_ref, w_ref, met_in, gx_ref, gb_ref, gd_ref, met_ref):
    total = block_total((own_ref, right_ref, left_ref), slice(None))
    inner, heads = gx_ref.shape[1], gd_ref.shape[1]
    gx_ref[...] = total[:, :inner]
    gb_ref[...] = total[:, inner : inner + gb_ref.shape[1]]
    start = inner + gb_ref.shape[1]
    gd_ref[...] = total[:, start : start + heads]
    met = jnp.sum(total * w_ref[...].astype(F32), axis=1, keepdims=True)
    met_ref[...] = met_in[...] + met


def totals(kernel, whole, came, others, shapes):
    rows = came[0].shape[0]
    fixed = lambda i: (0, 0)
    arrays = [*came, *others]
    return pl.pallas_call(
        kernel,
        grid=(1,),
        in_specs=[pl.BlockSpec((rows, whole.shape[1]), fixed)]
        + [pl.BlockSpec(a.shape, fixed) for a in arrays],
        out_specs=[pl.BlockSpec(shape.shape, fixed) for shape in shapes],
        out_shape=shapes,
        compiler_params=pltpu.CompilerParams(vmem_limit_bytes=VMEM_LIMIT),
    )(whole, *arrays)


def shaped(*shape, dtype=F32):
    return jax.ShapeDtypeStruct(shape, dtype)


def call(kernel, grid, ins, outs, shapes, scratch=(), micros=5.0):
    return pl.pallas_call(
        kernel,
        grid=grid,
        in_specs=ins,
        out_specs=outs,
        out_shape=shapes,
        scratch_shapes=list(scratch),
        compiler_params=pltpu.CompilerParams(vmem_limit_bytes=VMEM_LIMIT),
        cost_estimate=lasts(micros),
    )


def conv_back(d_conv, given, after, taps, batch, length, rows):
    width = d_conv.shape[1]
    count = length // rows
    turn = lambda b, i: (b * count + count - 1 - i, 0)
    block = pl.BlockSpec((rows, width), turn)
    total = batch * length
    return call(
        conv_back_kernel,
        (batch, count),
        [
            block,
            block,
            pl.BlockSpec((1, HALO, width), lambda b, i: (b, 0, 0)),
            pl.BlockSpec((KERNEL, width), lambda b, i: (0, 0)),
        ],
        [
            block,
            pl.BlockSpec((KERNEL, width), lambda b, i: (0, 0)),
            pl.BlockSpec((1, 1, rows), lambda b, i: (b * count + count - 1 - i, 0, 0)),
        ],
        [
            shaped(total, width, dtype=BF16),
            shaped(KERNEL, width),
            shaped(batch * count, 1, rows),
        ],
        [pltpu.VMEM((HALO, width), F32)],
        micros=8.0 * total * width / 2**20,
    )(d_conv, given, after, taps)


def body(
    tokens, norm_gain, w_z, w_x, w_bc, w_dt, conv_x, conv_bc, dt_bias, decay_rate,
    skip_gain, gate_gain, w_out, grad_out,
):
    ring = Ring(lax.axis_size("seq"))
    batch, length, own_width = tokens.shape
    model = norm_gain.shape[0] * ring.size
    total = batch * length
    inner = w_z.shape[1]
    heads = dt_bias.shape[0]
    inner_all = inner * lax.axis_size("head")
    pairs = heads // 2
    rows = min(SPAN, length)
    count = length // rows
    blocks = batch * count
    margin = KERNEL - 1
    here = lax.axis_index("head")

    slab = tokens.reshape(total, own_width)
    cot_rows = grad_out.reshape(total, own_width)
    bias_row = dt_bias.reshape(1, heads)
    rate_row = decay_rate.reshape(1, heads)
    skip_lanes = jnp.repeat(skip_gain, P_SIZE).reshape(1, inner)
    gate_f = gate_gain.astype(F32).reshape(1, inner)
    conv_xf = conv_x.astype(F32)
    conv_bcf = conv_bc.astype(F32)
    conv_w = jnp.concatenate([conv_xf, conv_bcf], axis=1)

    def edge(arrays, last):
        cut = [array.reshape(batch, length, -1) for array in arrays]
        cut = [array[:, length - margin :] if last else array[:, :margin] for array in cut]
        cut = jnp.concatenate(cut, axis=2)
        moves = [(i, i + 1) for i in range(ring.size - 1)]
        if not last:
            moves = [(b, a) for a, b in moves]
        got = lax.ppermute(cut, "seq", moves).astype(F32)
        pad = ((0, 0), (HALO - margin, 0), (0, 0)) if last else ((0, 0), (0, HALO - margin), (0, 0))
        return jnp.pad(got, pad)

    at = lambda b, i: (b * count + i, 0)
    back = lambda b, i: (b * count + count - 1 - i, 0)
    at3 = lambda b, i: (b * count + i, 0, 0)
    back3 = lambda b, i: (b * count + count - 1 - i, 0, 0)
    seq3 = lambda b, i: (b, 0, 0)
    fixed = lambda b, i: (0, 0)
    row_heads = pl.BlockSpec((1, heads), fixed)
    row_inner = pl.BlockSpec((1, inner), fixed)
    state_spec = pl.BlockSpec((1, N, inner), seq3)
    pair_flops = total * rows * inner

    block_spec = pl.BlockSpec((rows, inner), at)
    row_out = pl.BlockSpec((1, 1, rows), at3)
    c_spec = pl.BlockSpec((rows, LANES), lambda b, i: (b * count + i, inner // LANES + 1))
    head_cols = pl.BlockSpec((rows, heads), at)
    v_back = pl.BlockSpec((rows, inner + 2 * N), back)
    block_back = pl.BlockSpec((rows, inner), back)
    heads_back = pl.BlockSpec((rows, heads), back)
    bc_back = pl.BlockSpec((rows, 2 * N), back)
    def scan(x_in, bc_in, halo, dt_raw):
        conv_out, y_local, steps, cumulative, begun, offsets, left, left_w = call(
            functools.partial(scan_kernel, pairs),
            (batch, count),
            [
                pl.BlockSpec((rows, inner), at),
                pl.BlockSpec((rows, 2 * N), at),
                pl.BlockSpec((1, HALO, inner + 2 * N), seq3),
                pl.BlockSpec((rows, heads), at),
                pl.BlockSpec((KERNEL, inner + 2 * N), fixed),
                row_heads,
                row_heads,
                row_inner,
            ],
            [
                pl.BlockSpec((rows, inner + 2 * N), at),
                pl.BlockSpec((rows, inner), at),
                pl.BlockSpec((rows, heads), at),
                pl.BlockSpec((rows, heads), at),
                pl.BlockSpec((1, N, inner), at3),
                pl.BlockSpec((1, 1, inner), at3),
                state_spec,
                pl.BlockSpec((1, 1, inner), seq3),
            ],
            [
                shaped(total, inner + 2 * N),
                shaped(total, inner),
                shaped(total, heads),
                shaped(total, heads),
                shaped(blocks, N, inner),
                shaped(blocks, 1, inner),
                shaped(batch, N, inner),
                shaped(batch, 1, inner),
            ],
            [
                pltpu.VMEM((HALO, inner + 2 * N), F32),
                pltpu.VMEM((N, inner), F32),
                pltpu.VMEM((8, heads), F32),
                pltpu.VMEM((8, inner), F32),
            ],
            micros=14.5,
        )(x_in, bc_in, halo, dt_raw, conv_w, bias_row, rate_row, skip_lanes)
        return conv_out, y_local, steps, cumulative, begun, offsets, left, left_w

    own_block = model // ring.size
    g_rows = min(256, length)
    g_count = length // g_rows
    g_at = lambda b, i: (b * g_count + i, 0)
    g_at3 = lambda b, i: (b * g_count + i, 0, 0)
    g_block, g_row = pl.BlockSpec((g_rows, inner), g_at), pl.BlockSpec((1, 1, g_rows), g_at3)
    g_c = pl.BlockSpec((g_rows, LANES), lambda b, i: (b * g_count + i, inner // LANES + 1))
    g_heads_spec = pl.BlockSpec((g_rows, heads), g_at)
    act_spec = pl.BlockSpec((g_rows, own_block), g_at)
    late_spec = pl.BlockSpec((own_block, inner), fixed)
    wide_scratch = [pltpu.VMEM((g_rows, inner), F32), pltpu.VMEM((g_rows, inner), F32)]

    def gate(y_local, conv_out, came, cumulative, z_part, dm_part, late):
        return call(
            functools.partial(gate_kernel, pairs),
            (batch, g_count),
            [
                g_block, g_c, state_spec, g_heads_spec, g_block, g_block, row_inner,
                act_spec, act_spec, late_spec, late_spec,
            ],
            [g_block, pl.BlockSpec((1, 2, g_rows), g_at3)],
            [shaped(total, inner), shaped(batch * g_count, 2, g_rows)],
            wide_scratch,
            micros=7.0,
        )(y_local, conv_out, came, cumulative, z_part, dm_part, gate_f, *late)

    def gate_back(dm_part, ssd, z_part, gate_scale, product, cumulative, conv_out, late):
        return call(
            functools.partial(gate_back_kernel, pairs, inner_all),
            (batch, g_count),
            [
                g_block, g_block, g_block, g_row, g_row, row_inner, g_heads_spec, g_c,
                act_spec, act_spec, late_spec, late_spec,
            ],
            [g_block, g_block, state_spec, g_row, row_inner, g_block],
            [
                shaped(total, inner, dtype=BF16),
                shaped(total, inner),
                shaped(batch, N, inner),
                shaped(batch * g_count, 1, g_rows),
                shaped(1, inner),
                shaped(total, inner, dtype=BF16),
            ],
            wide_scratch,
            micros=9.0,
        )(dm_part, ssd, z_part, gate_scale, product, gate_f, cumulative, conv_out, *late)

    def scan_back(conv_out, d_ssd, steps, begun, offsets, came):
        du_local, dbc_local = call(
            functools.partial(scan_back_kernel, pairs),
            (batch, count),
            [
                v_back, block_back, heads_back, row_heads,
                pl.BlockSpec((1, N, inner), back3),
                pl.BlockSpec((1, 1, inner), back3),
                state_spec,
            ],
            [block_back, bc_back],
            [shaped(total, inner), shaped(total, 2 * N)],
            [pltpu.VMEM((N, inner), F32)],
            micros=18.0,
        )(conv_out, d_ssd, steps, rate_row, begun, offsets, came)
        return du_local, dbc_local

    def finish(conv_out, d_ssd, du_local, ssd, steps, cumulative, left_w, later, at_end, dbc_local, dt_raw):
        f_back = lambda b, i: (b * g_count + g_count - 1 - i, 0)
        f_spec = lambda width: pl.BlockSpec((g_rows, width), f_back)
        f_v, f_block, f_heads = f_spec(inner + 2 * N), f_spec(inner), f_spec(heads)
        f_maps, f_lanes = f_spec(2 * N), f_spec(LANES)
        lane_head = lax.broadcasted_iota(jnp.int32, (inner, heads), 0) // P_SIZE
        picker = (lane_head == lax.broadcasted_iota(jnp.int32, (inner, heads), 1)).astype(BF16)
        d_conv_x, d_bc_keep, d_bc_send, d_dt, g_skip, g_heads = call(
            functools.partial(finish_kernel, pairs, ring.on),
            (batch, g_count),
            [
                f_v, f_block, f_block, f_block, f_heads, f_heads,
                pl.BlockSpec((1, 1, inner), seq3), state_spec, state_spec, f_maps, f_heads,
                row_heads, row_heads, row_inner,
                pl.BlockSpec((inner, heads), fixed), pl.BlockSpec(memory_space=pltpu.SMEM),
            ],
            [
                f_block, f_lanes, f_lanes, f_heads, row_inner,
                pl.BlockSpec((2, heads), fixed),
            ],
            [
                shaped(total, inner, dtype=BF16),
                shaped(total, LANES),
                shaped(total, LANES),
                shaped(total, heads, dtype=BF16),
                shaped(1, inner),
                shaped(2, heads),
            ],
            [
                pltpu.VMEM((8, heads), F32),
                pltpu.VMEM((2 * g_rows, inner), BF16),
                pltpu.VMEM((2 * g_rows, inner), BF16),
            ],
            micros=15.0,
        )(
            conv_out, d_ssd, du_local, ssd, steps, cumulative, left_w, later, at_end, dbc_local,
            dt_raw, bias_row, rate_row, skip_lanes, picker,
            jnp.stack([here & 1, here >> 1]).astype(jnp.int32),
        )
        return d_conv_x, d_bc_keep, d_bc_send, d_dt, g_skip, g_heads

    split_pass = ring.on and batch == 2
    forth, back_pass = Passing(ring, 1, inner), Passing(ring, -1, inner)
    slope = lambda v: silu_slope(v, jax.nn.sigmoid(v))

    group = 2 * N // 4 if ring.on else 2 * N
    edge_at = inner + group
    spare = -(group + heads) % LANES
    per = w_z.shape[0]
    own_columns = lambda a: lax.dynamic_slice_in_dim(a, here * group, group, 1) if ring.on else a
    all_in = jnp.concatenate(
        [w_x, own_columns(w_bc), w_dt, jnp.zeros((w_x.shape[0], spare), BF16)], axis=1
    )

    def by_group(pieces):
        own, near, far, both = pieces
        return [
            jnp.where(
                here == g, own, jnp.where(here == g ^ 1, near, jnp.where(here == g ^ 2, far, both))
            )
            for g in range(4)
        ]

    def gather_groups(own):
        far = swap(own, "head", 2)
        return by_group([own, swap(own, "head", 1), far, swap(far, "head", 1)])

    def fold(a):
        return jnp.concatenate([a[: total // 2], a[total // 2 :]], axis=1)

    def unfold(a):
        n = a.shape[1] // 2
        return jnp.concatenate([a[:, :n], a[:, n:]], axis=0)
    spots, order = (ring.spots(), ring.blocks()) if ring.on else (None, None)

    def work(all_in, slab):
        own_gain = own_features(ring, norm_gain.astype(F32), own_width)
        square = head_sum(jnp.sum(slab * slab, axis=1))
        scale = lax.rsqrt(square / model + EPS)
        own_normed = (slab * scale[:, None] * own_gain).astype(BF16)
        return ring.hop((all_in, all_in)), own_gain, scale, own_normed

    hop1, own_gain, scale, own_normed = ring.phase(work, all_in, slab)
    far = across(ring, own_normed)

    def work(hop1, own, w_z, w_out, cot_rows):
        zo_in = jnp.concatenate([w_z, w_out.T], axis=0)
        hop2 = ring.hop(hop1)
        return hop2, ring.hop(hop2), beside(ring, own), zo_in, cot_rows.astype(BF16)

    hop2, hop3, near, zo_in, own_cot = ring.phase(work, hop1, own_normed, w_z, w_out, cot_rows)
    hop4, both = ring.phase(
        lambda hop3, far: (ring.last_hop(hop3), corner(ring, own_normed, far)), hop3, far
    )
    normed = (both, near, far, own_normed) if ring.on else (both,)

    def project_in(normed, hop1, hop2, hop3, hop4):
        if ring.on:
            x_in, rest, x_w, rest_w = with_spots(
                in_project_kernel, spots, normed, [all_in, *hop1, *hop2, *hop3, *hop4],
                [True, True, False, False],
                [
                    shaped(total, inner, dtype=BF16), shaped(total, all_in.shape[1] - inner),
                    shaped(model, inner, dtype=BF16),
                    shaped(model, all_in.shape[1] - inner, dtype=BF16),
                ],
            )
            groups = gather_groups(fold(rest[:, :group]).astype(BF16))
            bc_in = jnp.concatenate([unfold(piece) for piece in groups], axis=1)
        else:
            x_w = lax.all_gather(w_x, "seq", axis=0, tiled=True)
            rest_w = lax.all_gather(all_in[:, inner:], "seq", axis=0, tiled=True)
            rest = dot(normed[0], rest_w)
            x_in, bc_in = dot(normed[0], x_w).astype(BF16), rest[:, :group].astype(BF16)
        bc_own = jnp.pad(rest[:, :group].astype(BF16), ((0, 0), (0, -group % LANES)))
        return (
            x_in, bc_in, bc_own, rest[:, group : group + heads], x_w, rest_w,
            edge([x_in, bc_in], True),
        )

    def work(normed, hop1, hop2, hop3, hop4, zo_in):
        return ring.hop((zo_in, zo_in)), ring.phase(project_in, normed, hop1, hop2, hop3, hop4)

    hop1, (x_in, bc_in, bc_own, dt_raw, x_w, rest_w, halo) = ring.phase(
        work, normed, hop1, hop2, hop3, hop4, zo_in
    )

    def work(hop1, x_in, bc_in, halo, dt_raw, own_cot):
        scanned = scan(x_in, bc_in, halo, dt_raw)
        held = forth.pair(forth.begin(scanned[6], scanned[7])) if split_pass else ()
        return ring.hop(hop1), scanned, held, beside(ring, own_cot), across(ring, own_cot)

    hop2, scanned, held, near, far = ring.phase(work, hop1, x_in, bc_in, halo, dt_raw, own_cot)
    conv_out, y_local, steps, cumulative, begun, offsets, left, left_w = scanned
    def work(hop1, hop2, held, far, normed):
        moving = ring.hop(hop2)
        if not ring.on:
            z_w = lax.all_gather(w_z, "seq", axis=0, tiled=True)
            out_w = lax.all_gather(w_out.T, "seq", axis=0, tiled=True)
            cot = (corner(ring, own_cot, far),)
            none = jnp.zeros((total, own_block), BF16)
            given = dot(normed[0], z_w), dot(cot[0], out_w), z_w, out_w, none, none
            return moving, held, cot, given
        both = ring.phase(lambda far: corner(ring, own_cot, far), far)
        wide, weight = shaped(total, inner), shaped(model, inner, dtype=BF16)
        act = shaped(total, len(LATE) * own_block, dtype=BF16)
        given = with_spots(
            gate_project_kernel, spots, (*normed, both, near, far, own_cot), [zo_in, *hop1, *hop2],
            [True, True, False, False, True, True], [wide, wide, weight, weight, act, act],
        )
        held = forth.next_line(held) if split_pass else ()
        return moving, held, both, given

    hop3, held, cot, given = ring.phase(work, hop1, hop2, held, far, normed)
    if ring.on:
        cot = (cot, near, far, own_cot)
    z_part, dm_part, z_w, out_w, normed_late, cot_late = given

    def work(hop3, held, z_part, dm_part, normed_late, cot_late):
        held = forth.further_lines(held) if split_pass else ()
        if ring.on:
            wide = shaped(total, inner)
            z_part, dm_part = with_spots(
                gate_more_kernel, spots, (z_part, dm_part, normed_late, cot_late), hop3,
                [True, True], [wide, wide],
            )
        came = forth.end(held) if split_pass else states_scan(left, left_w, 1)
        return ring.last_hop(hop3), came, z_part, dm_part

    hop4, came, z_part, dm_part = ring.phase(
        work, hop3, held, z_part, dm_part, normed_late, cot_late
    )
    if not ring.on:
        hop4 = (jnp.zeros((own_block, inner), BF16),) * 2
    late = (normed_late, cot_late, *hop4)
    late_z, late_out = ([half, hop3[1], hop3[0]] if ring.on else [] for half in hop4)

    ssd, square_g = gate(y_local, conv_out, came, cumulative, z_part, dm_part, late)
    square_g = head_sum(square_g)
    gate_scale = lax.rsqrt(square_g[:, 0:1] / inner_all + EPS)
    product = square_g[:, 1:2]
    d_z, d_ssd, d_left, met_z, g_gate, mixed = gate_back(
        dm_part, ssd, z_part, gate_scale, product, cumulative, conv_out, late
    )

    far_spot = spots[4:5] if ring.on else None

    def work(d_left, left_w, normed, d_z, mixed, cot, normed_late, cot_late):
        held = back_pass.pair(back_pass.begin(d_left, left_w)) if split_pass else ()
        if ring.on:
            sums = ring.send(*outer_far([normed_late, cot_late], [d_z, mixed]))
            g_zo = outer(far_spot, order, (normed, [d_z]), (cot, [mixed]))
            return held, ring.add(g_zo, sums, 3), g_zo
        return held, (), (dot(normed[0], d_z, TN), dot(cot[0], mixed, TN))

    held, sums, g_zo = ring.phase(
        work, d_left, left_w, normed, d_z, mixed, cot, normed_late, cot_late
    )

    def work(held, sums, conv_out, d_ssd, steps, begun, offsets, came):
        sums = ring.hop(sums)
        held = back_pass.next_line(held) if split_pass else ()
        at_end = jnp.exp(left_w) * came + left
        value = conv_out[:, inner:]
        if ring.on:
            value = [value[:, g * group : (g + 1) * group] for g in range(4)]
            value = jnp.where(
                here < 2, jnp.where(here == 0, value[0], value[1]),
                jnp.where(here == 2, value[2], value[3]),
            )
        back = scan_back(conv_out, d_ssd, steps, begun, offsets, came)
        return held, sums, back, at_end, slope(value)

    held, sums, (du_local, dbc_local), at_end, own_slope = ring.phase(
        work, held, sums, conv_out, d_ssd, steps, begun, offsets, came
    )

    def work(held, sums, g_zo, mixed, out_w, late_out):
        held = back_pass.further_lines(held) if split_pass else ()
        branch = project(ring, spots, [mixed], [out_w], late_out, 1)
        return held, ring.add(g_zo, sums, 2), branch

    held, sums, branch = ring.phase(work, held, sums, g_zo, mixed, out_w, late_out)

    def work(held, branch):
        later = back_pass.end(held) if split_pass else states_scan(d_left, left_w, -1)
        return later, scatter_near(ring, branch)

    later, (out_far, out_own) = ring.phase(work, held, branch)

    def finish_maps(later, du_local, dbc_local, own_slope):
        d_conv_x, mine, send, d_dt, g_skip, g_heads = finish(
            conv_out, d_ssd, du_local, ssd, steps, cumulative, left_w, later, at_end,
            dbc_local, dt_raw,
        )
        if ring.on:
            mine = mine + swap(send, "head", 1)
            mine = mine[:, :group] + unfold(swap(fold(mine[:, group:]), "head", 2))
        else:
            mine = head_sum(jnp.concatenate([mine, send], axis=1))
        d_conv_bc = jnp.pad((mine * own_slope).astype(BF16), ((0, 0), (0, -group % LANES)))
        after = edge([d_conv_x, d_conv_bc], False)
        return d_conv_x, d_conv_bc, d_dt, g_skip, g_heads, after

    def work(later, sums, g_zo, du_local, dbc_local, own_slope):
        sums = ring.hop(sums)
        given = ring.phase(finish_maps, later, du_local, dbc_local, own_slope)
        return ring.add(g_zo, sums, 1), given

    sums, (d_conv_x, d_conv_bc, d_dt, g_skip, g_heads, after) = ring.phase(
        work, later, sums, g_zo, du_local, dbc_local, own_slope
    )

    share = 1.0 if ring.on else jnp.where(here == 0, 1.0, 0.0)
    after_x, after_bc = after[:, :, :inner], after[:, :, inner:]
    own_taps = jnp.pad(own_columns(conv_bcf), ((0, 0), (0, -group % LANES)))

    def work(
        sums, g_zo, d_conv_bc, after_bc, d_conv_x, after_x, d_dt, normed, normed_late, out_far
    ):
        d_x, g_conv_x, met_x = conv_back(d_conv_x, x_in, after_x, conv_xf, batch, length, g_rows)
        d_bc, g_conv_bc, met_bc = conv_back(
            d_conv_bc, bc_own, after_bc, own_taps, batch, length, g_rows
        )
        fill = jnp.zeros((total, spare), BF16)
        d_rest = jnp.concatenate([d_bc[:, :group], d_dt, fill], axis=1)
        last = ring.hop(sums)
        if ring.on:
            sums = ring.send(*outer_far([normed_late], [d_x, d_rest]))
            g_all = outer(far_spot, order, (normed, [d_x, d_rest]))
            sums = ring.add(g_all, sums, 3)
        else:
            sums = ()
            g_all = jnp.concatenate([dot(normed[0], d, TN) for d in (d_x, d_rest)], axis=1)
        met_dt = jnp.sum(d_dt.astype(F32) * dt_raw, axis=1)
        met = met_z.reshape(total) + (met_x + share * met_bc).reshape(total) + met_dt
        return (
            last, sums, d_x, d_rest, g_conv_x, g_conv_bc, met, g_all, across(ring, out_far),
        )

    last, sums, d_x, d_rest, g_conv_x, g_conv_bc, met, g_all, out_far = ring.phase(
        work, sums, g_zo, d_conv_bc, after_bc, d_conv_x, after_x, d_dt, normed, normed_late, out_far
    )
    g_conv_bc = g_conv_bc[:, :group]
    if ring.on:
        none = jnp.zeros((KERNEL, 2 * N), F32)
        g_conv_bc = lax.dynamic_update_slice(none, g_conv_bc, (0, here * group))
    small = jnp.concatenate(
        [
            g_conv_x.reshape(-1), g_conv_bc.reshape(-1), g_gate.reshape(-1),
            g_skip.reshape(-1), g_heads.reshape(-1),
        ]
    )

    def one_swap(array, bit):
        return array + swap(array, "seq", bit) if ring.on else array

    def work(sums, small, d_z, d_x, d_rest, z_w, x_w, rest_w, late_z, met):
        sums = ring.hop(sums)
        met = met + swap(met, "head", 1) if ring.on else head_sum(met)
        if not ring.on:
            columns = lax.broadcasted_iota(jnp.int32, (1, rest_w.shape[1]), 1)
            rest_w = jnp.where((columns < group) & (here > 0), 0.0, rest_w.astype(F32)).astype(BF16)
        back = project(ring, spots, [d_z, d_x, d_rest], [z_w, x_w, rest_w], late_z, 0)
        return sums, back, one_swap(small, 1), met

    sums, back_terms, small, met = ring.phase(
        work, sums, small, d_z, d_x, d_rest, z_w, x_w, rest_w, late_z, met
    )

    def work(sums, g_all, back_terms, met):
        far, d_normed = scatter_near(ring, back_terms)
        met = met + swap(met, "head", 2) if ring.on else met
        return ring.add(g_all, sums, 2), far, d_normed, met / scale

    sums, far, d_normed, dots = ring.phase(work, sums, g_all, back_terms, met)

    def third(sums, g_all, small, out_far, out_own, g_zo, last):
        mixed_out = slab + scatter_sum(ring, out_far, out_own)
        block, column = shaped(per, inner), shaped(per, 1)
        if ring.on:
            g_z, g_out, met_f = totals(
                total_zo_kernel, g_zo, last, [w_z], [block, shaped(inner, per), column]
            )
        else:
            g_z, g_out = (
                lax.psum_scatter(g.astype(BF16), "seq", scatter_dimension=0, tiled=True).astype(F32)
                for g in g_zo
            )
            g_out, met_f = g_out.T, jnp.sum(g_z * w_z.astype(F32), axis=1, keepdims=True)
        sums = ring.add(g_all, ring.hop(sums), 1)
        small = one_swap(one_swap(small, 2), 4) if ring.on else lax.psum(small, "seq")
        parts, start = [], 0
        for width in [KERNEL * inner, KERNEL * 2 * N, inner, inner, heads, heads]:
            parts.append(small[start : start + width])
            start += width
        return sums, parts, mixed_out, g_z, g_out, met_f

    def fourth(sums, g_all, met_f, sum_bc):
        last = ring.hop(sums)
        shapes = [shaped(per, inner), shaped(per, group), shaped(per, heads), shaped(per, 1)]
        if ring.on:
            g_x, g_bc, g_dt, met_f = totals(
                total_in_kernel, g_all, last, [all_in, met_f], shapes
            )
            g_bc = jnp.concatenate(gather_groups(g_bc), axis=1)
        else:
            g = lax.psum_scatter(g_all.astype(BF16), "seq", scatter_dimension=0, tiled=True)
            g = g.astype(F32)
            g_x, g_bc, g_dt = g[:, :inner], g[:, inner:edge_at], g[:, edge_at : edge_at + heads]
            columns = lax.broadcasted_iota(jnp.int32, (1, g.shape[1]), 1)
            once = jnp.where((columns >= inner) & (columns < edge_at), share, 1.0)
            met_f = met_f + jnp.sum(g * all_in.astype(F32) * once, axis=1, keepdims=True)
            sum_bc = sum_bc * (1.0 / lax.axis_size("head"))
        both = head_sum(jnp.concatenate([met_f[:, 0], sum_bc]))
        g_gain = both[:per] / norm_gain.astype(F32)
        return g_x, g_bc, g_dt, g_gain, both[per:]

    def work(sums, g_all, small, far, d_normed, dots, out_far, out_own, g_zo, last):
        far = across(ring, far)
        sums, parts, *given = third(sums, g_all, small, out_far, out_own, g_zo, last)
        ends = fourth(sums, g_all, given[-1], parts[1])
        d_normed = scatter_sum(ring, far, d_normed)
        grad_tokens = (
            cot_rows
            + (scale[:, None] * own_gain) * d_normed
            - slab * (scale * scale * scale * dots / model)[:, None]
        )
        return parts, given, ends, grad_tokens

    parts, (mixed_out, g_z, g_out, _), ends, grad_tokens = ring.phase(
        work, sums, g_all, small, far, d_normed, dots, out_far, out_own, g_zo, last
    )
    sum_x, _, sum_gate, sum_skip, sum_bias, sum_rate = parts
    g_x, g_bc, g_dt, g_gain, sum_bc = ends

    return (
        mixed_out.reshape(batch, length, own_width),
        grad_tokens.reshape(batch, length, own_width),
        g_gain,
        g_z,
        g_x,
        g_bc,
        g_dt,
        sum_x.reshape(KERNEL, inner),
        sum_bc.reshape(KERNEL, 2 * N),
        sum_bias,
        sum_rate,
        jnp.sum(sum_skip.reshape(heads, P_SIZE), axis=1),
        sum_gate,
        g_out,
    )


def solution(mesh):
    in_specs = (
        P(None, "seq", "head"),
        P("seq"),
        P("seq", "head"),
        P("seq", "head"),
        P("seq", None),
        P("seq", "head"),
        P(None, "head"),
        P(),
        P("head"),
        P("head"),
        P("head"),
        P("head"),
        P("head", "seq"),
        P(None, "seq", "head"),
    )
    out_specs = (
        P(None, "seq", "head"),
        P(None, "seq", "head"),
        P("seq"),
        P("seq", "head"),
        P("seq", "head"),
        P("seq", None),
        P("seq", "head"),
        P(None, "head"),
        P(),
        P("head"),
        P("head"),
        P("head"),
        P("head"),
        P("head", "seq"),
    )
    return jax.shard_map(body, mesh=mesh, in_specs=in_specs, out_specs=out_specs, check_vma=False)
```
